32 devices in a mesh: dp: 8 (over z, x), tensor: 4 (over y, core).
Axes of the slice: x: 2, y: 2, z: 4, core: 2. Of those that a mesh axis runs over, the one named last changes fastest.
Arguments:
- tokens_in: bfloat16 [4096, 768], P(('dp', 'tensor')), may hold values from -6 to 6
- out_grad: bfloat16 [4096, 768], P(('dp', 'tensor')), may hold values from -6 to 6
- lengths: int32 [8, 6], P('dp'), may hold values from 1 to 197, 512 in all within a row
- owners: int32 [72], replicated, may hold values from 0 to 7, as said below
- weight_store: float32 [80, 256, 768], P('dp', 'tensor'), may hold values from -1 to 1
- first_store: float32 [80, 256, 768], P('dp', 'tensor'), may hold values from -4096 to 4096
- second_store: float32 [80, 256, 768], P('dp', 'tensor'), may hold values from 512 to 8192
- shared_params: float32 [2, 8, 768], replicated, may hold values from -2 to 2, as said below
- shared_first: float32 [2, 8, 768], replicated, may hold values from -4096 to 4096
- shared_second: float32 [2, 8, 768], replicated, may hold values from 2048 to 32768
- split_params: float32 [2, 4, 3348], P(None, 'tensor'), may hold values from -3 to 3
- split_first: float32 [2, 4, 3348], P(None, 'tensor'), may hold values from -4096 to 4096
- split_second: float32 [2, 4, 3348], P(None, 'tensor'), may hold values from 512 to 8192
Outputs:
- block_out: bfloat16 [4096, 768], P(('dp', 'tensor'))
- input_grad: float32 [4096, 768], P(('dp', 'tensor'))
- matrix_grad: float32 [80, 256, 768], P('dp', 'tensor')
- matrix_first: float32 [80, 256, 768], P('dp', 'tensor')
- matrix_second: float32 [80, 256, 768], P('dp', 'tensor')
- matrix_weight: float32 [80, 256, 768], P('dp', 'tensor')
- shared_grad: float32 [2, 8, 768], replicated
- shared_moment: float32 [2, 8, 768], replicated
- shared_square: float32 [2, 8, 768], replicated
- shared_value: float32 [2, 8, 768], replicated
- split_grad: float32 [2, 4, 3348], P(None, 'tensor')
- split_moment: float32 [2, 4, 3348], P(None, 'tensor')
- split_square: float32 [2, 4, 3348], P(None, 'tensor')
- split_value: float32 [2, 4, 3348], P(None, 'tensor')
The draws below stay inside these ranges and needn't reach their ends.
Inputs may be any that keep to these rules, and one draw needn't show every extreme that they name: `owners`: no owner holds more than 10 blocks and some owner holds exactly 10. `lengths`: each row sums to 512. `shared_params`: rows 0, 2, 4, 6 lie in 0.7 to 1.3.
All inputs are finite; a program needn't handle non-finite values.
Results may differ from the reference program's by a relative error of at most 0.025.
Values may be sent and summed in bfloat16 or wider, within the bound.
No kernel may reach another device: no remote copies, remote signals or barrier semaphores. Data moves between devices by JAX's collectives and lax.ppermute only.
A program may use at most 192 MiB of HBM per device.

```python
import math
import jax
import jax.numpy as jnp
import numpy as np
from jax import lax

D = 768
HEADS = 12
HEAD = 64
FF = 3072
GRID = 14
TOK_DEV = 512
LAYERS = 2
VECTORS = 8
STEP = 10
IMG_TOKENS = 197
RELS = 732
IMG_DEV = 6
TOKENS = 4096
UNITS = 72
CAP = 10
SLOTS = 80
SPLIT_DEV = 3348
N_DP = 8
N_TENSOR = 4


def owner_choice(key):
    full_key, rest_key, order_key = jax.random.split(key, 3)
    full_owner = jax.random.randint(full_key, (), 0, N_DP, dtype=jnp.int32)
    others = jax.random.permutation(rest_key, (N_DP - 1) * CAP)[:UNITS - CAP].astype(jnp.int32)
    others = others + CAP * (others >= full_owner * CAP).astype(jnp.int32)
    chosen = jnp.concatenate([full_owner * CAP + jnp.arange(CAP, dtype=jnp.int32), others])
    order = jax.random.permutation(order_key, UNITS)
    return (chosen[order] // CAP).astype(jnp.int32)


def slot_places(owner_list):
    order = jnp.arange(UNITS, dtype=jnp.int32)
    same_owner = owner_list[:, None] == owner_list[None, :]
    earlier = order[None, :] < order[:, None]
    rank = jnp.sum((same_owner & earlier).astype(jnp.int32), axis=1)
    return (owner_list * CAP + rank).astype(jnp.int32)


def block_scales():
    heads_here = HEADS // N_TENSOR
    hidden_blocks = FF // (N_TENSOR * HEAD)
    scales = []
    for level in range(LAYERS):
        scales += [D ** (-0.5)] * (3 * heads_here) + [HEAD ** (-0.5)] * heads_here
        scales += [D ** (-0.5)] * hidden_blocks + [(FF // 2) ** (-0.5)] * hidden_blocks
    return jnp.array(scales, jnp.float32)


def mixed_values(key, shape, scale):
    normal_part = jnp.clip(jax.random.normal(key, shape, jnp.float32), -4.0, 4.0)
    return scale * normal_part


def square_values(key, shape, scale, lower, upper):
    return scale * jnp.exp(jax.random.uniform(key, shape, jnp.float32, math.log(lower), math.log(upper)))


def draw_owners(key, part):
    return owner_choice(key)


def draw_weight_store(key, part):
    places = slot_places(owner_choice(key))
    key = jax.random.fold_in(key, 11)
    match = (jnp.arange(SLOTS, dtype=jnp.int32)[:, None] == places[None, :]).astype(jnp.float32)
    used = jnp.sum(match, axis=1)
    slot_scale = jnp.sum(match * block_scales()[None, :], axis=1) + (1.0 - used) * D ** (-0.5)
    values = mixed_values(key, (SLOTS, HEAD * N_TENSOR, D), 1.0)
    return slot_scale[:, None, None] * values


def draw_first_store(key, part):
    key = jax.random.fold_in(key, 21)
    return mixed_values(key, (SLOTS, HEAD * N_TENSOR, D), 0.5 * math.sqrt(TOKENS))


def draw_second_store(key, part):
    key = jax.random.fold_in(key, 22)
    lower = 0.5
    return square_values(key, (SLOTS, HEAD * N_TENSOR, D), 0.25 * TOKENS, lower, 8.0)


def draw_shared_params(key, part):
    key = jax.random.fold_in(key, 31)
    shape = (LAYERS, VECTORS, D)
    gains = jax.random.uniform(key, shape, jnp.float32, 0.7, 1.3)
    shifts = jnp.clip(0.3 * jax.random.normal(jax.random.fold_in(key, 2), shape, jnp.float32), -1.2, 1.2)
    is_gain = (jnp.arange(VECTORS) % 2 == 0)[None, :, None]
    return jnp.where(is_gain, gains, shifts)


def draw_shared_first(key, part):
    key = jax.random.fold_in(key, 32)
    return mixed_values(key, (LAYERS, VECTORS, D), math.sqrt(TOKENS))


def draw_shared_second(key, part):
    key = jax.random.fold_in(key, 33)
    lower = 0.5
    return square_values(key, (LAYERS, VECTORS, D), 1.0 * TOKENS, lower, 8.0)


def draw_split_first(key, part):
    key = jax.random.fold_in(key, 41)
    return mixed_values(key, (LAYERS, N_TENSOR, SPLIT_DEV), 0.5 * math.sqrt(TOKENS))


def draw_split_second(key, part):
    key = jax.random.fold_in(key, 42)
    lower = 0.5
    return square_values(key, (LAYERS, N_TENSOR, SPLIT_DEV), 0.25 * TOKENS, lower, 8.0)


def levels(rng, extent, pieces, smallest, high):
    level = 1.0
    for dim, blocks in pieces:
        draws = jax.random.uniform(jax.random.fold_in(jax.random.fold_in(rng, 6), dim), (blocks,), jnp.float32, smallest / len(pieces), high / len(pieces))
        level = level * jnp.repeat(jnp.exp(draws), extent[dim] // blocks).reshape((-1,) + (1,) * (len(extent) - 1 - dim))
    return level


def profile(count, total, limit, slope):
    portions = [(1 << 20) // math.isqrt(grade ** slope) + 1 for grade in range(2, count + 1)]
    surplus, given = total - limit - (count - 1), [1] * (count - 1)
    while surplus > 0:
        movable = [i for i in range(count - 1) if given[i] < limit]
        pool, left = sum([portions[i] for i in movable]), surplus
        for i in movable:
            more = min(limit - given[i], max(1, left * portions[i] // pool), surplus)
            given[i] = given[i] + more
            surplus = surplus - more
    return np.array([limit] + given)


def ragged_sizes(key, number_of, total, bound, lean):
    if number_of == 2:
        one = jax.random.randint(key, (), max(1, total - bound), min(bound, total - 1) + 1)
        return jnp.stack([one, total - one])
    sizes = jnp.asarray(profile(number_of, total, bound, lean), jnp.int32)
    twos = (number_of - 1) // 2
    giver, taker = sizes[1:1 + 2 * twos:2], sizes[2:2 + 2 * twos:2]
    room = jnp.minimum(giver - 1, bound - taker)
    shifted = jax.random.randint(jax.random.fold_in(key, 1), (twos,), 0, 1 << 20) % (room + 1)
    sizes = sizes.at[1:1 + 2 * twos:2].set(giver - shifted).at[2:2 + 2 * twos:2].set(taker + shifted)
    return sizes[jax.random.permutation(jax.random.fold_in(key, 2), number_of)]


def noise(rng, extent, scale, most, cuts=(), kind=jnp.bfloat16):
    level = levels(rng, extent, cuts, -0.22, 0.18) if cuts else 1.0
    values = jax.random.normal(rng, extent, jnp.float32) * scale * level
    return jnp.minimum(jnp.maximum(values, -most), most).astype(kind)


def setup_inputs(seed: int = 0) -> dict:
    splits = jax.random.split(jax.random.key(seed), 14)
    return {
        "tokens_in": noise(splits[0], (TOKENS, D), 1.0, 6.0, ((0, 32),)),
        "out_grad": noise(splits[1], (TOKENS, D), 1.0, 6.0, ((0, 32),)),
        "lengths": jax.vmap(lambda own: ragged_sizes(own, IMG_DEV, TOK_DEV, IMG_TOKENS, 1))(jax.random.split(splits[2], N_DP)).reshape((N_DP, IMG_DEV)).astype(jnp.int32),
        "owners": draw_owners(jax.random.fold_in(splits[13], 71), 0),
        "weight_store": draw_weight_store(jax.random.fold_in(splits[13], 71), 0),
        "first_store": draw_first_store(jax.random.fold_in(splits[13], 71), 0),
        "second_store": draw_second_store(jax.random.fold_in(splits[13], 71), 0),
        "shared_params": draw_shared_params(jax.random.fold_in(splits[13], 71), 0),
        "shared_first": draw_shared_first(jax.random.fold_in(splits[13], 71), 0),
        "shared_second": draw_shared_second(jax.random.fold_in(splits[13], 71), 0),
        "split_params": noise(splits[10], (LAYERS, N_TENSOR, SPLIT_DEV), 0.5, 3.0, ((1, 4),), jnp.float32),
        "split_first": draw_split_first(jax.random.fold_in(splits[13], 71), 0),
        "split_second": draw_split_second(jax.random.fold_in(splits[13], 71), 0),
    }


@jax.custom_vjp
def low(v):
    return lax.optimization_barrier(v.astype(jnp.bfloat16)).astype(jnp.float32)

@jax.custom_vjp
def low_back(v):
    return v

def low_keep(v):
    return (low(v), None)

def low_pass(kept, grad):
    return (grad,)

def back_keep(v):
    return (v, None)

def back_low(kept, grad):
    return (low(grad),)
low.defvjp(low_keep, low_pass)
low_back.defvjp(back_keep, back_low)
norm_eps = 1e-06
beta_first = 0.5
beta_second = 0.5
adam_eps = 1e-08
rate_matrix = 0.05
rate_small = 0.3
weight_decay = 0.05
masked_score = -1e+30
highest = lax.Precision.HIGHEST

def norm_rows(values, gain, shift):
    center = values - lax.optimization_barrier(jnp.mean(values, axis=-1, keepdims=True))
    spread = lax.optimization_barrier(jnp.mean(center * center, axis=-1, keepdims=True))
    return center * lax.rsqrt(spread + norm_eps) * gain + shift

def image_layout(row_lengths, count):
    row_lengths = row_lengths.astype(jnp.int32)
    endings = jnp.cumsum(row_lengths).astype(jnp.int32)
    openings = (endings - row_lengths).astype(jnp.int32)
    places = jnp.arange(count, dtype=jnp.int32)
    inside = places[:, None] >= openings[None, :]
    segment = (lax.optimization_barrier(jnp.sum(inside.astype(jnp.int32), axis=1)) - 1).astype(jnp.int32)
    opening = lax.optimization_barrier(jnp.max(jnp.where(inside, openings[None, :], 0), axis=1)).astype(jnp.int32)
    return (segment, (places - opening).astype(jnp.int32))

def relative_index(query_pos, key_pos):
    side = 2 * GRID - 1
    query_row = (query_pos - 1) // GRID
    query_col = (query_pos - 1) % GRID
    key_row = (key_pos - 1) // GRID
    key_col = (key_pos - 1) % GRID
    inner = (query_row[:, None] - key_row[None, :] + GRID - 1) * side + (query_col[:, None] - key_col[None, :] + GRID - 1)
    inner = jnp.where(key_pos[None, :] == 0, RELS - 2, inner)
    inner = jnp.where(query_pos[:, None] == 0, RELS - 3, inner)
    inner = jnp.where((query_pos[:, None] == 0) & (key_pos[None, :] == 0), RELS - 1, inner)
    return inner.astype(jnp.int32)

def unit_slots(owners):
    order = jnp.arange(UNITS, dtype=jnp.int32)
    same_owner = owners[:, None] == owners[None, :]
    earlier = order[None, :] < order[:, None]
    rank = lax.optimization_barrier(jnp.sum((same_owner & earlier).astype(jnp.int32), axis=1)).astype(jnp.int32)
    return (owners * CAP + rank).astype(jnp.int32)

def build_matrices(units):
    heads_here = HEADS // N_TENSOR
    counts = [3 * heads_here, heads_here, FF // (N_TENSOR * HEAD), FF // (N_TENSOR * HEAD)]
    whole = []
    offset = 0
    for level in range(LAYERS):
        for kind in range(4):
            count = counts[kind]
            blocks = units[offset:offset + count]
            offset += count
            shards = blocks.reshape(count, N_TENSOR, HEAD, D).transpose(1, 0, 2, 3)
            if kind == 0:
                whole.append(shards.reshape(N_TENSOR, 3, heads_here, HEAD, D).transpose(1, 0, 2, 3, 4).reshape(3, HEADS * HEAD, D))
            else:
                whole.append(shards.reshape(N_TENSOR * count * HEAD, D))
    return whole

def unpack_split(split_row):
    width_here = HEADS // N_TENSOR * HEAD
    hidden_here = FF // N_TENSOR
    query_bias = split_row[:, :width_here].reshape(HEADS * HEAD)
    value_bias = split_row[:, width_here:2 * width_here].reshape(HEADS * HEAD)
    up_bias = split_row[:, 2 * width_here:2 * width_here + hidden_here].reshape(FF)
    table = split_row[:, 2 * width_here + hidden_here:].reshape(HEADS, RELS)
    return (query_bias, value_bias, up_bias, table)

def block_layer(resid, weights, shared, split_row, same_image, position_index):
    qkv_weight, proj_weight, up_weight, down_weight = weights
    query_bias, value_bias, up_bias, table = unpack_split(split_row)
    count = resid.shape[0]
    normed = low(norm_rows(resid, shared[0], shared[1]))
    queries = low_back(low(jnp.dot(normed, qkv_weight[0].T, precision=highest) + query_bias))
    keys = low_back(low(jnp.dot(normed, qkv_weight[1].T, precision=highest)))
    values = low_back(low(jnp.dot(normed, qkv_weight[2].T, precision=highest) + value_bias))
    query_heads = queries.reshape(count, HEADS, HEAD)
    key_heads = keys.reshape(count, HEADS, HEAD)
    value_heads = values.reshape(count, HEADS, HEAD)
    scores = jnp.einsum('qhd,khd->hqk', query_heads, key_heads, precision=highest) * HEAD ** (-0.5) + table[:, position_index]
    scores = low_back(scores)
    scores = jnp.where(same_image[None], scores, masked_score)
    largest = lax.optimization_barrier(jnp.max(scores, axis=-1, keepdims=True))
    expo = jnp.exp(scores - largest)
    probs = low(expo / lax.optimization_barrier(jnp.sum(expo, axis=-1, keepdims=True)))
    mixed = jnp.einsum('hqk,khd->qhd', probs, value_heads, precision=highest).reshape(count, HEADS * HEAD)
    mixed = low_back(low(mixed))
    attention = low_back(jnp.dot(mixed, proj_weight, precision=highest)) + shared[3]
    middle = resid + shared[2] * attention
    normed_two = low(norm_rows(middle, shared[4], shared[5]))
    hidden = low_back(jnp.dot(normed_two, up_weight.T, precision=highest)) + up_bias
    active = low(jax.nn.gelu(hidden, approximate=False))
    output = low_back(jnp.dot(active, down_weight, precision=highest)) + shared[7]
    return middle + shared[6] * output

def adam_step(weight, first, second, grad, rate, decay):
    first_new = beta_first * first + (1.0 - beta_first) * grad
    second_new = beta_second * second + (1.0 - beta_second) * grad * grad
    fix_first = 1.0 - beta_first ** STEP
    fix_second = 1.0 - beta_second ** STEP
    weight_new = weight - rate * (first_new / fix_first / (jnp.sqrt(second_new / fix_second) + adam_eps) + decay * weight)
    return (first_new, second_new, weight_new)

def reference(tokens_in, out_grad, lengths, owners, weight_store, first_store, second_store, shared_params, shared_first, shared_second, split_params, split_first, split_second):
    slots = unit_slots(owners.astype(jnp.int32))

    def forward(store, shared_all, split_all, tokens):
        weights = build_matrices(jnp.take(store, slots, axis=0))
        packed = tokens.reshape(N_DP, TOK_DEV, D)

        def one_row(carried):
            resid, row_lengths = carried
            segment, position = image_layout(row_lengths, TOK_DEV)
            same_image = segment[:, None] == segment[None, :]
            position_index = relative_index(position, position)
            for level in range(LAYERS):
                resid = block_layer(resid, weights[4 * level:4 * level + 4], shared_all[level], split_all[level], same_image, position_index)
            return resid
        return lax.map(jax.checkpoint(one_row), (packed, lengths)).reshape(TOKENS, D)
    result, pullback = jax.vjp(forward, weight_store, shared_params, split_params, tokens_in.astype(jnp.float32))
    store_grad, shared_grad, split_grad, input_grad = pullback(out_grad.astype(jnp.float32))
    used = jnp.any(jnp.arange(SLOTS, dtype=jnp.int32)[:, None] == slots[None, :], axis=1)[:, None, None]
    zeros = jnp.zeros_like(weight_store)
    matrix_first, matrix_second, matrix_weight = adam_step(weight_store, first_store, second_store, store_grad, rate_matrix, weight_decay)
    shared_moment, shared_square, shared_value = adam_step(shared_params, shared_first, shared_second, shared_grad, rate_small, 0.0)
    split_moment, split_square, split_value = adam_step(split_params, split_first, split_second, split_grad, rate_small, 0.0)
    return (result.astype(jnp.bfloat16), input_grad, jnp.where(used, store_grad, zeros), jnp.where(used, matrix_first, zeros), jnp.where(used, matrix_second, zeros), jnp.where(used, matrix_weight, zeros), shared_grad, shared_moment, shared_square, shared_value, split_grad, split_moment, split_square, split_value)
```

```python
import jax
import jax.numpy as jnp
from jax import lax
from jax.experimental import pallas as pl
from jax.experimental.pallas import tpu as pltpu
from jax.sharding import Mesh
from jax.sharding import PartitionSpec as P

D = 768
HEADS = 12
HEAD = 64
FF = 3072
GRID = 14
LAYERS = 2
STEP = 10
RELS = 732
SIDE = 2 * GRID - 1

PITCH = 16
CODES = 256
CLASS_CODE = GRID * PITCH
SPREAD = 512

norm_eps = 1e-06
beta_first = 0.5
beta_second = 0.5
adam_eps = 1e-08
rate_matrix = 0.05
rate_small = 0.3
weight_decay = 0.05
masked_score = -1e30

f32 = jnp.float32
bf16 = jnp.bfloat16
MIB = 1 << 20


def iota(shape, axis):
    return lax.broadcasted_iota(jnp.int32, shape, axis)


def matmul(a, b):
    return jnp.dot(a, b, preferred_element_type=f32)


def matmul_nt(a, b):
    return lax.dot_general(a, b, (((1,), (1,)), ((), ())), preferred_element_type=f32)


def matmul_tn(a, b):
    return lax.dot_general(a, b, (((0,), (0,)), ((), ())), preferred_element_type=f32)


def two_parts(v):
    high = v.astype(bf16)
    return high, (v - high.astype(f32)).astype(bf16)


def call(kernel, outs, args, name, flops, scratch=(), smem=(), limit=48):
    specs = [
        pl.BlockSpec(memory_space=pltpu.SMEM if i in smem else pltpu.VMEM)
        for i in range(len(args))
    ]
    shapes = [jax.ShapeDtypeStruct(s, d) for s, d in outs]
    moved = sum(a.size * a.dtype.itemsize for a in args)
    moved += sum(s.size * s.dtype.itemsize for s in shapes)
    return pl.pallas_call(
        kernel,
        out_shape=shapes,
        in_specs=specs,
        out_specs=[pl.BlockSpec(memory_space=pltpu.VMEM)] * len(shapes),
        scratch_shapes=list(scratch),
        compiler_params=pltpu.CompilerParams(vmem_limit_bytes=limit * MIB),
        cost_estimate=pl.CostEstimate(
            flops=int(flops), bytes_accessed=int(moved), transcendentals=0
        ),
        name=name,
    )(*args)


def swap(v, axis):
    return lax.ppermute(v, axis, [(0, 1), (1, 0)])


def gather_rows(piece):
    nz = lax.axis_size("z")
    parts = [piece]
    for s in range(1, nz):
        parts.append(lax.ppermute(piece, "z", [((i + s) % nz, i) for i in range(nz)]))
    here = jnp.stack(parts)
    return here, swap(here, "x")


def reduce_rows(keep, send):
    nz = lax.axis_size("z")
    got = swap(send, "x")
    part = (keep.astype(f32) + got.astype(f32)).astype(bf16)
    total = part[:, 0].astype(f32)
    for s in range(1, nz):
        total = total + lax.ppermute(
            part[:, s], "z", [(i, (i + s) % nz) for i in range(nz)]
        ).astype(f32)
    return total.astype(bf16)


def sum_over(v, axis):
    size = lax.axis_size(axis)
    step = 1
    while step < size:
        v = v + lax.ppermute(v, axis, [(i, i ^ step) for i in range(size)])
        step *= 2
    return v


def permute_kernel(index, source, out):
    def body(i, carry):
        out[i] = source[index[i]]
        return carry

    lax.fori_loop(0, out.shape[0], body, 0)


def permute_blocks(source, index, name):
    count = index.shape[0]
    return call(
        permute_kernel, [((count,) + source.shape[1:], source.dtype)], [index, source], name, 0, smem=(0,)
    )[0]


def bias_kernel(table, ends, code_c, seg_c, code_r, seg_r, bias, hot, hot_t, spread, tile):
    count = table.shape[0]
    tokens = code_c.shape[0]
    hot[...] = jnp.where(code_c[...] == iota((tokens, CODES), 1), 1.0, 0.0).astype(bf16)
    hot_t[...] = jnp.where(code_r[...] == iota((CODES, tokens), 0), 1.0, 0.0).astype(bf16)
    lift = jnp.where(iota((128, SPREAD), 1) // PITCH == iota((128, SPREAD), 0), 1.0, 0.0).astype(bf16)
    high, low = two_parts(table[...].reshape(count * 32, 128))
    lifted = (matmul(high, lift) + matmul(low, lift)).reshape(count, 32, SPREAD)
    offset = iota((32, SPREAD), 0) + (iota((32, SPREAD), 1) % PITCH) - (GRID - 1)
    spread[...] = jnp.zeros(spread.shape, f32)
    for c in range(GRID):
        spread[:, c, :] = jnp.sum(jnp.where((offset == c)[None], lifted, 0.0), axis=1)
    row = iota((CODES, CODES), 0)
    col = iota((CODES, CODES), 1)

    def one(h, carry):
        lines = spread[h]
        for r in range(GRID):
            back = (GRID - 1 - r) * PITCH
            moved = pltpu.roll(lines, (SPREAD - back) % SPREAD, 1) if back else lines
            tile[r * PITCH : (r + 1) * PITCH, :] = moved[:, :CODES]
        tile[CLASS_CODE:, :] = jnp.zeros((CODES - CLASS_CODE, CODES), f32)
        full = jnp.where(row == CLASS_CODE, ends[h, 0], tile[...])
        full = jnp.where(col == CLASS_CODE, ends[h, 1], full)
        full = jnp.where((col == CLASS_CODE) & (row == CLASS_CODE), ends[h, 2], full)
        high, low = two_parts(full)
        left_high = matmul(hot[...], high).astype(bf16)
        left_low = matmul(hot[...], low).astype(bf16)
        values = matmul(left_high, hot_t[...]) + matmul(left_low, hot_t[...])
        bias[h] = jnp.where(seg_c[...] == seg_r[...], values, masked_score)
        return carry

    lax.fori_loop(0, count, one, 0)


def attention_kernel(a0, a1, w_qkv, bias_q, bias_v, bias, w_out, qkv, mixed, logs, keep, send):
    half = a0.shape[0]
    heads = bias.shape[0]
    width = heads * HEAD
    for i, a in enumerate((a0, a1)):
        rows = pl.ds(i * half, half)
        proj = matmul_nt(a[...], w_qkv[...])
        qkv[rows, :width] = (proj[:, :width] + bias_q[...]).astype(bf16)
        qkv[rows, width : 2 * width] = proj[:, width : 2 * width].astype(bf16)
        qkv[rows, 2 * width :] = (proj[:, 2 * width :] + bias_v[...]).astype(bf16)
    outs = []
    for h in range(heads):
        q = qkv[:, h * HEAD : (h + 1) * HEAD] * jnp.asarray(HEAD**-0.5, bf16)
        k = qkv[:, width + h * HEAD : width + (h + 1) * HEAD]
        v = qkv[:, 2 * width + h * HEAD : 2 * width + (h + 1) * HEAD]
        s = matmul_nt(q, k) + bias[h]
        top = jnp.max(s, axis=-1, keepdims=True)
        e = jnp.exp(s - top)
        total = jnp.sum(e, axis=-1, keepdims=True)
        p = (e * (1.0 / total)).astype(bf16)
        outs.append(matmul(p, v))
        logs[:, h : h + 1] = top + jnp.log(total)
    mixed[...] = jnp.concatenate(outs, axis=1).astype(bf16)
    keep[...] = matmul(mixed[:half, :], w_out[...]).astype(bf16)
    send[...] = matmul(mixed[half:, :], w_out[...]).astype(bf16)


def attention_back_kernel(
    e0, e1, w_out, qkv, logs, bias, w_qkv, d_qkv, d_scores, keep, send
):
    half = e0.shape[0]
    heads = bias.shape[0]
    width = heads * HEAD
    scale = HEAD**-0.5
    d_mixed = jnp.concatenate(
        [matmul_nt(e0[...], w_out[...]), matmul_nt(e1[...], w_out[...])], axis=0
    ).astype(bf16)
    dq, dk, dv = [], [], []
    for h in range(heads):
        q = qkv[:, h * HEAD : (h + 1) * HEAD] * jnp.asarray(scale, bf16)
        k = qkv[:, width + h * HEAD : width + (h + 1) * HEAD]
        v = qkv[:, 2 * width + h * HEAD : 2 * width + (h + 1) * HEAD]
        g = d_mixed[:, h * HEAD : (h + 1) * HEAD]
        p = jnp.exp(matmul_nt(q, k) + bias[h] - logs[:, h : h + 1])
        dp = matmul_nt(g, v)
        pdp = p * dp
        ds = (pdp - p * jnp.sum(pdp, axis=-1, keepdims=True)).astype(bf16)
        d_scores[h] = ds
        dq.append(matmul(ds, k) * scale)
        dk.append(matmul_tn(ds, q))
        dv.append(matmul_tn(p.astype(bf16), g))
    d_qkv[...] = jnp.concatenate(dq + dk + dv, axis=1).astype(bf16)
    keep[...] = matmul(d_qkv[:half, :], w_qkv[...]).astype(bf16)
    send[...] = matmul(d_qkv[half:, :], w_qkv[...]).astype(bf16)


def attention_weights_kernel(
    d_qkv, mixed, a0, a1, e0, e1, d_scores, hot, hot_t, d_w, d_bias, d_table, d_ends
):
    half = a0.shape[0]
    heads = d_scores.shape[0]
    width = heads * HEAD
    d_w[: 3 * width, :] = (
        matmul_tn(d_qkv[:half, :], a0[...]) + matmul_tn(d_qkv[half:, :], a1[...])
    ).astype(bf16)
    d_w[3 * width :, :] = (
        matmul_tn(mixed[:half, :], e0[...]) + matmul_tn(mixed[half:, :], e1[...])
    ).astype(bf16)
    d_bias[...] = jnp.sum(d_qkv[...].astype(f32), axis=0, keepdims=True)
    lift = jnp.where(iota((128, SPREAD), 1) // PITCH == iota((128, SPREAD), 0), 1.0, 0.0).astype(bf16)
    offset = iota((32, SPREAD), 0) + (iota((32, SPREAD), 1) % PITCH) - (GRID - 1)
    row = iota((CODES, CODES), 0)
    col = iota((CODES, CODES), 1)
    for h in range(heads):
        high, low = two_parts(matmul(hot_t[...], d_scores[h]))
        tile = matmul(high, hot[...]) + matmul(low, hot[...])
        class_row = jnp.where(row == CLASS_CODE, tile, 0.0)
        class_col = jnp.where(col == CLASS_CODE, tile, 0.0)
        both = jnp.where(col == CLASS_CODE, class_row, 0.0)
        both_sum = jnp.sum(both, keepdims=True)
        row_sum = jnp.sum(class_row, keepdims=True) - both_sum
        col_sum = jnp.sum(class_col, keepdims=True) - both_sum
        lane = iota((1, 128), 1)
        d_ends[h] = jnp.where(
            lane == 0, row_sum, jnp.where(lane == 1, col_sum, jnp.where(lane == 2, both_sum, 0.0))
        )
        inner = jnp.where((row < CLASS_CODE) & (col < CLASS_CODE), tile, 0.0)
        lines = jnp.zeros((PITCH, SPREAD), f32)
        for r in range(GRID):
            wide = jnp.concatenate(
                [inner[r * PITCH : (r + 1) * PITCH, :], jnp.zeros((PITCH, SPREAD - CODES), f32)],
                axis=1,
            )
            shift = (GRID - 1 - r) * PITCH
            lines = lines + (pltpu.roll(wide, shift, 1) if shift else wide)
        spread = jnp.zeros((32, SPREAD), f32)
        for c in range(GRID):
            spread = spread + jnp.where(offset == c, lines[c : c + 1, :], 0.0)
        high, low = two_parts(spread)
        d_table[h] = matmul_nt(high, lift) + matmul_nt(low, lift)


def gelu_parts(z):
    cdf = 0.5 * (1.0 + lax.erf(z * (0.5**0.5)))
    density = jnp.exp(-0.5 * z * z) * 0.3989422804014327
    return z * cdf, cdf + z * density


def hidden_kernel(c0, c1, w1a, w1b, b1, w2a, w2b, u, slope, keep, send):
    rows = c0.shape[0]
    cols = w1a.shape[0]
    for i, (c, out) in enumerate(((c0, keep), (c1, send))):
        span = pl.ds(i * rows, rows)
        total = None
        for j, (w1, w2) in enumerate(((w1a, w2a), (w1b, w2b))):
            lanes = slice(j * cols, (j + 1) * cols)
            z = matmul_nt(c[...], w1[...]) + b1[:, lanes]
            value, grade = gelu_parts(z)
            value = value.astype(bf16)
            u[span, lanes] = value
            slope[span, lanes] = grade
            part = matmul(value, w2[...])
            total = part if total is None else total + part
        out[...] = total.astype(bf16)


def hidden_back_kernel(e0, e1, w1a, w1b, w2a, w2b, slope, dz, d_b1, keep, send):
    rows = e0.shape[0]
    cols = w1a.shape[0]
    sums = []
    for i, (e, out) in enumerate(((e0, keep), (e1, send))):
        span = pl.ds(i * rows, rows)
        total = None
        for j, (w1, w2) in enumerate(((w1a, w2a), (w1b, w2b))):
            lanes = slice(j * cols, (j + 1) * cols)
            grad = matmul_nt(e[...], w2[...]) * slope[span, lanes]
            line = jnp.sum(grad, axis=0, keepdims=True)
            if i == 0:
                sums.append(line)
            else:
                d_b1[:, lanes] = sums[j] + line
            grad = grad.astype(bf16)
            dz[span, lanes] = grad
            part = matmul(grad, w1[...])
            total = part if total is None else total + part
        out[...] = total.astype(bf16)


def hidden_weights_kernel(dz, u, c0, c1, e0, e1, keep, send):
    rows = c0.shape[0]
    cols = keep.shape[1]
    for i, (left, right0, right1) in enumerate(((dz, c0, c1), (u, e0, e1))):
        for j, out in enumerate((keep, send)):
            lanes = slice(j * cols, (j + 1) * cols)
            out[i] = (
                matmul_tn(left[:rows, lanes], right0[...])
                + matmul_tn(left[rows:, lanes], right1[...])
            ).astype(bf16)


def normed(v):
    center = v - jnp.mean(v, axis=-1, keepdims=True)
    inverse = lax.rsqrt(jnp.mean(center * center, axis=-1, keepdims=True) + norm_eps)
    return center * inverse, inverse


def both_sums(ours, theirs):
    rows = ours.shape[0] // 2
    return jnp.concatenate(
        [
            ours[:rows, :].astype(f32) + theirs[rows:, :].astype(f32),
            ours[rows:, :].astype(f32) + theirs[:rows, :].astype(f32),
        ],
        axis=0,
    )


def join_kernel(ours, theirs, x, vectors, x_next, low, branch):
    rows = branch.shape[0]
    y = both_sums(ours, theirs) + vectors[1:2, :]
    branch[...] = y[:rows, :]
    value = x[...] + vectors[0:1, :] * y
    x_next[...] = value
    hat, _ = normed(value)
    low[...] = (hat * vectors[2:3, :] + vectors[3:4, :]).astype(bf16)


def join_back(d_normed, x, upper, gain, branch, scale, sums):
    hat, inverse = normed(x)
    d_hat = d_normed * gain
    mean_a = jnp.mean(d_hat, axis=-1, keepdims=True)
    mean_b = jnp.mean(d_hat * hat, axis=-1, keepdims=True)
    dx = upper + inverse * (d_hat - mean_a - hat * mean_b)
    rows = sums.shape[0] and (branch.shape[0] if branch is not None else x.shape[0])
    sums[0:1, :] = jnp.sum(d_normed[:rows, :] * hat[:rows, :], axis=0, keepdims=True)
    sums[1:2, :] = jnp.sum(d_normed[:rows, :], axis=0, keepdims=True)
    if branch is not None:
        sums[2:3, :] = jnp.sum(dx[:rows, :] * branch[...], axis=0, keepdims=True)
        sums[3:4, :] = jnp.sum(scale * dx[:rows, :], axis=0, keepdims=True)
    return dx


def join_back_kernel(ours, theirs, x, upper, vectors, branch, dx, low, sums):
    scale = vectors[1:2, :]
    value = join_back(
        both_sums(ours, theirs), x[...], upper[...], vectors[0:1, :], branch, scale, sums
    )
    dx[...] = value
    low[...] = (scale * value).astype(bf16)


def last_back_kernel(ours, theirs, x, upper, vectors, dx, sums):
    d_normed = ours[...].astype(f32) + theirs[...].astype(f32)
    dx[...] = join_back(d_normed, x[...], upper[...], vectors[0:1, :], None, None, sums)


def adam_step(weight, first, second, grad, rate, decay):
    first_new = beta_first * first + (1.0 - beta_first) * grad
    second_new = beta_second * second + (1.0 - beta_second) * grad * grad
    fix_first = 1.0 - beta_first**STEP
    fix_second = 1.0 - beta_second**STEP
    weight_new = weight - rate * (
        first_new / fix_first / (jnp.sqrt(second_new / fix_second) + adam_eps) + decay * weight
    )
    return (first_new, second_new, weight_new)


def image_layout(row_lengths, count):
    endings = jnp.cumsum(row_lengths)
    openings = endings - row_lengths
    places = jnp.arange(count, dtype=jnp.int32)
    inside = places[:, None] >= openings[None, :]
    segment = jnp.sum(inside.astype(jnp.int32), axis=1) - 1
    opening = jnp.max(jnp.where(inside, openings[None, :], 0), axis=1)
    return (segment, places - opening)


def unit_slots(owners, capacity):
    count = owners.shape[0]
    order = jnp.arange(count, dtype=jnp.int32)
    same_owner = owners[:, None] == owners[None, :]
    earlier = order[None, :] < order[:, None]
    rank = jnp.sum((same_owner & earlier).astype(jnp.int32), axis=1)
    return owners * capacity + rank


def norm_rows(values, gain, shift):
    return (normed(values)[0] * gain + shift).astype(bf16)


def per_device(
    tokens_in,
    out_grad,
    lengths,
    owners,
    weight_store,
    first_store,
    second_store,
    shared_params,
    shared_first,
    shared_second,
    split_params,
    split_first,
    split_second,
):
    nz = lax.axis_size("z")
    owners_all = nz * 2
    piece = HEAD // owners_all
    parts = 4
    heads_here = HEADS // parts
    width = heads_here * HEAD
    hidden = FF // parts
    rows = tokens_in.shape[0]
    tokens = rows * parts
    half = tokens // 2
    capacity = weight_store.shape[0]
    my_z, my_x = lax.axis_index("z"), lax.axis_index("x")
    my_y, my_c = lax.axis_index("y"), lax.axis_index("core")

    slots = unit_slots(owners, capacity)
    dealt = weight_store.astype(bf16).reshape(capacity, owners_all, piece, D).transpose(1, 0, 2, 3)
    dealt = lax.all_to_all(dealt, ("z", "x"), 0, 0, tiled=True)
    pieces = permute_blocks(dealt.reshape(-1, piece, D), slots, "deal")

    counts = [3 * heads_here + heads_here, hidden // HEAD, hidden // HEAD]
    weights = []
    offset = 0
    for level in range(LAYERS):
        groups = []
        for kind, count in enumerate(counts):
            here, other = gather_rows(pieces[offset : offset + count])
            offset += count
            if kind == 0:
                whole = jnp.stack([here, other]).transpose(2, 0, 1, 3, 4).reshape(count * HEAD, D)
                groups += [whole[: 3 * width], whole[3 * width :]]
            else:
                groups += [here.reshape(-1, D), other.reshape(-1, D)]
        weights.append(groups)

    split = split_params[:, 0, :]
    vector_units = (2 * width + hidden) // HEAD
    vectors = split[:, : vector_units * HEAD].reshape(LAYERS, vector_units, nz, 2, piece)
    vectors = jnp.roll(vectors, (-my_z, -my_x), (2, 3)).transpose(0, 1, 3, 2, 4)
    bias_q = vectors[:, :heads_here].reshape(LAYERS, 1, width)
    bias_v = vectors[:, heads_here : 2 * heads_here].reshape(LAYERS, 1, width)
    bias_1 = vectors[:, 2 * heads_here :].transpose(0, 2, 3, 1, 4).reshape(LAYERS, 1, hidden)
    table = split[:, vector_units * HEAD :].reshape(LAYERS * heads_here, RELS)
    inner = table[:, : SIDE * SIDE].reshape(-1, SIDE, SIDE)[:, ::-1, :].transpose(0, 2, 1)
    inner = jnp.pad(inner, ((0, 0), (0, 32 - SIDE), (0, 128 - SIDE)))
    ends = table[:, SIDE * SIDE :]

    segment, position = image_layout(lengths[0], tokens)
    patch = position - 1
    code = jnp.where(position == 0, CLASS_CODE, (patch // GRID) * PITCH + patch % GRID)

    def local(v):
        v = jnp.roll(v.reshape(2, 2, rows), (-my_y, -my_c), (0, 1))
        return v.transpose(1, 0, 2).reshape(tokens)

    code, segment = local(code), local(segment)
    bias, hot, hot_t = call(
        bias_kernel,
        [
            ((LAYERS * heads_here, tokens, tokens), f32),
            ((tokens, CODES), bf16),
            ((CODES, tokens), bf16),
        ],
        [inner, ends, code[:, None], segment[:, None], code[None, :], segment[None, :]],
        "position_bias",
        1e9,
        scratch=[
            pltpu.VMEM((LAYERS * heads_here, PITCH, SPREAD), f32),
            pltpu.VMEM((CODES, CODES), f32),
        ],
        smem=(1,),
    )

    both = jnp.concatenate([tokens_in, out_grad], axis=0)
    near = swap(both, "y")
    x = jnp.concatenate([tokens_in, near[:rows]], axis=0).astype(f32)
    upper = jnp.concatenate([out_grad, near[rows:]], axis=0).astype(f32)
    a0 = norm_rows(x, shared_params[0, 0], shared_params[0, 1])
    a1 = swap(a0, "core")
    last_scale = shared_params[LAYERS - 1, 6]
    e0 = (last_scale * upper).astype(bf16)
    e1 = swap(e0, "core")

    def chip_sum(keep, send):
        return (keep.astype(f32) + swap(send, "core").astype(f32)).astype(bf16)

    saved = []
    for level in range(LAYERS):
        w_qkv, w_out, w1a, w1b, w2a, w2b = weights[level]
        shared = shared_params[level]
        qkv, mixed, logs, keep, send = call(
            attention_kernel,
            [
                ((tokens, 3 * width), bf16),
                ((tokens, width), bf16),
                ((tokens, 128), f32),
                ((half, D), bf16),
                ((half, D), bf16),
            ],
            [
                a0,
                a1,
                w_qkv,
                bias_q[level],
                bias_v[level],
                bias[level * heads_here : (level + 1) * heads_here],
                w_out,
            ],
            "attention",
            9e8,
        )
        ours = chip_sum(keep, send)
        theirs = swap(ours, "y")
        x_mid, c0, branch = call(
            join_kernel,
            [((half, D), f32), ((half, D), bf16), ((rows, D), f32)],
            [ours, theirs, x, shared[2:6]],
            "join",
            1e6,
        )
        c1 = swap(c0, "core")
        u, slope, keep, send = call(
            hidden_kernel,
            [
                ((tokens, hidden), bf16),
                ((tokens, hidden), f32),
                ((half, D), bf16),
                ((half, D), bf16),
            ],
            [c0, c1, w1a, w1b, bias_1[level], w2a, w2b],
            "hidden",
            12e8,
        )
        ours = chip_sum(keep, send)
        state = [x, a0, a1, qkv, mixed, logs, branch, x_mid, c0, c1, u, slope]
        if level + 1 < LAYERS:
            theirs = swap(ours, "y")
            following = shared_params[level + 1]
            x, a0, branch_two = call(
                join_kernel,
                [((half, D), f32), ((half, D), bf16), ((rows, D), f32)],
                [ours, theirs, x_mid, jnp.concatenate([shared[6:8], following[0:2]], axis=0)],
                "join",
                1e6,
            )
            a1 = swap(a0, "core")
        else:
            theirs = swap(ours[rows:], "y")
            branch_two = ours[:rows].astype(f32) + theirs.astype(f32) + shared[7]
            block_out = (x_mid[:rows] + shared[6] * branch_two).astype(bf16)
        saved.append(state + [branch_two])

    last_branch = saved[LAYERS - 1][-1]
    own_grad = out_grad.astype(f32)
    scale_two = jnp.sum(own_grad * last_branch, axis=0)
    shift_out = jnp.sum(last_scale * own_grad, axis=0)
    pieces_grad = [None] * LAYERS
    shared_grads = [None] * LAYERS
    split_grads = [None] * LAYERS
    for level in reversed(range(LAYERS)):
        w_qkv, w_out, w1a, w1b, w2a, w2b = weights[level]
        shared = shared_params[level]
        x, a0, a1, qkv, mixed, logs, branch, x_mid, c0, c1, u, slope, _ = saved[level]
        dz, d_b1, keep, send = call(
            hidden_back_kernel,
            [
                ((tokens, hidden), bf16),
                ((1, hidden), f32),
                ((half, D), bf16),
                ((half, D), bf16),
            ],
            [e0, e1, w1a, w1b, w2a, w2b, slope],
            "hidden_back",
            12e8,
        )
        ours = chip_sum(keep, send)
        theirs = swap(ours, "y")
        keep_w, send_w = call(
            hidden_weights_kernel,
            [((2, hidden // 2, D), bf16)] * 2,
            [dz, u, c0, c1, e0, e1],
            "hidden_weights",
            12e8,
        )
        shape = (2, nz, hidden // (2 * nz), D)
        hidden_grad = reduce_rows(keep_w.reshape(shape), send_w.reshape(shape))
        d_mid, e0, sums_two = call(
            join_back_kernel,
            [((half, D), f32), ((half, D), bf16), ((4, D), f32)],
            [ours, theirs, x_mid, upper, jnp.stack([shared[4], shared[2]]), branch],
            "join_back",
            1e6,
        )
        e1 = swap(e0, "core")
        d_qkv, d_scores, keep, send = call(
            attention_back_kernel,
            [
                ((tokens, 3 * width), bf16),
                ((heads_here, tokens, tokens), bf16),
                ((half, D), bf16),
                ((half, D), bf16),
            ],
            [
                e0,
                e1,
                w_out,
                qkv,
                logs,
                bias[level * heads_here : (level + 1) * heads_here],
                w_qkv,
            ],
            "attention_back",
            12e8,
        )
        ours = chip_sum(keep, send)
        if level > 0:
            theirs = swap(ours, "y")
        else:
            theirs = swap(ours[rows:], "y")
        d_w, d_bias, d_table, d_ends = call(
            attention_weights_kernel,
            [
                ((4 * width, D), bf16),
                ((1, 3 * width), f32),
                ((heads_here, 32, 128), f32),
                ((heads_here, 1, 128), f32),
            ],
            [d_qkv, mixed, a0, a1, e0, e1, d_scores, hot, hot_t],
            "attention_weights",
            12e8,
        )
        units = d_w.reshape(4 * heads_here, 2, nz, piece, D)
        attention_grad = reduce_rows(units[:, 0], units[:, 1])
        if level > 0:
            below = shared_params[level - 1]
            upper, e0, sums_one = call(
                join_back_kernel,
                [((half, D), f32), ((half, D), bf16), ((4, D), f32)],
                [ours, theirs, x, d_mid, jnp.stack([shared[0], below[6]]), saved[level - 1][-1]],
                "join_back",
                1e6,
            )
            e1 = swap(e0, "core")
        else:
            input_grad, sums_one = call(
                last_back_kernel,
                [((rows, D), f32), ((2, D), f32)],
                [ours[:rows], theirs, x[:rows], d_mid[:rows], shared[0:1]],
                "last_back",
                1e6,
            )
        shared_grads[level] = jnp.concatenate(
            [sums_one[0:2], sums_two[2:4], sums_two[0:2], jnp.stack([scale_two, shift_out])], axis=0
        )
        if level > 0:
            scale_two, shift_out = sums_one[2], sums_one[3]
        bias_1_grad = d_b1.reshape(2, nz, hidden // HEAD, piece).transpose(2, 0, 1, 3)
        d_vectors = jnp.concatenate(
            [
                d_bias[0, :width].reshape(-1, 2, nz, piece),
                d_bias[0, 2 * width :].reshape(-1, 2, nz, piece),
                bias_1_grad,
            ],
            axis=0,
        ).transpose(0, 2, 1, 3)
        d_vectors = jnp.roll(d_vectors, (my_z, my_x), (1, 2)).reshape(-1)
        d_inner = d_table[:, :SIDE, :SIDE].transpose(0, 2, 1)[:, ::-1, :].reshape(heads_here, -1)
        d_rel = jnp.concatenate([d_inner, d_ends[:, 0, :3]], axis=1).reshape(-1)
        split_grads[level] = jnp.concatenate([d_vectors, d_rel])
        pieces_grad[level] = jnp.concatenate(
            [attention_grad, hidden_grad.reshape(-1, piece, D)], axis=0
        )

    shared_part = jnp.concatenate(shared_grads, axis=0)
    shared_part = sum_over(sum_over(shared_part, "core"), "y")
    split_flat = jnp.stack(split_grads).reshape(-1)
    split_rows = -(-split_flat.shape[0] // D)
    split_part = jnp.pad(split_flat, (0, split_rows * D - split_flat.shape[0])).reshape(-1, D)
    small = sum_over(sum_over(jnp.concatenate([shared_part, split_part], axis=0), "x"), "z")
    shared_total = small[: shared_part.shape[0]].reshape(shared_params.shape)
    split_total = (
        small[shared_part.shape[0] :].reshape(-1)[: split_flat.shape[0]].reshape(split_params.shape)
    )

    all_pieces = jnp.concatenate(pieces_grad, axis=0)
    slot_ids = jnp.arange(owners_all * capacity, dtype=jnp.int32)
    match_all = slot_ids[:, None] == slots[None, :]
    unit_ids = jnp.arange(slots.shape[0], dtype=jnp.int32)
    unit_of = jnp.sum(jnp.where(match_all, unit_ids[None, :], 0), axis=1)
    by_slot = permute_blocks(all_pieces, unit_of, "to_slots").reshape(
        owners_all, capacity, piece, D
    )
    mine = lax.all_to_all(by_slot, ("z", "x"), 0, 0, tiled=True)
    mine = mine.transpose(1, 0, 2, 3).reshape(capacity, HEAD, D).astype(f32)
    my_ids = (my_z * 2 + my_x) * capacity + jnp.arange(capacity, dtype=jnp.int32)
    used = jnp.any(my_ids[:, None] == slots[None, :], axis=1)[:, None, None]
    zeros = jnp.zeros_like(weight_store)
    mine = jnp.where(used, mine, zeros)
    matrix_first, matrix_second, matrix_weight = adam_step(
        weight_store, first_store, second_store, mine, rate_matrix, weight_decay
    )
    shared_moment, shared_square, shared_value = adam_step(
        shared_params, shared_first, shared_second, shared_total, rate_small, 0.0
    )
    split_moment, split_square, split_value = adam_step(
        split_params, split_first, split_second, split_total, rate_small, 0.0
    )
    return (
        block_out,
        input_grad,
        mine,
        jnp.where(used, matrix_first, zeros),
        jnp.where(used, matrix_second, zeros),
        jnp.where(used, matrix_weight, zeros),
        shared_total,
        shared_moment,
        shared_square,
        shared_value,
        split_total,
        split_moment,
        split_square,
        split_value,
    )


def solution(mesh):
    dp, tensor = mesh.shape["dp"], mesh.shape["tensor"]
    fine = Mesh(mesh.devices.reshape(dp // 2, 2, tensor // 2, 2), ("z", "x", "y", "core"))
    data, split = ("z", "x"), ("y", "core")
    tokens = P(data + split, None)
    store = P(data, split, None)
    shards = P(None, split, None)
    return jax.shard_map(
        per_device,
        mesh=fine,
        in_specs=(tokens, tokens, P(data, None), P(), store, store, store, P(), P(), P())
        + (shards,) * 3,
        out_specs=(tokens, tokens) + (store,) * 4 + (P(),) * 4 + (shards,) * 4,
        check_vma=False,
    )
```

```python
import functools

import jax
import jax.numpy as jnp
from jax import lax
from jax.experimental import pallas as pl
from jax.experimental.pallas import tpu as pltpu
from jax.sharding import Mesh
from jax.sharding import PartitionSpec as P

D = 768
HEADS = 12
HEAD = 64
FF = 3072
GRID = 14
LAYERS = 2
STEP = 10
RELS = 732
SIDE = 2 * GRID - 1

PITCH = 16
CODES = 256
CLASS_CODE = GRID * PITCH
SPREAD = 512

PACK_B1 = 5
PACK_TABLE = 11
PACK_ENDS = 43
PACKED = 48

norm_eps = 1e-06
beta_first = 0.5
beta_second = 0.5
adam_eps = 1e-08
rate_matrix = 0.05
rate_small = 0.3
weight_decay = 0.05
masked_score = -1e30

f32 = jnp.float32
bf16 = jnp.bfloat16
MIB = 1 << 20
SCALE = 1e9


def iota(shape, axis):
    return lax.broadcasted_iota(jnp.int32, shape, axis)


def matmul(a, b):
    return jnp.dot(a, b, preferred_element_type=f32)


def matmul_nt(a, b):
    return lax.dot_general(a, b, (((1,), (1,)), ((), ())), preferred_element_type=f32)


def matmul_tn(a, b):
    return lax.dot_general(a, b, (((0,), (0,)), ((), ())), preferred_element_type=f32)


def two_parts(v):
    high = v.astype(bf16)
    return high, (v - high.astype(f32)).astype(bf16)


VMEM, SMEM, STAY, FAR = "vmem", "smem", "stay", "far"


def call(kernel, outs, args, name, us, scratch=(), limit=16, alias=None, **options):
    args = [a if isinstance(a, tuple) else (a, VMEM) for a in args]
    spaces = {VMEM: pltpu.VMEM, SMEM: pltpu.SMEM, FAR: pltpu.HBM}
    colors = {STAY: pltpu.VMEM, FAR: pltpu.HBM, VMEM: jax.ShapeDtypeStruct}
    in_specs = [pl.BlockSpec(memory_space=spaces[place]) for _, place in args]
    args = [
        (pltpu.with_memory_space_constraint(a, pltpu.HBM) if place == FAR else a, place)
        for a, place in args
    ]
    outs = [out if len(out) == 3 else (*out, VMEM) for out in outs]
    shapes = [colors[place](shape, dtype) for shape, dtype, place in outs]
    return pl.pallas_call(
        functools.partial(kernel, **options),
        out_shape=shapes,
        in_specs=in_specs,
        out_specs=[
            pl.BlockSpec(memory_space=pltpu.HBM if place == FAR else pltpu.VMEM) for _, _, place in outs
        ],
        scratch_shapes=list(scratch),
        input_output_aliases={alias + i: i for i in range(len(outs))} if alias is not None else {},
        compiler_params=pltpu.CompilerParams(vmem_limit_bytes=limit * MIB),
        cost_estimate=pl.CostEstimate(flops=int(us * SCALE), bytes_accessed=1, transcendentals=0),
        name=name,
    )(*[a for a, _ in args])


def swap(v, axis):
    return lax.ppermute(v, axis, [(0, 1), (1, 0)])


class Line:
    def __init__(self, ahead=1):
        self.come, self.ahead = [], ahead

    def send(self, v, axis, perm):
        if len(self.come) >= self.ahead:
            v = after(v, self.come[-self.ahead])
        self.come.append(lax.ppermute(v, axis, perm))
        return self.come[-1]


SWAP = [(0, 1), (1, 0)]
AHEAD = 1


def spans(order, capacity):
    pieces = []
    for s, parts in order:
        cuts = [capacity * i // parts for i in range(parts + 1)]
        pieces += [(s, a, b) for a, b in zip(cuts, cuts[1:])]
    return pieces


def gather_order(nz, capacity):
    if nz != 4:
        return spans([(s, 1) for s in range(nz)], capacity)
    return spans([(0, 1), (1, 1), (2, 2), (3, 2)], capacity)


def scatter_order(nz, capacity):
    if nz != 4:
        return spans([(s, 1) for s in range(1, nz)] + [(0, 1)], capacity)
    return spans([(2, 2), (1, 1), (3, 1), (0, 1)], capacity)


def gather_stores(store, order):
    nz = lax.axis_size("z")
    along_z, along_x = Line(AHEAD), Line()
    near, far = [], []
    for s, start, stop in order:
        piece = store if stop - start == store.shape[0] else store[start:stop]
        if s:
            piece = along_z.send(piece, "z", [((i + s) % nz, i) for i in range(nz)])
        near.append(piece)
        far.append(along_x.send(piece, "x", SWAP))
    return near + far


class ScatterSums:
    def __init__(self, grads, order):
        self.grads, self.order = grads, order
        self.along_z, self.along_x = Line(AHEAD), Line()
        self.totals, self.part, self.next = {}, None, 0

    def step(self):
        nz = lax.axis_size("z")
        s, _, _ = self.order[self.next]
        ours, theirs = self.grads[self.next], self.grads[len(self.order) + self.next]
        got = self.along_x.send(theirs, "x", SWAP)
        if self.part is not None:
            ours = after(ours, self.part)
        self.part = ours.astype(f32) + got.astype(f32)
        term = self.part
        if s:
            self.part = self.part.astype(bf16)
            term = self.along_z.send(self.part, "z", [(k, (k + s) % nz) for k in range(nz)])
        self.totals.setdefault(s, []).append(term)
        self.next += 1

    def result(self):
        totals = [jnp.concatenate(v, axis=0) if len(v) > 1 else v[0] for v in self.totals.values()]
        return sum(v.astype(f32) for v in totals)


def after(v, *others):
    return lax.optimization_barrier((v,) + others)[0]


def sum_over(v, axis):
    size = lax.axis_size(axis)
    step = 1
    while step < size:
        v = v + lax.ppermute(v, axis, [(i, i ^ step) for i in range(size)])
        step *= 2
    return v


def deal_kernel(near_unit, *refs, low, order):
    *blocks, first, second, third, semaphores = refs
    nz = near_unit.shape[0] // 2
    group = first.shape[0]
    outs = (first, second, third)
    for i, block in enumerate(blocks):
        s, start, stop = order[i % len(order)]
        owner = s + nz * (i // len(order))
        for k in range(stop - start):
            unit = near_unit[owner, start + k] - low
            for j, out in enumerate(outs):

                @pl.when((unit >= j * group) & (unit < (j + 1) * group))
                def _():
                    pltpu.make_async_copy(block.at[k], out.at[unit - j * group], semaphores.at[j]).start()

    for j, out in enumerate(outs):
        pltpu.make_async_copy(out, out, semaphores.at[j]).wait()


def lifting(rows):
    return jnp.where(
        SIDE - 1 - iota((rows, SPREAD), 1) // PITCH == iota((rows, SPREAD), 0), 1.0, 0.0
    ).astype(bf16)


def column_offset():
    return iota((32, SPREAD), 0) + (iota((32, SPREAD), 1) % PITCH) - (GRID - 1)


def prepare_kernel(
    table, ends, code_c, seg_c, code_r, seg_r, hot, hot_t, *rest
):
    *biases, spread, tile = rest
    heads = table.shape[0] // len(biases)
    tokens = code_c.shape[0]
    hot[...] = jnp.where(code_c[...] == iota((tokens, CODES), 1), 1.0, 0.0).astype(bf16)
    hot_t[...] = jnp.where(code_r[...] == iota((CODES, tokens), 0), 1.0, 0.0).astype(bf16)
    lift = lifting(32)
    offset = column_offset()
    spread[...] = jnp.zeros(spread.shape, f32)
    for h in range(table.shape[0]):
        high, low = two_parts(table[h])
        lifted = matmul_tn(high, lift) + matmul_tn(low, lift)
        for c in range(GRID):
            line = jnp.sum(jnp.where(offset == c, lifted, 0.0), axis=0, keepdims=True)
            spread[h, c : c + 1, :] = line
    row = iota((CODES, CODES), 0)
    col = iota((CODES, CODES), 1)
    for level, bias in enumerate(biases):

        def one(head, carry):
            h = level * heads + head
            lines = spread[h]
            for r in range(GRID):
                back = (GRID - 1 - r) * PITCH
                moved = pltpu.roll(lines, (SPREAD - back) % SPREAD, 1) if back else lines
                tile[r * PITCH : (r + 1) * PITCH, :] = moved[:, :CODES]
            tile[CLASS_CODE:, :] = jnp.zeros((CODES - CLASS_CODE, CODES), f32)
            full = jnp.where(row == CLASS_CODE, ends[h, 0], tile[...])
            full = jnp.where(col == CLASS_CODE, ends[h, 1], full)
            full = jnp.where((col == CLASS_CODE) & (row == CLASS_CODE), ends[h, 2], full)
            high, low = two_parts(full)
            left_high = matmul(hot[...], high).astype(bf16)
            left_low = matmul(hot[...], low).astype(bf16)
            values = matmul(left_high, hot_t[...]) + matmul(left_low, hot_t[...])
            bias[head] = jnp.where(seg_c[...] == seg_r[...], values, masked_score)
            return carry

        lax.fori_loop(0, heads, one, 0)


def normed(v):
    center = v - jnp.mean(v, axis=-1, keepdims=True)
    inverse = lax.rsqrt(jnp.mean(center * center, axis=-1, keepdims=True) + norm_eps)
    return center * inverse, inverse


def start_kernel(tokens, grads, near, shared, x, low, x_saved, upper, e):
    rows = tokens.shape[0]
    x[:rows, :] = tokens[...].astype(f32)
    x[rows:, :] = near[:rows, :].astype(f32)
    x_saved[...] = x[...]
    hat, _ = normed(x[...])
    low[...] = (hat * shared[0, 0:1, :] + shared[0, 1:2, :]).astype(bf16)
    upper[:rows, :] = grads[...].astype(f32)
    upper[rows:, :] = near[rows:, :].astype(f32)
    e[...] = (shared[LAYERS - 1, 6:7, :] * upper[...]).astype(bf16)


def attention_kernel(a0, a1, vector, bias, w, qkv, mixed, logs, a0_saved, a1_saved, keep, send):
    a0_saved[...] = a0[...]
    a1_saved[...] = a1[...]
    half = a0.shape[0]
    heads = bias.shape[0]
    width = heads * HEAD
    out = qkv
    for i, a in enumerate((a0, a1)):
        rows = pl.ds(i * half, half)
        proj = matmul_nt(a[...], w[: 3 * width, :]) + vector[:, : 3 * width]
        out[rows, :] = proj.astype(bf16)
    bias = bias
    parts = []
    for h in range(heads):
        q = out[:, h * HEAD : (h + 1) * HEAD] * jnp.asarray(HEAD**-0.5, bf16)
        k = out[:, width + h * HEAD : width + (h + 1) * HEAD]
        v = out[:, 2 * width + h * HEAD : 2 * width + (h + 1) * HEAD]
        s = matmul_nt(q, k) + bias[h]
        top = jnp.max(s, axis=-1, keepdims=True)
        e = jnp.exp(s - top)
        total = jnp.sum(e, axis=-1, keepdims=True)
        p = (e * (1.0 / total)).astype(bf16)
        parts.append(matmul(p, v))
        logs[:, h : h + 1] = top + jnp.log(total)
    mixed[...] = jnp.concatenate(parts, axis=1).astype(bf16)
    w_out = w[3 * width :, :]
    keep[...] = matmul(mixed[:half, :], w_out).astype(bf16)
    send[...] = matmul(mixed[half:, :], w_out).astype(bf16)


def attention_back_kernel(
    e0, e1, w_true, qkv, logs, bias, d_qkv, d_scores, e0_saved, e1_saved, keep, send
):
    e0_saved[...] = e0[...]
    e1_saved[...] = e1[...]
    half = e0.shape[0]
    heads = bias.shape[0]
    width = heads * HEAD
    scale = HEAD**-0.5
    w = w_true
    w_out = w[3 * width :, :]
    d_mixed = jnp.concatenate(
        [matmul_nt(e0[...], w_out), matmul_nt(e1[...], w_out)], axis=0
    ).astype(bf16)
    qkv, logs, bias = qkv, logs, bias
    dq, dk, dv = [], [], []
    for h in range(heads):
        q = qkv[:, h * HEAD : (h + 1) * HEAD] * jnp.asarray(scale, bf16)
        k = qkv[:, width + h * HEAD : width + (h + 1) * HEAD]
        v = qkv[:, 2 * width + h * HEAD : 2 * width + (h + 1) * HEAD]
        g = d_mixed[:, h * HEAD : (h + 1) * HEAD]
        p = jnp.exp(matmul_nt(q, k) + bias[h] - logs[:, h : h + 1])
        dp = matmul_nt(g, v)
        pdp = p * dp
        ds = (pdp - p * jnp.sum(pdp, axis=-1, keepdims=True)).astype(bf16)
        d_scores[h] = ds
        dq.append(matmul(ds, k) * scale)
        dk.append(matmul_tn(ds, q))
        dv.append(matmul_tn(p.astype(bf16), g))
    out = d_qkv
    out[...] = jnp.concatenate(dq + dk + dv, axis=1).astype(bf16)
    keep[...] = matmul(out[:half, :], w[: 3 * width, :]).astype(bf16)
    send[...] = matmul(out[half:, :], w[: 3 * width, :]).astype(bf16)


def table_kernel(d_qkv, d_b1, scores, hot, hot_t, packed):
    heads = scores.shape[0]
    width = heads * HEAD
    packed[...] = jnp.zeros(packed.shape, f32)
    line = jnp.sum(d_qkv[...].astype(f32), axis=0, keepdims=True)
    for start in range(0, 3 * width, 128):
        stop = min(start + 128, 3 * width)
        packed[start // 128 : start // 128 + 1, : stop - start] = line[:, start:stop]
    line = d_b1[...]
    for start in range(0, line.shape[1], 128):
        at = PACK_B1 + start // 128
        packed[at : at + 1, :] = line[:, start : start + 128]
    lift = lifting(32)
    offset = column_offset()
    row = iota((CODES, CODES), 0)
    col = iota((CODES, CODES), 1)
    for h in range(heads):
        high, low = two_parts(matmul(hot_t[...], scores[h]))
        tile = matmul(high, hot[...]) + matmul(low, hot[...])
        class_row = jnp.where(row == CLASS_CODE, tile, 0.0)
        class_col = jnp.where(col == CLASS_CODE, tile, 0.0)
        both = jnp.where(col == CLASS_CODE, class_row, 0.0)
        both_sum = jnp.sum(both, keepdims=True)
        row_sum = jnp.sum(class_row, keepdims=True) - both_sum
        col_sum = jnp.sum(class_col, keepdims=True) - both_sum
        lane = iota((1, 128), 1)
        packed[PACK_ENDS + h : PACK_ENDS + h + 1, :] = jnp.where(
            lane == 0, row_sum, jnp.where(lane == 1, col_sum, jnp.where(lane == 2, both_sum, 0.0))
        )
        inner = jnp.where((row < CLASS_CODE) & (col < CLASS_CODE), tile, 0.0)
        lines = jnp.zeros((PITCH, SPREAD), f32)
        for r in range(GRID):
            wide = jnp.concatenate(
                [inner[r * PITCH : (r + 1) * PITCH, :], jnp.zeros((PITCH, SPREAD - CODES), f32)],
                axis=1,
            )
            shift = (GRID - 1 - r) * PITCH
            lines = lines + (pltpu.roll(wide, shift, 1) if shift else wide)
        spread = jnp.zeros((32, SPREAD), f32)
        for c in range(GRID):
            spread = spread + jnp.where(offset == c, lines[c : c + 1, :], 0.0)
        high, low = two_parts(spread)
        packed[PACK_TABLE : PACK_TABLE + 32, 32 * h : 32 * h + 32] = matmul_nt(
            lift, high
        ) + matmul_nt(lift, low)


def gelu_parts(z):
    cdf = 0.5 * (1.0 + lax.erf(z * (0.5**0.5)))
    density = jnp.exp(-0.5 * z * z) * 0.3989422804014327
    return z * cdf, cdf + z * density


def hidden_kernel(c0, c1, b1, w1, w2, u, slope, c0_saved, c1_saved, keep, send):
    c0_saved[...] = c0[...]
    c1_saved[...] = c1[...]
    rows = c0.shape[0]
    cols = w1.shape[0] // 2
    for i, (c, out) in ((1, (c1, send)), (0, (c0, keep))):
        span = pl.ds(i * rows, rows)
        total = None
        for j in range(2):
            lanes = slice(j * cols, (j + 1) * cols)
            z = matmul_nt(c[...], w1[lanes, :]) + b1[:, lanes]
            value, grade = gelu_parts(z)
            value = value.astype(bf16)
            u[span, lanes] = value
            slope[span, lanes] = grade
            part = matmul(value, w2[lanes, :])
            total = part if total is None else total + part
        out[...] = total.astype(bf16)


def hidden_back_kernel(e0, e1, w1, w2, slope, dz, e0_saved, e1_saved, d_b1, keep, send):
    e0_saved[...] = e0[...]
    e1_saved[...] = e1[...]
    rows = e0.shape[0]
    cols = w1.shape[0] // 2
    w2, slope, w1 = w2, slope, w1
    sums = [None, None]
    for i, (e, out) in ((1, (e1, send)), (0, (e0, keep))):
        span = pl.ds(i * rows, rows)
        total = None
        for j in range(2):
            lanes = slice(j * cols, (j + 1) * cols)
            grad = matmul_nt(e[...], w2[lanes, :]) * slope[span, lanes]
            line = jnp.sum(grad, axis=0, keepdims=True)
            sums[j] = line if sums[j] is None else sums[j] + line
            grad = grad.astype(bf16)
            dz[span, lanes] = grad
            part = matmul(grad, w1[lanes, :])
            total = part if total is None else total + part
        out[...] = total.astype(bf16)
    d_b1[...] = jnp.concatenate(sums, axis=1)


def put_blocks(blocks, near_slot, first, outs, capacity, semaphore):
    for u in range(blocks.shape[0]):
        place = near_slot[first + u]
        if len(outs) == 1:
            pltpu.make_async_copy(blocks.at[u], outs[0].at[place], semaphore).start()
            continue
        for j, out in enumerate(outs):

            @pl.when((place >= j * capacity) & (place < (j + 1) * capacity))
            def _():
                pltpu.make_async_copy(blocks.at[u], out.at[place - j * capacity], semaphore).start()


def weights_kernel(near_slot, left0, right00, right01, left1, right10, right11, *refs, first, count, capacity):
    *refs, blocks, semaphore = refs
    outs = refs[-count:]
    half = right00.shape[0]
    at = 0
    for left, right0, right1 in ((left0, right00, right01), (left1, right10, right11)):
        grad = matmul_tn(left[:half, :], right0[...]) + matmul_tn(left[half:, :], right1[...])
        stop = at + grad.shape[0] // HEAD
        blocks[at:stop] = grad.astype(bf16).reshape(stop - at, HEAD, grad.shape[1])
        put_blocks(blocks.at[at:stop], near_slot, first + at, outs, capacity, semaphore)
        at = stop
    pltpu.make_async_copy(blocks, blocks, semaphore).wait()


def both_sums(ours, theirs):
    rows = ours.shape[0] // 2
    return jnp.concatenate(
        [
            ours[:rows, :].astype(f32) + theirs[rows:, :].astype(f32),
            ours[rows:, :].astype(f32) + theirs[:rows, :].astype(f32),
        ],
        axis=0,
    )


def join(level, kind):
    def kernel(ours, theirs, x, shared, x_next, low, branch, x_saved):
        rows = branch.shape[0]
        here = (level, 2, 3) if kind == 0 else (level, 6, 7)
        then = (level, 4, 5) if kind == 0 else (level + 1, 0, 1)
        y = both_sums(ours, theirs) + shared[here[0], here[2] : here[2] + 1, :]
        branch[...] = y[:rows, :]
        value = x[...] + shared[here[0], here[1] : here[1] + 1, :] * y
        x_next[...] = value
        x_saved[...] = x_next[...]
        hat, _ = normed(value)
        gain, shift = (shared[then[0], i : i + 1, :] for i in then[1:])
        low[...] = (hat * gain + shift).astype(bf16)

    return kernel


def through_norm(d_normed, x, upper, gain):
    hat, inverse = normed(x)
    d_hat = d_normed * gain
    mean_a = jnp.mean(d_hat, axis=-1, keepdims=True)
    mean_b = jnp.mean(d_hat * hat, axis=-1, keepdims=True)
    return upper + inverse * (d_hat - mean_a - hat * mean_b), d_normed * hat


def join_back(gain_at, scale_at):
    def kernel(ours, theirs, x, upper, branch, shared, dx, low, sums):
        rows = branch.shape[0]
        gain, scale = (shared[i, j : j + 1, :] for i, j in (gain_at, scale_at))
        d_normed = both_sums(ours, theirs)
        value, product = through_norm(d_normed, x[...], upper[...], gain)
        dx[...] = value
        e = scale * value
        low[...] = e.astype(bf16)
        sums[0:1, :] = jnp.sum(product[:rows, :], axis=0, keepdims=True)
        sums[1:2, :] = jnp.sum(d_normed[:rows, :], axis=0, keepdims=True)
        sums[2:3, :] = jnp.sum(value[:rows, :] * branch[...], axis=0, keepdims=True)
        sums[3:4, :] = jnp.sum(e[:rows, :], axis=0, keepdims=True)

    return kernel


def last_back_kernel(ours, theirs, x, upper, shared, dx, sums):
    rows = dx.shape[0]
    d_normed = ours[:rows, :].astype(f32) + theirs[...].astype(f32)
    value, product = through_norm(d_normed, x[:rows, :], upper[:rows, :], shared[0, 0:1, :])
    dx[...] = value
    sums[0:1, :] = jnp.sum(product, axis=0, keepdims=True)
    sums[1:2, :] = jnp.sum(d_normed, axis=0, keepdims=True)


def adam_step(weight, first, second, grad, rate, decay):
    first_new = beta_first * first + (1.0 - beta_first) * grad
    second_new = beta_second * second + (1.0 - beta_second) * grad * grad
    fix_first = 1.0 - beta_first**STEP
    fix_second = 1.0 - beta_second**STEP
    weight_new = weight - rate * (
        first_new / fix_first / (jnp.sqrt(second_new / fix_second) + adam_eps) + decay * weight
    )
    return (first_new, second_new, weight_new)


def image_layout(row_lengths, count):
    endings = jnp.cumsum(row_lengths)
    openings = endings - row_lengths
    places = jnp.arange(count, dtype=jnp.int32)
    inside = places[:, None] >= openings[None, :]
    segment = jnp.sum(inside.astype(jnp.int32), axis=1) - 1
    opening = jnp.max(jnp.where(inside, openings[None, :], 0), axis=1)
    return (segment, places - opening)


def unit_slots(owners, capacity):
    count = owners.shape[0]
    order = jnp.arange(count, dtype=jnp.int32)
    same_owner = owners[:, None] == owners[None, :]
    earlier = order[None, :] < order[:, None]
    rank = jnp.sum((same_owner & earlier).astype(jnp.int32), axis=1)
    return owners * capacity + rank


def per_device(
    tokens_in,
    out_grad,
    lengths,
    owners,
    weight_store,
    first_store,
    second_store,
    shared_params,
    shared_first,
    shared_second,
    split_params,
    split_first,
    split_second,
):
    nz = lax.axis_size("z")
    owners_all = nz * 2
    parts = 4
    heads_here = HEADS // parts
    width = heads_here * HEAD
    hidden = FF // parts
    rows = tokens_in.shape[0]
    tokens = rows * parts
    half = tokens // 2
    capacity = weight_store.shape[0]
    my_z, my_x = lax.axis_index("z"), lax.axis_index("x")
    my_y, my_c = lax.axis_index("y"), lax.axis_index("core")

    slots = unit_slots(owners, capacity)
    order = gather_order(nz, capacity)
    blocks = gather_stores(weight_store.astype(bf16), order)

    group = hidden // HEAD
    near_x = (my_x + jnp.arange(2, dtype=jnp.int32)) % 2
    near_z = (my_z + jnp.arange(nz, dtype=jnp.int32)) % nz
    owner_of = (near_z[None, :] * 2 + near_x[:, None]).reshape(-1)
    unit_ids = jnp.arange(slots.shape[0], dtype=jnp.int32)
    near_slots = owner_of[:, None] * capacity + jnp.arange(capacity, dtype=jnp.int32)[None, :]
    near_match = near_slots[:, :, None] == slots[None, None, :]
    near_unit = jnp.sum(jnp.where(near_match, unit_ids, 0), axis=2)
    near_unit = jnp.where(jnp.any(near_match, axis=2), near_unit, slots.shape[0])
    back_order = scatter_order(nz, capacity)
    in_pieces = owners_all == 8
    near_ids = [[0] * capacity for _ in range(owners_all)]
    for i, (s, start, stop) in enumerate(back_order):
        for x in range(2):
            for k in range(start, stop):
                near_ids[x * nz + s][k] = (x * len(back_order) + i) * capacity + k - start
    if not in_pieces:
        near_ids = [[p * capacity + k for k in range(capacity)] for p in range(owners_all)]
    near_ids = jnp.asarray(near_ids, jnp.int32)[:, :, None]
    near_slot = jnp.sum(jnp.where(near_match, near_ids, 0), axis=(0, 1))

    segment, position = image_layout(lengths[0], tokens)
    patch = position - 1
    code = jnp.where(position == 0, CLASS_CODE, (patch // GRID) * PITCH + patch % GRID)

    def local(v):
        v = jnp.roll(v.reshape(2, 2, rows), (-my_y, -my_c), (0, 1))
        return v.transpose(1, 0, 2).reshape(tokens)

    code, segment = local(code), local(segment)
    split = split_params[:, 0, :]
    bias_qv = jnp.concatenate(
        [split[:, :width], jnp.zeros((LAYERS, width), f32), split[:, width : 2 * width]], axis=1
    )
    bias_1 = split[:, 2 * width : 2 * width + hidden]
    table = split[:, 2 * width + hidden :].reshape(LAYERS * heads_here, RELS)
    inner = table[:, : SIDE * SIDE].reshape(-1, SIDE, SIDE)
    inner = jnp.pad(inner, ((0, 0), (0, 32 - SIDE), (0, 32 - SIDE)))
    hot, hot_t, *bias = call(
        prepare_kernel,
        [
            ((tokens, CODES), bf16, STAY),
            ((CODES, tokens), bf16, STAY),
        ]
        + [((heads_here, tokens, tokens), f32, STAY)] * LAYERS,
        [
            inner,
            (table[:, SIDE * SIDE :], SMEM),
            code[:, None],
            segment[:, None],
            code[None, :],
            segment[None, :],
        ],
        "prepare",
        6,
        scratch=[
            pltpu.VMEM((LAYERS * heads_here, PITCH, SPREAD), f32),
            pltpu.VMEM((CODES, CODES), f32),
        ],
    )
    def weights_of(level, *others):
        shape = (group, HEAD, D)
        low = 3 * group * level
        if in_pieces:
            taken = call(
                deal_kernel,
                [(shape, bf16, STAY)] * 3,
                [(after(near_unit, *others) if others else near_unit, SMEM)]
                + [(b, FAR) for b in blocks],
                "deal",
                2,
                scratch=[pltpu.SemaphoreType.DMA((3,))],
                low=low,
                order=order,
            )
        else:
            whole = jnp.concatenate(blocks, axis=0)
            place = jnp.sum(
                jnp.where(near_unit.reshape(-1)[None, :] == unit_ids[:, None], jnp.arange(whole.shape[0])[None, :], 0),
                axis=1,
            )
            whole = jnp.take(whole, place, axis=0)
            taken = [whole[low + i * group : low + (i + 1) * group] for i in range(3)]
        return [v.reshape(-1, D) for v in taken]

    both = jnp.concatenate([tokens_in, out_grad], axis=0)
    x, a0, x_far, upper, e0 = call(
        start_kernel,
        [
            ((half, D), f32),
            ((half, D), bf16),
            ((half, D), f32, STAY),
            ((half, D), f32, STAY),
            ((half, D), bf16),
        ],
        [tokens_in, out_grad, swap(both, "y"), shared_params],
        "start",
        0,
    )
    a1 = swap(a0, "core")

    def chip_sum(keep, send):
        return (keep.astype(f32) + swap(send, "core").astype(f32)).astype(bf16)

    def joined(level, kind, ours, theirs, x):
        return call(
            join(level, kind),
            [
                ((half, D), f32),
                ((half, D), bf16),
                ((rows, D), f32, STAY),
                ((half, D), f32, STAY),
            ],
            [ours, theirs, x, shared_params],
            "join",
            0,
        )

    saved = []
    for level in range(LAYERS):
        if level == 0:
            weights = [weights_of(0)]
        w_head, w1, w2 = weights[level]
        qkv, mixed, logs, a0_far, a1_far, keep, send = call(
            attention_kernel,
            [
                ((tokens, 3 * width), bf16, STAY),
                ((tokens, width), bf16, STAY),
                ((tokens, 128), f32, STAY),
                ((half, D), bf16, STAY),
                ((half, D), bf16, STAY),
                ((half, D), bf16),
                ((half, D), bf16),
            ],
            [a0, a1, bias_qv[level : level + 1], bias[level], w_head],
            "attention",
            0,
        )
        ours = chip_sum(keep, send)
        theirs = swap(ours, "y")
        if level == 0:
            weights.append(weights_of(1, ours))
            x = after(x, *weights[1])
        else:
            e0 = after(e0, ours)
            e1 = swap(e0, "core")
        x_mid, c0, branch, x_mid_far = joined(level, 0, ours, theirs, x)
        c1 = swap(c0, "core")
        u, slope, c0_far, c1_far, keep, send = call(
            hidden_kernel,
            [
                ((tokens, hidden), bf16, STAY),
                ((tokens, hidden), f32, STAY),
                ((half, D), bf16, STAY),
                ((half, D), bf16, STAY),
                ((half, D), bf16),
                ((half, D), bf16),
            ],
            [c0, c1, bias_1[level : level + 1], w1, w2],
            "hidden",
            0,
        )
        state = (x_far, a0_far, a1_far, qkv, mixed, logs, w_head, branch)
        state += (x_mid_far, c0_far, c1_far, u, slope, w1, w2)
        if level + 1 < LAYERS:
            ours = chip_sum(keep, send)
            theirs = swap(ours, "y")
            x, a0, branch_two, x_far = joined(level, 1, ours, theirs, x_mid)
            a1 = swap(a0, "core")
        else:
            final_parts = (keep, send)
            branch_two = None
        saved.append(state + (branch_two,))

    grads = None
    sizes = [stop - start for _, start, stop in back_order] * 2 if in_pieces else [owners_all * capacity]
    buffers = [((size, HEAD, D), bf16, FAR) for size in sizes]
    norm_sums, table_args = [], []
    for level in reversed(range(LAYERS)):
        x_far, a0_far, a1_far, qkv, mixed, logs, w_head, branch = saved[level][:8]
        x_mid_far, c0_far, c1_far, u, slope, w1, w2 = saved[level][8:15]
        dz, e0_far, e1_far, d_b1, keep, send = call(
            hidden_back_kernel,
            [
                ((tokens, hidden), bf16, STAY),
                ((half, D), bf16, STAY),
                ((half, D), bf16, STAY),
                ((1, hidden), f32),
                ((half, D), bf16),
                ((half, D), bf16),
            ],
            [e0, e1, w1, w2, slope],
            "hidden_back",
            0,
        )
        ours = chip_sum(keep, send)
        theirs = swap(ours, "y")
        first = 3 * group * level
        args = [(near_slot, SMEM), after(dz, ours), c0_far, c1_far, u, e0_far, e1_far]
        grads = call(
            weights_kernel,
            buffers,
            args + [(v, FAR) for v in grads or ()],
            "hidden_weights",
            2.5,
            scratch=[pltpu.VMEM((2 * group, HEAD, D), bf16), pltpu.SemaphoreType.DMA],
            alias=len(args) if grads else None,
            first=first + group,
            count=len(buffers),
            capacity=capacity,
        )
        d_mid, e0, sums_two = call(
            join_back((level, 4), (level, 2)),
            [((half, D), f32), ((half, D), bf16), ((4, D), f32)],
            [
                ours,
                theirs,
                after(x_mid_far, grads[0]),
                upper,
                branch,
                shared_params,
            ],
            "join_back",
            0,
        )
        e1 = swap(e0, "core")
        d_qkv, d_scores, e0_far, e1_far, keep, send = call(
            attention_back_kernel,
            [
                ((tokens, 3 * width), bf16, STAY),
                ((heads_here, tokens, tokens), bf16, STAY),
                ((half, D), bf16, STAY),
                ((half, D), bf16, STAY),
                ((half, D), bf16),
                ((half, D), bf16),
            ],
            [e0, e1, w_head, qkv, logs, bias[level]],
            "attention_back",
            0,
        )
        if level > 0:
            ours = chip_sum(keep, send)
            theirs = swap(ours, "y")
            d_qkv = after(d_qkv, ours)
        args = [(near_slot, SMEM), d_qkv, a0_far, a1_far, mixed, e0_far, e1_far]
        grads = call(
            weights_kernel,
            buffers,
            args + [(v, FAR) for v in grads],
            "attention_weights",
            2,
            scratch=[pltpu.VMEM((group, HEAD, D), bf16), pltpu.SemaphoreType.DMA],
            alias=len(args),
            first=first,
            count=len(buffers),
            capacity=capacity,
        )
        table_args.append([d_qkv, d_b1, d_scores, hot, hot_t])
        if level > 0:
            x_far = after(x_far, grads[0])
            upper, e0, sums_one = call(
                join_back((level, 0), (level - 1, 6)),
                [((half, D), f32), ((half, D), bf16), ((4, D), f32)],
                [ours, theirs, x_far, d_mid, saved[level - 1][-1], shared_params],
                "join_back",
                0,
                )
            e1 = swap(e0, "core")
        else:
            if not in_pieces:
                grads = [
                    grads[0][p * capacity + start : p * capacity + stop]
                    for x in range(2)
                    for s, start, stop in back_order
                    for p in [x * nz + s]
                ]
            scatter = ScatterSums(grads, back_order)
            scatter.step()
            last = scatter.part
            ours = chip_sum(keep, after(send, last))
            input_grad, sums_one = call(
                last_back_kernel,
                [((rows, D), f32), ((2, D), f32)],
                [ours, swap(ours[rows:], "y"), x_far, d_mid, shared_params],
                "last_back",
                0,
                )
        norm_sums.append((sums_one, sums_two))

    keep, send = after(final_parts, last)
    ours = chip_sum(keep, send)
    final_branch = (
        ours[:rows].astype(f32) + swap(ours[rows:], "y").astype(f32) + shared_params[LAYERS - 1, 7]
    )
    last_scale = shared_params[LAYERS - 1, 6]
    block_out = (x_mid[:rows] + last_scale * final_branch).astype(bf16)
    own_grad = out_grad.astype(f32)
    branch_sums = jnp.stack(
        [jnp.sum(own_grad * final_branch, axis=0), jnp.sum(last_scale * own_grad, axis=0)]
    )
    shared_grads, packed = [], []
    for sums, args in zip(norm_sums, table_args):
        sums_one, sums_two = sums
        shared_grads = [sums_one[0:2], sums_two[2:4], sums_two[0:2], branch_sums] + shared_grads
        branch_sums = sums_one[2:4]
        table = call(
            table_kernel, [((PACKED, 128), f32)], [after(args[0], last)] + args[1:], "table", 3
        )[0]
        packed.insert(0, table)

    shared_part = jnp.concatenate(shared_grads, axis=0)
    shared_part = sum_over(sum_over(shared_part, "core"), "y")
    small = jnp.concatenate([shared_part.reshape(-1, 128)] + packed, axis=0)
    scatter.step()
    scatter.step()
    small = small + scatter.along_x.send(small, "x", SWAP)
    while scatter.next < len(back_order) - 1:
        scatter.step()
    small = sum_over(small, "z")
    small = after(small, scatter.part)
    scatter.step()
    mine = scatter.result()
    lines = shared_part.size // 128
    shared_total = small[:lines].reshape(shared_params.shape)
    split_grads = []
    for level in range(LAYERS):
        part = small[lines + level * PACKED : lines + (level + 1) * PACKED]
        flat = part[: 3 * width // 128 + hidden // 128 + 1].reshape(-1)
        d_bias, d_b1 = flat[: 3 * width], flat[PACK_B1 * 128 : PACK_B1 * 128 + hidden]
        d_rel = jnp.concatenate(
            [
                part[PACK_TABLE : PACK_TABLE + SIDE, : 32 * heads_here]
                .reshape(SIDE, heads_here, 32)[:, :, :SIDE]
                .transpose(1, 0, 2)
                .reshape(heads_here, -1),
                part[PACK_ENDS : PACK_ENDS + heads_here, :3],
            ],
            axis=1,
        )
        split_grads.append(
            jnp.concatenate([d_bias[:width], d_bias[2 * width :], d_b1, d_rel.reshape(-1)])
        )
    split_total = jnp.stack(split_grads)[:, None, :]

    my_ids = (my_z * 2 + my_x) * capacity + jnp.arange(capacity, dtype=jnp.int32)
    used = jnp.any(my_ids[:, None] == slots[None, :], axis=1)[:, None, None]
    zeros = jnp.zeros_like(weight_store)
    mine = jnp.where(used, mine, zeros)
    matrix_first, matrix_second, matrix_weight = adam_step(
        weight_store, first_store, second_store, mine, rate_matrix, weight_decay
    )
    shared_moment, shared_square, shared_value = adam_step(
        shared_params, shared_first, shared_second, shared_total, rate_small, 0.0
    )
    split_moment, split_square, split_value = adam_step(
        split_params, split_first, split_second, split_total, rate_small, 0.0
    )
    return (
        block_out,
        input_grad,
        mine,
        jnp.where(used, matrix_first, zeros),
        jnp.where(used, matrix_second, zeros),
        jnp.where(used, matrix_weight, zeros),
        shared_total,
        shared_moment,
        shared_square,
        shared_value,
        split_total,
        split_moment,
        split_square,
        split_value,
    )


def solution(mesh):
    dp, tensor = mesh.shape["dp"], mesh.shape["tensor"]
    fine = Mesh(mesh.devices.reshape(dp // 2, 2, tensor // 2, 2), ("z", "x", "y", "core"))
    data, split = ("z", "x"), ("y", "core")
    tokens = P(data + split, None)
    store = P(data, split, None)
    shards = P(None, split, None)
    return jax.shard_map(
        per_device,
        mesh=fine,
        in_specs=(tokens, tokens, P(data, None), P(), store, store, store, P(), P(), P())
        + (shards,) * 3,
        out_specs=(tokens, tokens) + (store,) * 4 + (P(),) * 4 + (shards,) * 4,
        check_vma=False,
    )
```

```python
import functools

import jax
import jax.numpy as jnp
from jax import lax
from jax.experimental import pallas as pl
from jax.experimental.pallas import tpu as pltpu
from jax.sharding import Mesh
from jax.sharding import PartitionSpec as P

D = 768
HEADS = 12
HEAD = 64
FF = 3072
GRID = 14
LAYERS = 2
STEP = 10
RELS = 732
SIDE = 2 * GRID - 1

PITCH = 16
CODES = 256
CLASS_CODE = GRID * PITCH
SPREAD = 512

PACK_B1 = 5
PACK_TABLE = 11
PACK_ENDS = 43
PACKED = 48

norm_eps = 1e-06
beta_first = 0.5
beta_second = 0.5
adam_eps = 1e-08
rate_matrix = 0.05
rate_small = 0.3
weight_decay = 0.05
masked_score = -1e30

f32 = jnp.float32
bf16 = jnp.bfloat16
MIB = 1 << 20
SCALE = 1e9


def iota(shape, axis):
    return lax.broadcasted_iota(jnp.int32, shape, axis)


def matmul(a, b):
    return jnp.dot(a, b, preferred_element_type=f32)


def matmul_nt(a, b):
    return lax.dot_general(a, b, (((1,), (1,)), ((), ())), preferred_element_type=f32)


def matmul_tn(a, b):
    return lax.dot_general(a, b, (((0,), (0,)), ((), ())), preferred_element_type=f32)


def two_parts(v):
    high = v.astype(bf16)
    return high, (v - high.astype(f32)).astype(bf16)


VMEM, SMEM, STAY, FAR = "vmem", "smem", "stay", "far"


def call(kernel, outs, args, name, us, scratch=(), limit=16, alias=None, **options):
    args = [a if isinstance(a, tuple) else (a, VMEM) for a in args]
    spaces = {VMEM: pltpu.VMEM, SMEM: pltpu.SMEM, FAR: pltpu.HBM}
    colors = {STAY: pltpu.VMEM, FAR: pltpu.HBM, VMEM: jax.ShapeDtypeStruct}
    in_specs = [pl.BlockSpec(memory_space=spaces[place]) for _, place in args]
    args = [
        (pltpu.with_memory_space_constraint(a, pltpu.HBM) if place == FAR else a, place)
        for a, place in args
    ]
    outs = [out if len(out) == 3 else (*out, VMEM) for out in outs]
    shapes = [colors[place](shape, dtype) for shape, dtype, place in outs]
    return pl.pallas_call(
        functools.partial(kernel, **options),
        out_shape=shapes,
        in_specs=in_specs,
        out_specs=[
            pl.BlockSpec(memory_space=pltpu.HBM if place == FAR else pltpu.VMEM) for _, _, place in outs
        ],
        scratch_shapes=list(scratch),
        input_output_aliases={alias + i: i for i in range(len(outs))} if alias is not None else {},
        compiler_params=pltpu.CompilerParams(vmem_limit_bytes=limit * MIB),
        cost_estimate=pl.CostEstimate(flops=int(us * SCALE), bytes_accessed=1, transcendentals=0),
        name=name,
    )(*[a for a, _ in args])


def swap(v, axis):
    return lax.ppermute(v, axis, [(0, 1), (1, 0)])


class Line:
    def __init__(self, ahead=1):
        self.come, self.ahead = [], ahead

    def send(self, v, axis, perm):
        if len(self.come) >= self.ahead:
            v = after(v, self.come[-self.ahead])
        self.come.append(lax.ppermute(v, axis, perm))
        return self.come[-1]


SWAP = [(0, 1), (1, 0)]


def low_bit(s):
    return s & -s


def gather_stores(store, near):
    nz = lax.axis_size("z")
    along_z, along_x = Line(2), Line()
    blocks = [store]
    for s in range(1, nz):
        perm = [(i, i ^ low_bit(s)) for i in range(nz)]
        sent = blocks[s - low_bit(s)]
        blocks.append(along_z.send(after(sent, near) if s == 2 else sent, "z", perm))
    return blocks + [along_x.send(v, "x", SWAP) for v in blocks]


class ScatterSums:
    def __init__(self, grads):
        self.grads, self.count = grads, len(grads) // 2
        self.along_z, self.along_x = Line(), Line()
        self.come = [[] for _ in range(self.count)]
        self.parts = []

    def step(self):
        s = self.count - 1 - len(self.parts)
        got = self.along_x.send(self.grads[self.count + s], "x", SWAP)
        ours = self.grads[s]
        if self.parts:
            ours = after(ours, self.parts[-1])
        part = sum(v.astype(f32) for v in [ours, got] + self.come[s])
        if s:
            part = part.astype(bf16)
            perm = [(i, i ^ low_bit(s)) for i in range(self.count)]
            if s == 1:
                self.along_z.ahead = 2
            self.come[s - low_bit(s)].append(self.along_z.send(part, "z", perm))
        self.parts.append(part)


def after(v, *others):
    return lax.optimization_barrier((v,) + others)[0]


def sum_over(v, axis):
    size = lax.axis_size(axis)
    step = 1
    while step < size:
        v = v + lax.ppermute(v, axis, [(i, i ^ step) for i in range(size)])
        step *= 2
    return v


def deal_kernel(near_unit, *refs, low):
    *blocks, first, second, third, semaphores = refs
    group = first.shape[0]
    outs = (first, second, third)
    for owner, block in enumerate(blocks):
        for k in range(block.shape[0]):
            unit = near_unit[owner, k] - low
            for j, out in enumerate(outs):

                @pl.when((unit >= j * group) & (unit < (j + 1) * group))
                def _():
                    pltpu.make_async_copy(block.at[k], out.at[unit - j * group], semaphores.at[j]).start()

    for j, out in enumerate(outs):
        pltpu.make_async_copy(out, out, semaphores.at[j]).wait()


def lifting(rows):
    return jnp.where(
        SIDE - 1 - iota((rows, SPREAD), 1) // PITCH == iota((rows, SPREAD), 0), 1.0, 0.0
    ).astype(bf16)


def column_offset():
    return iota((32, SPREAD), 0) + (iota((32, SPREAD), 1) % PITCH) - (GRID - 1)


def prepare_kernel(
    table, ends, code_c, seg_c, code_r, seg_r, hot, hot_t, *rest
):
    *biases, spread, tile = rest
    heads = table.shape[0] // len(biases)
    tokens = code_c.shape[0]
    hot[...] = jnp.where(code_c[...] == iota((tokens, CODES), 1), 1.0, 0.0).astype(bf16)
    hot_t[...] = jnp.where(code_r[...] == iota((CODES, tokens), 0), 1.0, 0.0).astype(bf16)
    lift = lifting(32)
    offset = column_offset()
    spread[...] = jnp.zeros(spread.shape, f32)
    for h in range(table.shape[0]):
        high, low = two_parts(table[h])
        lifted = matmul_tn(high, lift) + matmul_tn(low, lift)
        for c in range(GRID):
            line = jnp.sum(jnp.where(offset == c, lifted, 0.0), axis=0, keepdims=True)
            spread[h, c : c + 1, :] = line
    row = iota((CODES, CODES), 0)
    col = iota((CODES, CODES), 1)
    for level, bias in enumerate(biases):

        def one(head, carry):
            h = level * heads + head
            lines = spread[h]
            for r in range(GRID):
                back = (GRID - 1 - r) * PITCH
                moved = pltpu.roll(lines, (SPREAD - back) % SPREAD, 1) if back else lines
                tile[r * PITCH : (r + 1) * PITCH, :] = moved[:, :CODES]
            tile[CLASS_CODE:, :] = jnp.zeros((CODES - CLASS_CODE, CODES), f32)
            full = jnp.where(row == CLASS_CODE, ends[h, 0], tile[...])
            full = jnp.where(col == CLASS_CODE, ends[h, 1], full)
            full = jnp.where((col == CLASS_CODE) & (row == CLASS_CODE), ends[h, 2], full)
            high, low = two_parts(full)
            left_high = matmul(hot[...], high).astype(bf16)
            left_low = matmul(hot[...], low).astype(bf16)
            values = matmul(left_high, hot_t[...]) + matmul(left_low, hot_t[...])
            bias[head] = jnp.where(seg_c[...] == seg_r[...], values, masked_score)
            return carry

        lax.fori_loop(0, heads, one, 0)


def normed(v):
    center = v - jnp.mean(v, axis=-1, keepdims=True)
    inverse = lax.rsqrt(jnp.mean(center * center, axis=-1, keepdims=True) + norm_eps)
    return center * inverse, inverse


def start_kernel(tokens, grads, near, shared, x, low, x_saved, upper, e):
    rows = tokens.shape[0]
    x[:rows, :] = tokens[...].astype(f32)
    x[rows:, :] = near[:rows, :].astype(f32)
    x_saved[...] = x[...]
    hat, _ = normed(x[...])
    low[...] = (hat * shared[0, 0:1, :] + shared[0, 1:2, :]).astype(bf16)
    upper[:rows, :] = grads[...].astype(f32)
    upper[rows:, :] = near[rows:, :].astype(f32)
    e[...] = (shared[LAYERS - 1, 6:7, :] * upper[...]).astype(bf16)


def attention_kernel(a0, a1, vector, bias, w, qkv, mixed, logs, a0_saved, a1_saved, keep, send):
    a0_saved[...] = a0[...]
    a1_saved[...] = a1[...]
    half = a0.shape[0]
    heads = bias.shape[0]
    width = heads * HEAD
    out = qkv
    for i, a in enumerate((a0, a1)):
        rows = pl.ds(i * half, half)
        proj = matmul_nt(a[...], w[: 3 * width, :]) + vector[:, : 3 * width]
        out[rows, :] = proj.astype(bf16)
    bias = bias
    parts = []
    for h in range(heads):
        q = out[:, h * HEAD : (h + 1) * HEAD] * jnp.asarray(HEAD**-0.5, bf16)
        k = out[:, width + h * HEAD : width + (h + 1) * HEAD]
        v = out[:, 2 * width + h * HEAD : 2 * width + (h + 1) * HEAD]
        s = matmul_nt(q, k) + bias[h]
        top = jnp.max(s, axis=-1, keepdims=True)
        e = jnp.exp(s - top)
        total = jnp.sum(e, axis=-1, keepdims=True)
        p = (e * (1.0 / total)).astype(bf16)
        parts.append(matmul(p, v))
        logs[:, h : h + 1] = top + jnp.log(total)
    mixed[...] = jnp.concatenate(parts, axis=1).astype(bf16)
    w_out = w[3 * width :, :]
    keep[...] = matmul(mixed[:half, :], w_out).astype(bf16)
    send[...] = matmul(mixed[half:, :], w_out).astype(bf16)


def attention_back_kernel(
    e0, e1, w_true, qkv, logs, bias, d_qkv, d_scores, e0_saved, e1_saved, keep, send
):
    e0_saved[...] = e0[...]
    e1_saved[...] = e1[...]
    half = e0.shape[0]
    heads = bias.shape[0]
    width = heads * HEAD
    scale = HEAD**-0.5
    w = w_true
    w_out = w[3 * width :, :]
    d_mixed = jnp.concatenate(
        [matmul_nt(e0[...], w_out), matmul_nt(e1[...], w_out)], axis=0
    ).astype(bf16)
    qkv, logs, bias = qkv, logs, bias
    dq, dk, dv = [], [], []
    for h in range(heads):
        q = qkv[:, h * HEAD : (h + 1) * HEAD] * jnp.asarray(scale, bf16)
        k = qkv[:, width + h * HEAD : width + (h + 1) * HEAD]
        v = qkv[:, 2 * width + h * HEAD : 2 * width + (h + 1) * HEAD]
        g = d_mixed[:, h * HEAD : (h + 1) * HEAD]
        p = jnp.exp(matmul_nt(q, k) + bias[h] - logs[:, h : h + 1])
        dp = matmul_nt(g, v)
        pdp = p * dp
        ds = (pdp - p * jnp.sum(pdp, axis=-1, keepdims=True)).astype(bf16)
        d_scores[h] = ds
        dq.append(matmul(ds, k) * scale)
        dk.append(matmul_tn(ds, q))
        dv.append(matmul_tn(p.astype(bf16), g))
    out = d_qkv
    out[...] = jnp.concatenate(dq + dk + dv, axis=1).astype(bf16)
    keep[...] = matmul(out[:half, :], w[: 3 * width, :]).astype(bf16)
    send[...] = matmul(out[half:, :], w[: 3 * width, :]).astype(bf16)


def table_kernel(d_qkv, d_b1, scores, hot, hot_t, packed):
    heads = scores.shape[0]
    width = heads * HEAD
    packed[...] = jnp.zeros(packed.shape, f32)
    line = jnp.sum(d_qkv[...].astype(f32), axis=0, keepdims=True)
    for start in range(0, 3 * width, 128):
        stop = min(start + 128, 3 * width)
        packed[start // 128 : start // 128 + 1, : stop - start] = line[:, start:stop]
    line = d_b1[...]
    for start in range(0, line.shape[1], 128):
        at = PACK_B1 + start // 128
        packed[at : at + 1, :] = line[:, start : start + 128]
    lift = lifting(32)
    offset = column_offset()
    row = iota((CODES, CODES), 0)
    col = iota((CODES, CODES), 1)
    for h in range(heads):
        high, low = two_parts(matmul(hot_t[...], scores[h]))
        tile = matmul(high, hot[...]) + matmul(low, hot[...])
        class_row = jnp.where(row == CLASS_CODE, tile, 0.0)
        class_col = jnp.where(col == CLASS_CODE, tile, 0.0)
        both = jnp.where(col == CLASS_CODE, class_row, 0.0)
        both_sum = jnp.sum(both, keepdims=True)
        row_sum = jnp.sum(class_row, keepdims=True) - both_sum
        col_sum = jnp.sum(class_col, keepdims=True) - both_sum
        lane = iota((1, 128), 1)
        packed[PACK_ENDS + h : PACK_ENDS + h + 1, :] = jnp.where(
            lane == 0, row_sum, jnp.where(lane == 1, col_sum, jnp.where(lane == 2, both_sum, 0.0))
        )
        inner = jnp.where((row < CLASS_CODE) & (col < CLASS_CODE), tile, 0.0)
        lines = jnp.zeros((PITCH, SPREAD), f32)
        for r in range(GRID):
            wide = jnp.concatenate(
                [inner[r * PITCH : (r + 1) * PITCH, :], jnp.zeros((PITCH, SPREAD - CODES), f32)],
                axis=1,
            )
            shift = (GRID - 1 - r) * PITCH
            lines = lines + (pltpu.roll(wide, shift, 1) if shift else wide)
        spread = jnp.zeros((32, SPREAD), f32)
        for c in range(GRID):
            spread = spread + jnp.where(offset == c, lines[c : c + 1, :], 0.0)
        high, low = two_parts(spread)
        packed[PACK_TABLE : PACK_TABLE + 32, 32 * h : 32 * h + 32] = matmul_nt(
            lift, high
        ) + matmul_nt(lift, low)


def gelu_parts(z):
    cdf = 0.5 * (1.0 + lax.erf(z * (0.5**0.5)))
    density = jnp.exp(-0.5 * z * z) * 0.3989422804014327
    return z * cdf, cdf + z * density


def hidden_kernel(c0, c1, b1, w1, w2, u, slope, c0_saved, c1_saved, keep, send):
    c0_saved[...] = c0[...]
    c1_saved[...] = c1[...]
    rows = c0.shape[0]
    cols = w1.shape[0] // 2
    for i, (c, out) in ((1, (c1, send)), (0, (c0, keep))):
        span = pl.ds(i * rows, rows)
        total = None
        for j in range(2):
            lanes = slice(j * cols, (j + 1) * cols)
            z = matmul_nt(c[...], w1[lanes, :]) + b1[:, lanes]
            value, grade = gelu_parts(z)
            value = value.astype(bf16)
            u[span, lanes] = value
            slope[span, lanes] = grade
            part = matmul(value, w2[lanes, :])
            total = part if total is None else total + part
        out[...] = total.astype(bf16)


def hidden_back_kernel(e0, e1, w1, w2, slope, dz, e0_saved, e1_saved, d_b1, keep, send):
    e0_saved[...] = e0[...]
    e1_saved[...] = e1[...]
    rows = e0.shape[0]
    cols = w1.shape[0] // 2
    w2, slope, w1 = w2, slope, w1
    sums = [None, None]
    for i, (e, out) in ((1, (e1, send)), (0, (e0, keep))):
        span = pl.ds(i * rows, rows)
        total = None
        for j in range(2):
            lanes = slice(j * cols, (j + 1) * cols)
            grad = matmul_nt(e[...], w2[lanes, :]) * slope[span, lanes]
            line = jnp.sum(grad, axis=0, keepdims=True)
            sums[j] = line if sums[j] is None else sums[j] + line
            grad = grad.astype(bf16)
            dz[span, lanes] = grad
            part = matmul(grad, w1[lanes, :])
            total = part if total is None else total + part
        out[...] = total.astype(bf16)
    d_b1[...] = jnp.concatenate(sums, axis=1)


def put_blocks(blocks, near_slot, first, outs, capacity, semaphore):
    for u in range(blocks.shape[0]):
        place = near_slot[first + u]
        if len(outs) == 1:
            pltpu.make_async_copy(blocks.at[u], outs[0].at[place], semaphore).start()
            continue
        for j, out in enumerate(outs):

            @pl.when((place >= j * capacity) & (place < (j + 1) * capacity))
            def _():
                pltpu.make_async_copy(blocks.at[u], out.at[place - j * capacity], semaphore).start()


def weights_kernel(near_slot, left0, right00, right01, left1, right10, right11, *refs, first, count, capacity):
    *refs, blocks, semaphore = refs
    outs = refs[-count:]
    half = right00.shape[0]
    at = 0
    for left, right0, right1 in ((left0, right00, right01), (left1, right10, right11)):
        grad = matmul_tn(left[:half, :], right0[...]) + matmul_tn(left[half:, :], right1[...])
        stop = at + grad.shape[0] // HEAD
        blocks[at:stop] = grad.astype(bf16).reshape(stop - at, HEAD, grad.shape[1])
        put_blocks(blocks.at[at:stop], near_slot, first + at, outs, capacity, semaphore)
        at = stop
    pltpu.make_async_copy(blocks, blocks, semaphore).wait()


def both_sums(ours, theirs):
    rows = ours.shape[0] // 2
    return jnp.concatenate(
        [
            ours[:rows, :].astype(f32) + theirs[rows:, :].astype(f32),
            ours[rows:, :].astype(f32) + theirs[:rows, :].astype(f32),
        ],
        axis=0,
    )


def join(level, kind):
    def kernel(ours, theirs, x, shared, x_next, low, branch, x_saved):
        rows = branch.shape[0]
        here = (level, 2, 3) if kind == 0 else (level, 6, 7)
        then = (level, 4, 5) if kind == 0 else (level + 1, 0, 1)
        y = both_sums(ours, theirs) + shared[here[0], here[2] : here[2] + 1, :]
        branch[...] = y[:rows, :]
        value = x[...] + shared[here[0], here[1] : here[1] + 1, :] * y
        x_next[...] = value
        x_saved[...] = x_next[...]
        hat, _ = normed(value)
        gain, shift = (shared[then[0], i : i + 1, :] for i in then[1:])
        low[...] = (hat * gain + shift).astype(bf16)

    return kernel


def through_norm(d_normed, x, upper, gain):
    hat, inverse = normed(x)
    d_hat = d_normed * gain
    mean_a = jnp.mean(d_hat, axis=-1, keepdims=True)
    mean_b = jnp.mean(d_hat * hat, axis=-1, keepdims=True)
    return upper + inverse * (d_hat - mean_a - hat * mean_b), d_normed * hat


def join_back(gain_at, scale_at):
    def kernel(ours, theirs, x, upper, branch, shared, dx, low, sums):
        rows = branch.shape[0]
        gain, scale = (shared[i, j : j + 1, :] for i, j in (gain_at, scale_at))
        d_normed = both_sums(ours, theirs)
        value, product = through_norm(d_normed, x[...], upper[...], gain)
        dx[...] = value
        e = scale * value
        low[...] = e.astype(bf16)
        sums[0:1, :] = jnp.sum(product[:rows, :], axis=0, keepdims=True)
        sums[1:2, :] = jnp.sum(d_normed[:rows, :], axis=0, keepdims=True)
        sums[2:3, :] = jnp.sum(value[:rows, :] * branch[...], axis=0, keepdims=True)
        sums[3:4, :] = jnp.sum(e[:rows, :], axis=0, keepdims=True)

    return kernel


def last_back_kernel(ours, theirs, x, upper, shared, dx, sums):
    rows = dx.shape[0]
    d_normed = ours[:rows, :].astype(f32) + theirs[...].astype(f32)
    value, product = through_norm(d_normed, x[:rows, :], upper[:rows, :], shared[0, 0:1, :])
    dx[...] = value
    sums[0:1, :] = jnp.sum(product, axis=0, keepdims=True)
    sums[1:2, :] = jnp.sum(d_normed, axis=0, keepdims=True)


def adam_step(weight, first, second, grad, rate, decay):
    first_new = beta_first * first + (1.0 - beta_first) * grad
    second_new = beta_second * second + (1.0 - beta_second) * grad * grad
    fix_first = 1.0 - beta_first**STEP
    fix_second = 1.0 - beta_second**STEP
    weight_new = weight - rate * (
        first_new / fix_first / (jnp.sqrt(second_new / fix_second) + adam_eps) + decay * weight
    )
    return (first_new, second_new, weight_new)


def image_layout(row_lengths, count):
    endings = jnp.cumsum(row_lengths)
    openings = endings - row_lengths
    places = jnp.arange(count, dtype=jnp.int32)
    inside = places[:, None] >= openings[None, :]
    segment = jnp.sum(inside.astype(jnp.int32), axis=1) - 1
    opening = jnp.max(jnp.where(inside, openings[None, :], 0), axis=1)
    return (segment, places - opening)


def unit_slots(owners, capacity):
    count = owners.shape[0]
    order = jnp.arange(count, dtype=jnp.int32)
    same_owner = owners[:, None] == owners[None, :]
    earlier = order[None, :] < order[:, None]
    rank = jnp.sum((same_owner & earlier).astype(jnp.int32), axis=1)
    return owners * capacity + rank


def per_device(
    tokens_in,
    out_grad,
    lengths,
    owners,
    weight_store,
    first_store,
    second_store,
    shared_params,
    shared_first,
    shared_second,
    split_params,
    split_first,
    split_second,
):
    nz = lax.axis_size("z")
    owners_all = nz * 2
    parts = 4
    heads_here = HEADS // parts
    width = heads_here * HEAD
    hidden = FF // parts
    rows = tokens_in.shape[0]
    tokens = rows * parts
    half = tokens // 2
    capacity = weight_store.shape[0]
    my_z, my_x = lax.axis_index("z"), lax.axis_index("x")
    my_y, my_c = lax.axis_index("y"), lax.axis_index("core")

    slots = unit_slots(owners, capacity)
    both = swap(jnp.concatenate([tokens_in, out_grad], axis=0), "y")
    blocks = gather_stores(weight_store.astype(bf16), both)

    group = hidden // HEAD
    near_x = (my_x + jnp.arange(2, dtype=jnp.int32)) % 2
    near_z = my_z ^ jnp.arange(nz, dtype=jnp.int32)
    owner_of = (near_z[None, :] * 2 + near_x[:, None]).reshape(-1)
    unit_ids = jnp.arange(slots.shape[0], dtype=jnp.int32)
    near_slots = owner_of[:, None] * capacity + jnp.arange(capacity, dtype=jnp.int32)[None, :]
    near_match = near_slots[:, :, None] == slots[None, None, :]
    near_unit = jnp.sum(jnp.where(near_match, unit_ids, 0), axis=2)
    near_unit = jnp.where(jnp.any(near_match, axis=2), near_unit, slots.shape[0])
    in_pieces = owners_all == 8
    near_ids = jnp.arange(owners_all * capacity, dtype=jnp.int32).reshape(owners_all, capacity, 1)
    near_slot = jnp.sum(jnp.where(near_match, near_ids, 0), axis=(0, 1))

    segment, position = image_layout(lengths[0], tokens)
    patch = position - 1
    code = jnp.where(position == 0, CLASS_CODE, (patch // GRID) * PITCH + patch % GRID)

    def local(v):
        v = jnp.roll(v.reshape(2, 2, rows), (-my_y, -my_c), (0, 1))
        return v.transpose(1, 0, 2).reshape(tokens)

    code, segment = local(code), local(segment)
    split = split_params[:, 0, :]
    bias_qv = jnp.concatenate(
        [split[:, :width], jnp.zeros((LAYERS, width), f32), split[:, width : 2 * width]], axis=1
    )
    bias_1 = split[:, 2 * width : 2 * width + hidden]
    table = split[:, 2 * width + hidden :].reshape(LAYERS * heads_here, RELS)
    inner = table[:, : SIDE * SIDE].reshape(-1, SIDE, SIDE)
    inner = jnp.pad(inner, ((0, 0), (0, 32 - SIDE), (0, 32 - SIDE)))
    hot, hot_t, *bias = call(
        prepare_kernel,
        [
            ((tokens, CODES), bf16, STAY),
            ((CODES, tokens), bf16, STAY),
        ]
        + [((heads_here, tokens, tokens), f32, STAY)] * LAYERS,
        [
            inner,
            (table[:, SIDE * SIDE :], SMEM),
            code[:, None],
            segment[:, None],
            code[None, :],
            segment[None, :],
        ],
        "prepare",
        6,
        scratch=[
            pltpu.VMEM((LAYERS * heads_here, PITCH, SPREAD), f32),
            pltpu.VMEM((CODES, CODES), f32),
        ],
    )
    def weights_of(level, *others):
        shape = (group, HEAD, D)
        low = 3 * group * level
        if in_pieces:
            taken = call(
                deal_kernel,
                [(shape, bf16, STAY)] * 3,
                [(after(near_unit, *others) if others else near_unit, SMEM)]
                + [(b, FAR) for b in blocks],
                "deal",
                2,
                scratch=[pltpu.SemaphoreType.DMA((3,))],
                low=low,
            )
        else:
            whole = jnp.concatenate(blocks, axis=0)
            place = jnp.sum(
                jnp.where(near_unit.reshape(-1)[None, :] == unit_ids[:, None], jnp.arange(whole.shape[0])[None, :], 0),
                axis=1,
            )
            whole = jnp.take(whole, place, axis=0)
            taken = [whole[low + i * group : low + (i + 1) * group] for i in range(3)]
        return [v.reshape(-1, D) for v in taken]

    x, a0, x_far, upper, e0 = call(
        start_kernel,
        [
            ((half, D), f32),
            ((half, D), bf16),
            ((half, D), f32, STAY),
            ((half, D), f32, STAY),
            ((half, D), bf16),
        ],
        [tokens_in, out_grad, both, shared_params],
        "start",
        0,
    )
    a1 = swap(a0, "core")

    def chip_sum(keep, send):
        return (keep.astype(f32) + swap(send, "core").astype(f32)).astype(bf16)

    def joined(level, kind, ours, theirs, x):
        return call(
            join(level, kind),
            [
                ((half, D), f32),
                ((half, D), bf16),
                ((rows, D), f32, STAY),
                ((half, D), f32, STAY),
            ],
            [ours, theirs, x, shared_params],
            "join",
            0,
        )

    saved = []
    for level in range(LAYERS):
        if level == 0:
            weights = [weights_of(0)]
        w_head, w1, w2 = weights[level]
        qkv, mixed, logs, a0_far, a1_far, keep, send = call(
            attention_kernel,
            [
                ((tokens, 3 * width), bf16, STAY),
                ((tokens, width), bf16, STAY),
                ((tokens, 128), f32, STAY),
                ((half, D), bf16, STAY),
                ((half, D), bf16, STAY),
                ((half, D), bf16),
                ((half, D), bf16),
            ],
            [a0, a1, bias_qv[level : level + 1], bias[level], w_head],
            "attention",
            0,
        )
        ours = chip_sum(keep, send)
        theirs = swap(ours, "y")
        if level == 0:
            weights.append(weights_of(1, ours))
            x = after(x, *weights[1])
        else:
            e0 = after(e0, ours)
            e1 = swap(e0, "core")
        x_mid, c0, branch, x_mid_far = joined(level, 0, ours, theirs, x)
        c1 = swap(c0, "core")
        u, slope, c0_far, c1_far, keep, send = call(
            hidden_kernel,
            [
                ((tokens, hidden), bf16, STAY),
                ((tokens, hidden), f32, STAY),
                ((half, D), bf16, STAY),
                ((half, D), bf16, STAY),
                ((half, D), bf16),
                ((half, D), bf16),
            ],
            [c0, c1, bias_1[level : level + 1], w1, w2],
            "hidden",
            0,
        )
        state = (x_far, a0_far, a1_far, qkv, mixed, logs, w_head, branch)
        state += (x_mid_far, c0_far, c1_far, u, slope, w1, w2)
        if level + 1 < LAYERS:
            ours = chip_sum(keep, send)
            theirs = swap(ours, "y")
            x, a0, branch_two, x_far = joined(level, 1, ours, theirs, x_mid)
            a1 = swap(a0, "core")
        else:
            final_parts = (keep, send)
            branch_two = None
        saved.append(state + (branch_two,))

    grads = None
    sizes = [capacity] * owners_all if in_pieces else [owners_all * capacity]
    buffers = [((size, HEAD, D), bf16, FAR) for size in sizes]
    norm_sums, tables = [], [None] * LAYERS
    for level in reversed(range(LAYERS)):
        x_far, a0_far, a1_far, qkv, mixed, logs, w_head, branch = saved[level][:8]
        x_mid_far, c0_far, c1_far, u, slope, w1, w2 = saved[level][8:15]
        dz, e0_far, e1_far, d_b1, keep, send = call(
            hidden_back_kernel,
            [
                ((tokens, hidden), bf16, STAY),
                ((half, D), bf16, STAY),
                ((half, D), bf16, STAY),
                ((1, hidden), f32),
                ((half, D), bf16),
                ((half, D), bf16),
            ],
            [e0, e1, w1, w2, slope],
            "hidden_back",
            0,
        )
        ours = chip_sum(keep, send)
        theirs = swap(ours, "y")
        first = 3 * group * level
        args = [(near_slot, SMEM), after(dz, ours), c0_far, c1_far, u, e0_far, e1_far]
        grads = call(
            weights_kernel,
            buffers,
            args + [(v, FAR) for v in grads or ()],
            "hidden_weights",
            2.5,
            scratch=[pltpu.VMEM((2 * group, HEAD, D), bf16), pltpu.SemaphoreType.DMA],
            alias=len(args) if grads else None,
            first=first + group,
            count=len(buffers),
            capacity=capacity,
        )
        waiting = [grads[0]]
        if level + 1 < LAYERS:
            args = [after(above[0], ours)] + list(above[1:])
            tables[level + 1] = call(table_kernel, [((PACKED, 128), f32)], args, "table", 3)[0]
            waiting += [tables[level + 1], theirs_early]
        d_mid, e0, sums_two = call(
            join_back((level, 4), (level, 2)),
            [((half, D), f32), ((half, D), bf16), ((4, D), f32)],
            [
                ours,
                theirs,
                after(x_mid_far, *waiting),
                upper,
                branch,
                shared_params,
            ],
            "join_back",
            0,
        )
        e1 = swap(e0, "core")
        d_qkv, d_scores, e0_far, e1_far, keep, send = call(
            attention_back_kernel,
            [
                ((tokens, 3 * width), bf16, STAY),
                ((heads_here, tokens, tokens), bf16, STAY),
                ((half, D), bf16, STAY),
                ((half, D), bf16, STAY),
                ((half, D), bf16),
                ((half, D), bf16),
            ],
            [e0, e1, w_head, qkv, logs, bias[level]],
            "attention_back",
            0,
        )
        if level > 0:
            ours = chip_sum(keep, send)
            theirs = swap(ours, "y")
            d_qkv = after(d_qkv, ours)
        args = [(near_slot, SMEM), d_qkv, a0_far, a1_far, mixed, e0_far, e1_far]
        grads = call(
            weights_kernel,
            buffers,
            args + [(v, FAR) for v in grads],
            "attention_weights",
            2,
            scratch=[pltpu.VMEM((group, HEAD, D), bf16), pltpu.SemaphoreType.DMA],
            alias=len(args),
            first=first,
            count=len(buffers),
            capacity=capacity,
        )
        table_args = (d_qkv, d_b1, d_scores, hot, hot_t)
        if level > 0:
            x_far = after(x_far, grads[0])
            upper, e0, sums_one = call(
                join_back((level, 0), (level - 1, 6)),
                [((half, D), f32), ((half, D), bf16), ((4, D), f32)],
                [ours, theirs, x_far, d_mid, saved[level - 1][-1], shared_params],
                "join_back",
                0,
                )
            e1 = swap(e0, "core")
            above = table_args
            early = chip_sum(after(final_parts[0], e0), after(final_parts[1], e0))
            theirs_early = swap(early[rows:], "y")
        else:
            if not in_pieces:
                grads = jnp.split(grads[0], owners_all, axis=0)
            args = [after(table_args[0], grads[0])] + list(table_args[1:])
            tables[0] = call(table_kernel, [((PACKED, 128), f32)], args, "table", 3)[0]
            ours = chip_sum(keep, after(send, grads[0]))
            scatter = ScatterSums(grads)
            scatter.step()
            input_grad, sums_one = call(
                last_back_kernel,
                [((rows, D), f32), ((2, D), f32)],
                [ours, swap(ours[rows:], "y"), x_far, d_mid, shared_params],
                "last_back",
                0,
                )
        norm_sums.append((sums_one, sums_two))

    final_branch = (
        early[:rows].astype(f32) + theirs_early.astype(f32) + shared_params[LAYERS - 1, 7]
    )
    last_scale = shared_params[LAYERS - 1, 6]
    block_out = (x_mid[:rows] + last_scale * final_branch).astype(bf16)
    own_grad = out_grad.astype(f32)
    branch_sums = jnp.stack(
        [jnp.sum(own_grad * final_branch, axis=0), jnp.sum(last_scale * own_grad, axis=0)]
    )
    shared_grads = []
    for sums_one, sums_two in norm_sums:
        shared_grads = [sums_one[0:2], sums_two[2:4], sums_two[0:2], branch_sums] + shared_grads
        branch_sums = sums_one[2:4]

    shared_part = jnp.concatenate(shared_grads, axis=0)
    shared_part = sum_over(sum_over(shared_part, "core"), "y")
    small = jnp.concatenate([shared_part.reshape(-1, 128)] + tables, axis=0)
    small = small + scatter.along_x.send(small, "x", SWAP)
    while len(scatter.parts) < scatter.count - 1:
        scatter.step()
    small = after(small, scatter.along_z.come[0])
    step = 1
    while step < nz:
        come = lax.ppermute(small, "z", [(i, i ^ step) for i in range(nz)])
        step *= 2
        small = small + (come if step < nz else after(come, scatter.parts[-1]))
    scatter.step()
    mine = scatter.parts[-1]
    lines = shared_part.size // 128
    shared_total = small[:lines].reshape(shared_params.shape)
    split_grads = []
    for level in range(LAYERS):
        part = small[lines + level * PACKED : lines + (level + 1) * PACKED]
        flat = part[: 3 * width // 128 + hidden // 128 + 1].reshape(-1)
        d_bias, d_b1 = flat[: 3 * width], flat[PACK_B1 * 128 : PACK_B1 * 128 + hidden]
        d_rel = jnp.concatenate(
            [
                part[PACK_TABLE : PACK_TABLE + SIDE, : 32 * heads_here]
                .reshape(SIDE, heads_here, 32)[:, :, :SIDE]
                .transpose(1, 0, 2)
                .reshape(heads_here, -1),
                part[PACK_ENDS : PACK_ENDS + heads_here, :3],
            ],
            axis=1,
        )
        split_grads.append(
            jnp.concatenate([d_bias[:width], d_bias[2 * width :], d_b1, d_rel.reshape(-1)])
        )
    split_total = jnp.stack(split_grads)[:, None, :]

    my_ids = (my_z * 2 + my_x) * capacity + jnp.arange(capacity, dtype=jnp.int32)
    used = jnp.any(my_ids[:, None] == slots[None, :], axis=1)[:, None, None]
    zeros = jnp.zeros_like(weight_store)
    mine = jnp.where(used, mine, zeros)
    matrix_first, matrix_second, matrix_weight = adam_step(
        weight_store, first_store, second_store, mine, rate_matrix, weight_decay
    )
    shared_moment, shared_square, shared_value = adam_step(
        shared_params, shared_first, shared_second, shared_total, rate_small, 0.0
    )
    split_moment, split_square, split_value = adam_step(
        split_params, split_first, split_second, split_total, rate_small, 0.0
    )
    return (
        block_out,
        input_grad,
        mine,
        jnp.where(used, matrix_first, zeros),
        jnp.where(used, matrix_second, zeros),
        jnp.where(used, matrix_weight, zeros),
        shared_total,
        shared_moment,
        shared_square,
        shared_value,
        split_total,
        split_moment,
        split_square,
        split_value,
    )


def solution(mesh):
    dp, tensor = mesh.shape["dp"], mesh.shape["tensor"]
    fine = Mesh(mesh.devices.reshape(dp // 2, 2, tensor // 2, 2), ("z", "x", "y", "core"))
    data, split = ("z", "x"), ("y", "core")
    tokens = P(data + split, None)
    store = P(data, split, None)
    shards = P(None, split, None)
    return jax.shard_map(
        per_device,
        mesh=fine,
        in_specs=(tokens, tokens, P(data, None), P(), store, store, store, P(), P(), P())
        + (shards,) * 3,
        out_specs=(tokens, tokens) + (store,) * 4 + (P(),) * 4 + (shards,) * 4,
        check_vma=False,
    )
```

```python
import functools

import jax
import jax.numpy as jnp
from jax import lax
from jax.experimental import pallas as pl
from jax.experimental.pallas import tpu as pltpu
from jax.sharding import Mesh
from jax.sharding import PartitionSpec as P

D = 768
HEADS = 12
HEAD = 64
FF = 3072
GRID = 14
LAYERS = 2
STEP = 10
RELS = 732
SIDE = 2 * GRID - 1

PITCH = 16
CODES = 256
CLASS_CODE = GRID * PITCH
SPREAD = 512

PACK_B1 = 5
PACK_TABLE = 11
PACK_ENDS = 43
PACKED = 48

norm_eps = 1e-06
beta_first = 0.5
beta_second = 0.5
adam_eps = 1e-08
rate_matrix = 0.05
rate_small = 0.3
weight_decay = 0.05
masked_score = -1e30

f32 = jnp.float32
bf16 = jnp.bfloat16
MIB = 1 << 20
SCALE = 1e9


def iota(shape, axis):
    return lax.broadcasted_iota(jnp.int32, shape, axis)


def matmul(a, b):
    return jnp.dot(a, b, preferred_element_type=f32)


def matmul_nt(a, b):
    return lax.dot_general(a, b, (((1,), (1,)), ((), ())), preferred_element_type=f32)


def matmul_tn(a, b):
    return lax.dot_general(a, b, (((0,), (0,)), ((), ())), preferred_element_type=f32)


def two_parts(v):
    high = v.astype(bf16)
    return high, (v - high.astype(f32)).astype(bf16)


VMEM, SMEM, STAY, FAR = "vmem", "smem", "stay", "far"


def call(kernel, outs, args, name, us, scratch=(), limit=16, alias=None, **options):
    args = [a if isinstance(a, tuple) else (a, VMEM) for a in args]
    spaces = {VMEM: pltpu.VMEM, SMEM: pltpu.SMEM, FAR: pltpu.HBM}
    colors = {STAY: pltpu.VMEM, FAR: pltpu.HBM, VMEM: jax.ShapeDtypeStruct}
    in_specs = [pl.BlockSpec(memory_space=spaces[place]) for _, place in args]
    args = [
        (pltpu.with_memory_space_constraint(a, pltpu.HBM) if place == FAR else a, place)
        for a, place in args
    ]
    outs = [out if len(out) == 3 else (*out, VMEM) for out in outs]
    shapes = [colors[place](shape, dtype) for shape, dtype, place in outs]
    return pl.pallas_call(
        functools.partial(kernel, **options),
        out_shape=shapes,
        in_specs=in_specs,
        out_specs=[
            pl.BlockSpec(memory_space=pltpu.HBM if place == FAR else pltpu.VMEM) for _, _, place in outs
        ],
        scratch_shapes=list(scratch),
        input_output_aliases={alias + i: i for i in range(len(outs))} if alias is not None else {},
        compiler_params=pltpu.CompilerParams(vmem_limit_bytes=limit * MIB),
        cost_estimate=pl.CostEstimate(flops=int(us * SCALE), bytes_accessed=1, transcendentals=0),
        name=name,
    )(*[a for a, _ in args])


def swap(v, axis):
    return lax.ppermute(v, axis, [(0, 1), (1, 0)])


class Line:
    def __init__(self, ahead=1):
        self.come, self.ahead = [], ahead

    def send(self, v, axis, perm):
        if len(self.come) >= self.ahead:
            v = after(v, self.come[-self.ahead])
        self.come.append(lax.ppermute(v, axis, perm))
        return self.come[-1]


SWAP = [(0, 1), (1, 0)]


def low_bit(s):
    return s & -s


def gather_stores(store, near):
    nz = lax.axis_size("z")
    along_z, along_x = Line(2), Line()
    blocks = [store]
    for s in range(1, nz):
        perm = [(i, i ^ low_bit(s)) for i in range(nz)]
        sent = blocks[s - low_bit(s)]
        blocks.append(along_z.send(after(sent, near) if s == 2 else sent, "z", perm))
    return blocks + [along_x.send(v, "x", SWAP) for v in blocks]


class ScatterSums:
    def __init__(self, ours, theirs):
        self.ours, self.theirs, self.count = ours, theirs, len(ours)
        self.along_z, self.along_x = Line(), Line()
        self.come = [[] for _ in ours]
        self.parts, self.all_parts = [], []

    def step(self):
        s = self.count - 1 - len(self.parts)
        sent = []
        last = self.parts[-1:]
        for ours, theirs in zip(self.ours[s], self.theirs[s]):
            got = self.along_x.send(theirs, "x", SWAP)
            if last:
                ours = after(ours, *last)
            come = self.come[s] if s else self.come[s][:-1]
            part = sum(v.astype(f32) for v in [ours, got] + come)
            if s:
                part = part.astype(bf16)
                perm = [(i, i ^ low_bit(s)) for i in range(self.count)]
                if s == 1:
                    self.along_z.ahead = 2
                sent.append(self.along_z.send(part, "z", perm))
            last = [part]
            self.all_parts.append(part)
        if s:
            self.come[s - low_bit(s)].append(jnp.concatenate(sent, axis=0) if len(sent) > 1 else sent[0])
        self.parts.append(part)


def after(v, *others):
    return lax.optimization_barrier((v,) + others)[0]


def sum_over(v, axis):
    size = lax.axis_size(axis)
    step = 1
    while step < size:
        v = v + lax.ppermute(v, axis, [(i, i ^ step) for i in range(size)])
        step *= 2
    return v


def deal_kernel(near_unit, *refs, low):
    *blocks, first, second, third, semaphores = refs
    group = first.shape[0]
    outs = (first, second, third)
    for owner, block in enumerate(blocks):
        for k in range(block.shape[0]):
            unit = near_unit[owner, k] - low
            for j, out in enumerate(outs):

                @pl.when((unit >= j * group) & (unit < (j + 1) * group))
                def _():
                    pltpu.make_async_copy(block.at[k], out.at[unit - j * group], semaphores.at[j]).start()

    for j, out in enumerate(outs):
        pltpu.make_async_copy(out, out, semaphores.at[j]).wait()


def lifting(rows):
    return jnp.where(
        SIDE - 1 - iota((rows, SPREAD), 1) // PITCH == iota((rows, SPREAD), 0), 1.0, 0.0
    ).astype(bf16)


def column_offset():
    return iota((32, SPREAD), 0) + (iota((32, SPREAD), 1) % PITCH) - (GRID - 1)


def prepare_kernel(
    table, ends, code_c, seg_c, code_r, seg_r, hot, hot_t, *rest
):
    *biases, spread, tile = rest
    heads = table.shape[0] // len(biases)
    tokens = code_c.shape[0]
    hot[...] = jnp.where(code_c[...] == iota((tokens, CODES), 1), 1.0, 0.0).astype(bf16)
    hot_t[...] = jnp.where(code_r[...] == iota((CODES, tokens), 0), 1.0, 0.0).astype(bf16)
    lift = lifting(32)
    offset = column_offset()
    spread[...] = jnp.zeros(spread.shape, f32)
    for h in range(table.shape[0]):
        high, low = two_parts(table[h])
        lifted = matmul_tn(high, lift) + matmul_tn(low, lift)
        for c in range(GRID):
            line = jnp.sum(jnp.where(offset == c, lifted, 0.0), axis=0, keepdims=True)
            spread[h, c : c + 1, :] = line
    row = iota((CODES, CODES), 0)
    col = iota((CODES, CODES), 1)
    for level, bias in enumerate(biases):

        def one(head, carry):
            h = level * heads + head
            lines = spread[h]
            for r in range(GRID):
                back = (GRID - 1 - r) * PITCH
                moved = pltpu.roll(lines, (SPREAD - back) % SPREAD, 1) if back else lines
                tile[r * PITCH : (r + 1) * PITCH, :] = moved[:, :CODES]
            tile[CLASS_CODE:, :] = jnp.zeros((CODES - CLASS_CODE, CODES), f32)
            full = jnp.where(row == CLASS_CODE, ends[h, 0], tile[...])
            full = jnp.where(col == CLASS_CODE, ends[h, 1], full)
            full = jnp.where((col == CLASS_CODE) & (row == CLASS_CODE), ends[h, 2], full)
            high, low = two_parts(full)
            left_high = matmul(hot[...], high).astype(bf16)
            left_low = matmul(hot[...], low).astype(bf16)
            values = matmul(left_high, hot_t[...]) + matmul(left_low, hot_t[...])
            bias[head] = jnp.where(seg_c[...] == seg_r[...], values, masked_score)
            return carry

        lax.fori_loop(0, heads, one, 0)


def normed(v):
    center = v - jnp.mean(v, axis=-1, keepdims=True)
    inverse = lax.rsqrt(jnp.mean(center * center, axis=-1, keepdims=True) + norm_eps)
    return center * inverse, inverse


def start_kernel(tokens, grads, near, shared, x, low, x_saved, upper, e):
    rows = tokens.shape[0]
    x[:rows, :] = tokens[...].astype(f32)
    x[rows:, :] = near[:rows, :].astype(f32)
    x_saved[...] = x[...]
    hat, _ = normed(x[...])
    low[...] = (hat * shared[0, 0:1, :] + shared[0, 1:2, :]).astype(bf16)
    upper[:rows, :] = grads[...].astype(f32)
    upper[rows:, :] = near[rows:, :].astype(f32)
    e[...] = (shared[LAYERS - 1, 6:7, :] * upper[...]).astype(bf16)


def attention_kernel(a0, a1, vector, bias, w, qkv, mixed, logs, a0_saved, a1_saved, keep, send):
    a0_saved[...] = a0[...]
    a1_saved[...] = a1[...]
    half = a0.shape[0]
    heads = bias.shape[0]
    width = heads * HEAD
    out = qkv
    for i, a in enumerate((a0, a1)):
        rows = pl.ds(i * half, half)
        proj = matmul_nt(a[...], w[: 3 * width, :]) + vector[:, : 3 * width]
        out[rows, :] = proj.astype(bf16)
    bias = bias
    parts = []
    for h in range(heads):
        q = out[:, h * HEAD : (h + 1) * HEAD] * jnp.asarray(HEAD**-0.5, bf16)
        k = out[:, width + h * HEAD : width + (h + 1) * HEAD]
        v = out[:, 2 * width + h * HEAD : 2 * width + (h + 1) * HEAD]
        s = matmul_nt(q, k) + bias[h]
        top = jnp.max(s, axis=-1, keepdims=True)
        e = jnp.exp(s - top)
        total = jnp.sum(e, axis=-1, keepdims=True)
        p = (e * (1.0 / total)).astype(bf16)
        parts.append(matmul(p, v))
        logs[:, h : h + 1] = top + jnp.log(total)
    mixed[...] = jnp.concatenate(parts, axis=1).astype(bf16)
    w_out = w[3 * width :, :]
    keep[...] = matmul(mixed[:half, :], w_out).astype(bf16)
    send[...] = matmul(mixed[half:, :], w_out).astype(bf16)


def attention_back_kernel(
    e0, e1, w_true, qkv, logs, bias, d_qkv, d_scores, e0_saved, e1_saved, keep, send
):
    e0_saved[...] = e0[...]
    e1_saved[...] = e1[...]
    half = e0.shape[0]
    heads = bias.shape[0]
    width = heads * HEAD
    scale = HEAD**-0.5
    w = w_true
    w_out = w[3 * width :, :]
    d_mixed = jnp.concatenate(
        [matmul_nt(e0[...], w_out), matmul_nt(e1[...], w_out)], axis=0
    ).astype(bf16)
    qkv, logs, bias = qkv, logs, bias
    dq, dk, dv = [], [], []
    for h in range(heads):
        q = qkv[:, h * HEAD : (h + 1) * HEAD] * jnp.asarray(scale, bf16)
        k = qkv[:, width + h * HEAD : width + (h + 1) * HEAD]
        v = qkv[:, 2 * width + h * HEAD : 2 * width + (h + 1) * HEAD]
        g = d_mixed[:, h * HEAD : (h + 1) * HEAD]
        p = jnp.exp(matmul_nt(q, k) + bias[h] - logs[:, h : h + 1])
        dp = matmul_nt(g, v)
        pdp = p * dp
        ds = (pdp - p * jnp.sum(pdp, axis=-1, keepdims=True)).astype(bf16)
        d_scores[h] = ds
        dq.append(matmul(ds, k) * scale)
        dk.append(matmul_tn(ds, q))
        dv.append(matmul_tn(p.astype(bf16), g))
    out = d_qkv
    out[...] = jnp.concatenate(dq + dk + dv, axis=1).astype(bf16)
    keep[...] = matmul(out[:half, :], w[: 3 * width, :]).astype(bf16)
    send[...] = matmul(out[half:, :], w[: 3 * width, :]).astype(bf16)


def table_kernel(d_qkv, d_b1, scores, hot, hot_t, packed):
    heads = scores.shape[0]
    width = heads * HEAD
    packed[...] = jnp.zeros(packed.shape, f32)
    line = jnp.sum(d_qkv[...].astype(f32), axis=0, keepdims=True)
    for start in range(0, 3 * width, 128):
        stop = min(start + 128, 3 * width)
        packed[start // 128 : start // 128 + 1, : stop - start] = line[:, start:stop]
    line = d_b1[...]
    for start in range(0, line.shape[1], 128):
        at = PACK_B1 + start // 128
        packed[at : at + 1, :] = line[:, start : start + 128]
    lift = lifting(32)
    offset = column_offset()
    row = iota((CODES, CODES), 0)
    col = iota((CODES, CODES), 1)
    for h in range(heads):
        high, low = two_parts(matmul(hot_t[...], scores[h]))
        tile = matmul(high, hot[...]) + matmul(low, hot[...])
        class_row = jnp.where(row == CLASS_CODE, tile, 0.0)
        class_col = jnp.where(col == CLASS_CODE, tile, 0.0)
        both = jnp.where(col == CLASS_CODE, class_row, 0.0)
        both_sum = jnp.sum(both, keepdims=True)
        row_sum = jnp.sum(class_row, keepdims=True) - both_sum
        col_sum = jnp.sum(class_col, keepdims=True) - both_sum
        lane = iota((1, 128), 1)
        packed[PACK_ENDS + h : PACK_ENDS + h + 1, :] = jnp.where(
            lane == 0, row_sum, jnp.where(lane == 1, col_sum, jnp.where(lane == 2, both_sum, 0.0))
        )
        inner = jnp.where((row < CLASS_CODE) & (col < CLASS_CODE), tile, 0.0)
        lines = jnp.zeros((PITCH, SPREAD), f32)
        for r in range(GRID):
            wide = jnp.concatenate(
                [inner[r * PITCH : (r + 1) * PITCH, :], jnp.zeros((PITCH, SPREAD - CODES), f32)],
                axis=1,
            )
            shift = (GRID - 1 - r) * PITCH
            lines = lines + (pltpu.roll(wide, shift, 1) if shift else wide)
        spread = jnp.zeros((32, SPREAD), f32)
        for c in range(GRID):
            spread = spread + jnp.where(offset == c, lines[c : c + 1, :], 0.0)
        high, low = two_parts(spread)
        packed[PACK_TABLE : PACK_TABLE + 32, 32 * h : 32 * h + 32] = matmul_nt(
            lift, high
        ) + matmul_nt(lift, low)


def gelu_parts(z):
    cdf = 0.5 * (1.0 + lax.erf(z * (0.5**0.5)))
    density = jnp.exp(-0.5 * z * z) * 0.3989422804014327
    return z * cdf, cdf + z * density


def hidden_kernel(c0, c1, b1, w1, w2, u, slope, c0_saved, c1_saved, keep, send):
    c0_saved[...] = c0[...]
    c1_saved[...] = c1[...]
    rows = c0.shape[0]
    cols = w1.shape[0] // 2
    for i, (c, out) in ((1, (c1, send)), (0, (c0, keep))):
        span = pl.ds(i * rows, rows)
        total = None
        for j in range(2):
            lanes = slice(j * cols, (j + 1) * cols)
            z = matmul_nt(c[...], w1[lanes, :]) + b1[:, lanes]
            value, grade = gelu_parts(z)
            value = value.astype(bf16)
            u[span, lanes] = value
            slope[span, lanes] = grade
            part = matmul(value, w2[lanes, :])
            total = part if total is None else total + part
        out[...] = total.astype(bf16)


def hidden_back_kernel(e0, e1, w1, w2, slope, dz, e0_saved, e1_saved, d_b1, keep, send):
    e0_saved[...] = e0[...]
    e1_saved[...] = e1[...]
    rows = e0.shape[0]
    cols = w1.shape[0] // 2
    w2, slope, w1 = w2, slope, w1
    sums = [None, None]
    for i, (e, out) in ((1, (e1, send)), (0, (e0, keep))):
        span = pl.ds(i * rows, rows)
        total = None
        for j in range(2):
            lanes = slice(j * cols, (j + 1) * cols)
            grad = matmul_nt(e[...], w2[lanes, :]) * slope[span, lanes]
            line = jnp.sum(grad, axis=0, keepdims=True)
            sums[j] = line if sums[j] is None else sums[j] + line
            grad = grad.astype(bf16)
            dz[span, lanes] = grad
            part = matmul(grad, w1[lanes, :])
            total = part if total is None else total + part
        out[...] = total.astype(bf16)
    d_b1[...] = jnp.concatenate(sums, axis=1)


def put_blocks(blocks, near_slot, first, outs, capacity, semaphore):
    for u in range(blocks.shape[0]):
        place = near_slot[first + u]
        if len(outs) == 1:
            pltpu.make_async_copy(blocks.at[u], outs[0].at[place], semaphore).start()
            continue
        for j, out in enumerate(outs):

            @pl.when((place >= j * capacity) & (place < (j + 1) * capacity))
            def _():
                pltpu.make_async_copy(blocks.at[u], out.at[place - j * capacity], semaphore).start()


def weights_kernel(near_slot, left0, right00, right01, left1, right10, right11, *refs, first, count, capacity):
    *refs, blocks, semaphore = refs
    outs = refs[-count:]
    half = right00.shape[0]
    at = 0
    for left, right0, right1 in ((left0, right00, right01), (left1, right10, right11)):
        grad = matmul_tn(left[:half, :], right0[...]) + matmul_tn(left[half:, :], right1[...])
        stop = at + grad.shape[0] // HEAD
        blocks[at:stop] = grad.astype(bf16).reshape(stop - at, HEAD, grad.shape[1])
        put_blocks(blocks.at[at:stop], near_slot, first + at, outs, capacity, semaphore)
        at = stop
    pltpu.make_async_copy(blocks, blocks, semaphore).wait()


def both_sums(ours, theirs):
    rows = ours.shape[0] // 2
    return jnp.concatenate(
        [
            ours[:rows, :].astype(f32) + theirs[rows:, :].astype(f32),
            ours[rows:, :].astype(f32) + theirs[:rows, :].astype(f32),
        ],
        axis=0,
    )


def join(level, kind):
    def kernel(ours, theirs, x, shared, x_next, low, branch, x_saved):
        rows = branch.shape[0]
        here = (level, 2, 3) if kind == 0 else (level, 6, 7)
        then = (level, 4, 5) if kind == 0 else (level + 1, 0, 1)
        y = both_sums(ours, theirs) + shared[here[0], here[2] : here[2] + 1, :]
        branch[...] = y[:rows, :]
        value = x[...] + shared[here[0], here[1] : here[1] + 1, :] * y
        x_next[...] = value
        x_saved[...] = x_next[...]
        hat, _ = normed(value)
        gain, shift = (shared[then[0], i : i + 1, :] for i in then[1:])
        low[...] = (hat * gain + shift).astype(bf16)

    return kernel


def through_norm(d_normed, x, upper, gain):
    hat, inverse = normed(x)
    d_hat = d_normed * gain
    mean_a = jnp.mean(d_hat, axis=-1, keepdims=True)
    mean_b = jnp.mean(d_hat * hat, axis=-1, keepdims=True)
    return upper + inverse * (d_hat - mean_a - hat * mean_b), d_normed * hat


def join_back(gain_at, scale_at):
    def kernel(ours, theirs, x, upper, branch, shared, dx, low, sums):
        rows = branch.shape[0]
        gain, scale = (shared[i, j : j + 1, :] for i, j in (gain_at, scale_at))
        d_normed = both_sums(ours, theirs)
        value, product = through_norm(d_normed, x[...], upper[...], gain)
        dx[...] = value
        e = scale * value
        low[...] = e.astype(bf16)
        sums[0:1, :] = jnp.sum(product[:rows, :], axis=0, keepdims=True)
        sums[1:2, :] = jnp.sum(d_normed[:rows, :], axis=0, keepdims=True)
        sums[2:3, :] = jnp.sum(value[:rows, :] * branch[...], axis=0, keepdims=True)
        sums[3:4, :] = jnp.sum(e[:rows, :], axis=0, keepdims=True)

    return kernel


def last_back_kernel(ours, theirs, x, upper, shared, dx, sums):
    rows = dx.shape[0]
    d_normed = ours[:rows, :].astype(f32) + theirs[...].astype(f32)
    value, product = through_norm(d_normed, x[:rows, :], upper[:rows, :], shared[0, 0:1, :])
    dx[...] = value
    sums[0:1, :] = jnp.sum(product, axis=0, keepdims=True)
    sums[1:2, :] = jnp.sum(d_normed, axis=0, keepdims=True)


def adam_step(weight, first, second, grad, rate, decay):
    first_new = beta_first * first + (1.0 - beta_first) * grad
    second_new = beta_second * second + (1.0 - beta_second) * grad * grad
    fix_first = 1.0 - beta_first**STEP
    fix_second = 1.0 - beta_second**STEP
    weight_new = weight - rate * (
        first_new / fix_first / (jnp.sqrt(second_new / fix_second) + adam_eps) + decay * weight
    )
    return (first_new, second_new, weight_new)


def fetch_kernel(*refs):
    count = len(refs) // 2
    copies = [
        pltpu.make_async_copy(refs[i], refs[count + i], refs[-1].at[i]) for i in range(count)
    ]
    for copy in copies:
        copy.start()
    for copy in copies:
        copy.wait()


def update_kernel(used, base, come, weight, first, second, *refs):
    outs, scratch, semaphores = refs[:4], refs[4:8], refs[8]
    for k in range(base.shape[0]):
        grad = base[k] + come[k].astype(f32)
        values = (grad,) + adam_step(weight[k], first[k], second[k], grad, rate_matrix, weight_decay)
        for i, value in enumerate(values):
            scratch[i][k] = jnp.where(used[k] > 0, value, 0.0)
            pltpu.make_async_copy(scratch[i].at[k], outs[i].at[k], semaphores.at[i]).start()
    for i in range(4):
        pltpu.make_async_copy(scratch[i], outs[i], semaphores.at[i]).wait()


def image_layout(row_lengths, count):
    endings = jnp.cumsum(row_lengths)
    openings = endings - row_lengths
    places = jnp.arange(count, dtype=jnp.int32)
    inside = places[:, None] >= openings[None, :]
    segment = jnp.sum(inside.astype(jnp.int32), axis=1) - 1
    opening = jnp.max(jnp.where(inside, openings[None, :], 0), axis=1)
    return (segment, places - opening)


def unit_slots(owners, capacity):
    count = owners.shape[0]
    order = jnp.arange(count, dtype=jnp.int32)
    same_owner = owners[:, None] == owners[None, :]
    earlier = order[None, :] < order[:, None]
    rank = jnp.sum((same_owner & earlier).astype(jnp.int32), axis=1)
    return owners * capacity + rank


def per_device(
    tokens_in,
    out_grad,
    lengths,
    owners,
    weight_store,
    first_store,
    second_store,
    shared_params,
    shared_first,
    shared_second,
    split_params,
    split_first,
    split_second,
):
    nz = lax.axis_size("z")
    owners_all = nz * 2
    parts = 4
    heads_here = HEADS // parts
    width = heads_here * HEAD
    hidden = FF // parts
    rows = tokens_in.shape[0]
    tokens = rows * parts
    half = tokens // 2
    capacity = weight_store.shape[0]
    my_z, my_x = lax.axis_index("z"), lax.axis_index("x")
    my_y, my_c = lax.axis_index("y"), lax.axis_index("core")

    slots = unit_slots(owners, capacity)
    both = swap(jnp.concatenate([tokens_in, out_grad], axis=0), "y")
    blocks = gather_stores(weight_store.astype(bf16), both)

    group = hidden // HEAD
    near_x = (my_x + jnp.arange(2, dtype=jnp.int32)) % 2
    near_z = my_z ^ jnp.arange(nz, dtype=jnp.int32)
    owner_of = (near_z[None, :] * 2 + near_x[:, None]).reshape(-1)
    unit_ids = jnp.arange(slots.shape[0], dtype=jnp.int32)
    near_slots = owner_of[:, None] * capacity + jnp.arange(capacity, dtype=jnp.int32)[None, :]
    near_match = near_slots[:, :, None] == slots[None, None, :]
    near_unit = jnp.sum(jnp.where(near_match, unit_ids, 0), axis=2)
    near_unit = jnp.where(jnp.any(near_match, axis=2), near_unit, slots.shape[0])
    in_pieces = owners_all == 8
    sizes = [owners_all * capacity]
    near_ids = [[p * capacity + k for k in range(capacity)] for p in range(owners_all)]
    if in_pieces:
        cut = capacity // 2
        sizes, near_ids = [], []
        for p in range(owners_all):
            ids = []
            for size in [cut, capacity - cut] if p % nz == nz - 1 else [capacity]:
                ids += [len(sizes) * capacity + k for k in range(size)]
                sizes.append(size)
            near_ids.append(ids)
    near_ids = jnp.asarray(near_ids, jnp.int32)[:, :, None]
    near_slot = jnp.sum(jnp.where(near_match, near_ids, 0), axis=(0, 1))

    segment, position = image_layout(lengths[0], tokens)
    patch = position - 1
    code = jnp.where(position == 0, CLASS_CODE, (patch // GRID) * PITCH + patch % GRID)

    def local(v):
        v = jnp.roll(v.reshape(2, 2, rows), (-my_y, -my_c), (0, 1))
        return v.transpose(1, 0, 2).reshape(tokens)

    code, segment = local(code), local(segment)
    split = split_params[:, 0, :]
    bias_qv = jnp.concatenate(
        [split[:, :width], jnp.zeros((LAYERS, width), f32), split[:, width : 2 * width]], axis=1
    )
    bias_1 = split[:, 2 * width : 2 * width + hidden]
    table = split[:, 2 * width + hidden :].reshape(LAYERS * heads_here, RELS)
    inner = table[:, : SIDE * SIDE].reshape(-1, SIDE, SIDE)
    inner = jnp.pad(inner, ((0, 0), (0, 32 - SIDE), (0, 32 - SIDE)))
    hot, hot_t, *bias = call(
        prepare_kernel,
        [
            ((tokens, CODES), bf16, STAY),
            ((CODES, tokens), bf16, STAY),
        ]
        + [((heads_here, tokens, tokens), f32, STAY)] * LAYERS,
        [
            inner,
            (table[:, SIDE * SIDE :], SMEM),
            code[:, None],
            segment[:, None],
            code[None, :],
            segment[None, :],
        ],
        "prepare",
        6,
        scratch=[
            pltpu.VMEM((LAYERS * heads_here, PITCH, SPREAD), f32),
            pltpu.VMEM((CODES, CODES), f32),
        ],
    )
    def weights_of(level, *others):
        shape = (group, HEAD, D)
        low = 3 * group * level
        if in_pieces:
            taken = call(
                deal_kernel,
                [(shape, bf16, STAY)] * 3,
                [(after(near_unit, *others) if others else near_unit, SMEM)]
                + [(b, FAR) for b in blocks],
                "deal",
                2,
                scratch=[pltpu.SemaphoreType.DMA((3,))],
                low=low,
            )
        else:
            whole = jnp.concatenate(blocks, axis=0)
            place = jnp.sum(
                jnp.where(near_unit.reshape(-1)[None, :] == unit_ids[:, None], jnp.arange(whole.shape[0])[None, :], 0),
                axis=1,
            )
            whole = jnp.take(whole, place, axis=0)
            taken = [whole[low + i * group : low + (i + 1) * group] for i in range(3)]
        return [v.reshape(-1, D) for v in taken]

    x, a0, x_far, upper, e0 = call(
        start_kernel,
        [
            ((half, D), f32),
            ((half, D), bf16),
            ((half, D), f32, STAY),
            ((half, D), f32, STAY),
            ((half, D), bf16),
        ],
        [tokens_in, out_grad, both, shared_params],
        "start",
        0,
    )
    a1 = swap(a0, "core")

    def chip_sum(keep, send):
        return (keep.astype(f32) + swap(send, "core").astype(f32)).astype(bf16)

    def joined(level, kind, ours, theirs, x):
        return call(
            join(level, kind),
            [
                ((half, D), f32),
                ((half, D), bf16),
                ((rows, D), f32, STAY),
                ((half, D), f32, STAY),
            ],
            [ours, theirs, x, shared_params],
            "join",
            0,
        )

    saved = []
    for level in range(LAYERS):
        if level == 0:
            weights = [weights_of(0)]
        w_head, w1, w2 = weights[level]
        qkv, mixed, logs, a0_far, a1_far, keep, send = call(
            attention_kernel,
            [
                ((tokens, 3 * width), bf16, STAY),
                ((tokens, width), bf16, STAY),
                ((tokens, 128), f32, STAY),
                ((half, D), bf16, STAY),
                ((half, D), bf16, STAY),
                ((half, D), bf16),
                ((half, D), bf16),
            ],
            [a0, a1, bias_qv[level : level + 1], bias[level], w_head],
            "attention",
            0,
        )
        ours = chip_sum(keep, send)
        theirs = swap(ours, "y")
        if level == 0:
            weights.append(weights_of(1, ours))
            x = after(x, *weights[1])
        else:
            e0 = after(e0, ours)
            e1 = swap(e0, "core")
        x_mid, c0, branch, x_mid_far = joined(level, 0, ours, theirs, x)
        c1 = swap(c0, "core")
        u, slope, c0_far, c1_far, keep, send = call(
            hidden_kernel,
            [
                ((tokens, hidden), bf16, STAY),
                ((tokens, hidden), f32, STAY),
                ((half, D), bf16, STAY),
                ((half, D), bf16, STAY),
                ((half, D), bf16),
                ((half, D), bf16),
            ],
            [c0, c1, bias_1[level : level + 1], w1, w2],
            "hidden",
            0,
        )
        state = (x_far, a0_far, a1_far, qkv, mixed, logs, w_head, branch)
        state += (x_mid_far, c0_far, c1_far, u, slope, w1, w2)
        if level + 1 < LAYERS:
            ours = chip_sum(keep, send)
            theirs = swap(ours, "y")
            x, a0, branch_two, x_far = joined(level, 1, ours, theirs, x_mid)
            a1 = swap(a0, "core")
        else:
            final_parts = (keep, send)
            branch_two = None
        saved.append(state + (branch_two,))

    grads = None
    buffers = [((size, HEAD, D), bf16, FAR) for size in sizes]
    norm_sums, tables = [], [None] * LAYERS
    for level in reversed(range(LAYERS)):
        x_far, a0_far, a1_far, qkv, mixed, logs, w_head, branch = saved[level][:8]
        x_mid_far, c0_far, c1_far, u, slope, w1, w2 = saved[level][8:15]
        dz, e0_far, e1_far, d_b1, keep, send = call(
            hidden_back_kernel,
            [
                ((tokens, hidden), bf16, STAY),
                ((half, D), bf16, STAY),
                ((half, D), bf16, STAY),
                ((1, hidden), f32),
                ((half, D), bf16),
                ((half, D), bf16),
            ],
            [e0, e1, w1, w2, slope],
            "hidden_back",
            0,
        )
        ours = chip_sum(keep, send)
        theirs = swap(ours, "y")
        first = 3 * group * level
        args = [(near_slot, SMEM), after(dz, ours), c0_far, c1_far, u, e0_far, e1_far]
        grads = call(
            weights_kernel,
            buffers,
            args + [(v, FAR) for v in grads or ()],
            "hidden_weights",
            2.5,
            scratch=[pltpu.VMEM((2 * group, HEAD, D), bf16), pltpu.SemaphoreType.DMA],
            alias=len(args) if grads else None,
            first=first + group,
            count=len(buffers),
            capacity=capacity,
        )
        waiting = [grads[0]]
        if level + 1 < LAYERS:
            args = [after(above[0], ours)] + list(above[1:])
            tables[level + 1] = call(table_kernel, [((PACKED, 128), f32)], args, "table", 3)[0]
            waiting += [tables[level + 1], theirs_early]
        d_mid, e0, sums_two = call(
            join_back((level, 4), (level, 2)),
            [((half, D), f32), ((half, D), bf16), ((4, D), f32)],
            [
                ours,
                theirs,
                after(x_mid_far, *waiting),
                upper,
                branch,
                shared_params,
            ],
            "join_back",
            0,
        )
        e1 = swap(e0, "core")
        d_qkv, d_scores, e0_far, e1_far, keep, send = call(
            attention_back_kernel,
            [
                ((tokens, 3 * width), bf16, STAY),
                ((heads_here, tokens, tokens), bf16, STAY),
                ((half, D), bf16, STAY),
                ((half, D), bf16, STAY),
                ((half, D), bf16),
                ((half, D), bf16),
            ],
            [e0, e1, w_head, qkv, logs, bias[level]],
            "attention_back",
            0,
        )
        if level > 0:
            ours = chip_sum(keep, send)
            theirs = swap(ours, "y")
            d_qkv = after(d_qkv, ours)
        args = [(near_slot, SMEM), d_qkv, a0_far, a1_far, mixed, e0_far, e1_far]
        grads = call(
            weights_kernel,
            buffers,
            args + [(v, FAR) for v in grads],
            "attention_weights",
            2,
            scratch=[pltpu.VMEM((group, HEAD, D), bf16), pltpu.SemaphoreType.DMA],
            alias=len(args),
            first=first,
            count=len(buffers),
            capacity=capacity,
        )
        table_args = (d_qkv, d_b1, d_scores, hot, hot_t)
        if level > 0:
            x_far = after(x_far, grads[0])
            upper, e0, sums_one = call(
                join_back((level, 0), (level - 1, 6)),
                [((half, D), f32), ((half, D), bf16), ((4, D), f32)],
                [ours, theirs, x_far, d_mid, saved[level - 1][-1], shared_params],
                "join_back",
                0,
                )
            e1 = swap(e0, "core")
            above = table_args
            early = chip_sum(after(final_parts[0], e0), after(final_parts[1], e0))
            theirs_early = swap(early[rows:], "y")
        else:
            if not in_pieces:
                grads = jnp.split(grads[0], owners_all, axis=0)
                pieces = [[v] for v in grads]
            else:
                pieces = []
                for v in grads:
                    if pieces and v.shape[0] < capacity and len(pieces[-1]) == 1 and pieces[-1][0].shape[0] < capacity:
                        pieces[-1].append(v)
                    else:
                        pieces.append([v])
            args = [after(table_args[0], grads[0])] + list(table_args[1:])
            tables[0] = call(table_kernel, [((PACKED, 128), f32)], args, "table", 3)[0]
            ours = chip_sum(keep, after(send, grads[0]))
            scatter = ScatterSums(pieces[:nz], pieces[nz:])
            scatter.step()
            input_grad, sums_one = call(
                last_back_kernel,
                [((rows, D), f32), ((2, D), f32)],
                [ours, swap(ours[rows:], "y"), after(x_far, scatter.all_parts[0]), d_mid, shared_params],
                "last_back",
                0,
                )
        norm_sums.append((sums_one, sums_two))

    final_branch = (
        early[:rows].astype(f32) + theirs_early.astype(f32) + shared_params[LAYERS - 1, 7]
    )
    last_scale = shared_params[LAYERS - 1, 6]
    block_out = (x_mid[:rows] + last_scale * final_branch).astype(bf16)
    own_grad = out_grad.astype(f32)
    branch_sums = jnp.stack(
        [jnp.sum(own_grad * final_branch, axis=0), jnp.sum(last_scale * own_grad, axis=0)]
    )
    shared_grads = []
    for sums_one, sums_two in norm_sums:
        shared_grads = [sums_one[0:2], sums_two[2:4], sums_two[0:2], branch_sums] + shared_grads
        branch_sums = sums_one[2:4]

    shared_part = jnp.concatenate(shared_grads, axis=0)
    shared_part = sum_over(sum_over(shared_part, "core"), "y")
    small = jnp.concatenate([shared_part.reshape(-1, 128)] + tables, axis=0)
    small = small + scatter.along_x.send(small, "x", SWAP)
    scatter.step()
    step = nz // 2
    while step:
        if step == 1:
            small = after(small, scatter.along_x.come[2], scatter.parts[1])
        small = small + lax.ppermute(small, "z", [(i, i ^ step) for i in range(nz)])
        step //= 2
    while len(scatter.parts) < scatter.count:
        scatter.step()
    lines = shared_part.size // 128
    shared_total = small[:lines].reshape(shared_params.shape)
    split_grads = []
    for level in range(LAYERS):
        part = small[lines + level * PACKED : lines + (level + 1) * PACKED]
        flat = part[: 3 * width // 128 + hidden // 128 + 1].reshape(-1)
        d_bias, d_b1 = flat[: 3 * width], flat[PACK_B1 * 128 : PACK_B1 * 128 + hidden]
        d_rel = jnp.concatenate(
            [
                part[PACK_TABLE : PACK_TABLE + SIDE, : 32 * heads_here]
                .reshape(SIDE, heads_here, 32)[:, :, :SIDE]
                .transpose(1, 0, 2)
                .reshape(heads_here, -1),
                part[PACK_ENDS : PACK_ENDS + heads_here, :3],
            ],
            axis=1,
        )
        split_grads.append(
            jnp.concatenate([d_bias[:width], d_bias[2 * width :], d_b1, d_rel.reshape(-1)])
        )
    split_total = jnp.stack(split_grads)[:, None, :]

    my_ids = (my_z * 2 + my_x) * capacity + jnp.arange(capacity, dtype=jnp.int32)
    used = jnp.any(my_ids[:, None] == slots[None, :], axis=1).astype(jnp.int32)
    base, come = scatter.parts[-1], scatter.come[0][-1]
    store = (weight_store.shape, f32)
    state = call(
        fetch_kernel,
        [(*store, STAY)] * 3,
        [(v, FAR) for v in after((weight_store, first_store, second_store), base)],
        "fetch",
        2,
        scratch=[pltpu.SemaphoreType.DMA((3,))],
    )
    mine, matrix_first, matrix_second, matrix_weight = call(
        update_kernel,
        [(*store, FAR)] * 4,
        [(used, SMEM), base, come] + list(state),
        "update",
        3,
        scratch=[pltpu.VMEM(*store)] * 4 + [pltpu.SemaphoreType.DMA((4,))],
        limit=24,
    )
    shared_moment, shared_square, shared_value = adam_step(
        shared_params, shared_first, shared_second, shared_total, rate_small, 0.0
    )
    split_moment, split_square, split_value = adam_step(
        split_params, split_first, split_second, split_total, rate_small, 0.0
    )
    return (
        block_out,
        input_grad,
        mine,
        matrix_first,
        matrix_second,
        matrix_weight,
        shared_total,
        shared_moment,
        shared_square,
        shared_value,
        split_total,
        split_moment,
        split_square,
        split_value,
    )


def solution(mesh):
    dp, tensor = mesh.shape["dp"], mesh.shape["tensor"]
    fine = Mesh(mesh.devices.reshape(dp // 2, 2, tensor // 2, 2), ("z", "x", "y", "core"))
    data, split = ("z", "x"), ("y", "core")
    tokens = P(data + split, None)
    store = P(data, split, None)
    shards = P(None, split, None)
    return jax.shard_map(
        per_device,
        mesh=fine,
        in_specs=(tokens, tokens, P(data, None), P(), store, store, store, P(), P(), P())
        + (shards,) * 3,
        out_specs=(tokens, tokens) + (store,) * 4 + (P(),) * 4 + (shards,) * 4,
        check_vma=False,
    )
```

```python
import functools

import jax
import jax.numpy as jnp
from jax import lax
from jax.experimental import pallas as pl
from jax.experimental.pallas import tpu as pltpu
from jax.sharding import Mesh
from jax.sharding import PartitionSpec as P

D = 768
HEADS = 12
HEAD = 64
FF = 3072
GRID = 14
LAYERS = 2
STEP = 10
RELS = 732
SIDE = 2 * GRID - 1

PITCH = 16
CODES = 256
CLASS_CODE = GRID * PITCH
SPREAD = 512

PACK_B1 = 5
PACK_TABLE = 11
PACK_ENDS = 43
PACKED = 48

norm_eps = 1e-06
beta_first = 0.5
beta_second = 0.5
adam_eps = 1e-08
rate_matrix = 0.05
rate_small = 0.3
weight_decay = 0.05
masked_score = -1e30

f32 = jnp.float32
bf16 = jnp.bfloat16
MIB = 1 << 20
SCALE = 1e9


def iota(shape, axis):
    return lax.broadcasted_iota(jnp.int32, shape, axis)


def matmul(a, b):
    return jnp.dot(a, b, preferred_element_type=f32)


def matmul_nt(a, b):
    return lax.dot_general(a, b, (((1,), (1,)), ((), ())), preferred_element_type=f32)


def matmul_tn(a, b):
    return lax.dot_general(a, b, (((0,), (0,)), ((), ())), preferred_element_type=f32)


def two_parts(v):
    high = v.astype(bf16)
    return high, (v - high.astype(f32)).astype(bf16)


VMEM, SMEM, STAY, FAR = "vmem", "smem", "stay", "far"


def call(kernel, outs, args, name, us, scratch=(), limit=16, alias=None, **options):
    args = [a if isinstance(a, tuple) else (a, VMEM) for a in args]
    spaces = {VMEM: pltpu.VMEM, SMEM: pltpu.SMEM, FAR: pltpu.HBM}
    colors = {STAY: pltpu.VMEM, FAR: pltpu.HBM, VMEM: jax.ShapeDtypeStruct}
    in_specs = [pl.BlockSpec(memory_space=spaces[place]) for _, place in args]
    args = [
        (pltpu.with_memory_space_constraint(a, pltpu.HBM) if place == FAR else a, place)
        for a, place in args
    ]
    outs = [out if len(out) == 3 else (*out, VMEM) for out in outs]
    shapes = [colors[place](shape, dtype) for shape, dtype, place in outs]
    return pl.pallas_call(
        functools.partial(kernel, **options),
        out_shape=shapes,
        in_specs=in_specs,
        out_specs=[
            pl.BlockSpec(memory_space=pltpu.HBM if place == FAR else pltpu.VMEM) for _, _, place in outs
        ],
        scratch_shapes=list(scratch),
        input_output_aliases={alias + i: i for i in range(len(outs))} if alias is not None else {},
        compiler_params=pltpu.CompilerParams(vmem_limit_bytes=limit * MIB),
        cost_estimate=pl.CostEstimate(flops=int(us * SCALE), bytes_accessed=1, transcendentals=0),
        name=name,
    )(*[a for a, _ in args])


def swap(v, axis):
    return lax.ppermute(v, axis, [(0, 1), (1, 0)])


class Line:
    def __init__(self, ahead=1):
        self.come, self.ahead = [], ahead

    def send(self, v, axis, perm):
        if len(self.come) >= self.ahead:
            v = after(v, self.come[-self.ahead])
        self.come.append(lax.ppermute(v, axis, perm))
        return self.come[-1]


SWAP = [(0, 1), (1, 0)]


def ring(nz):
    return list(range(0, nz, 2)) + list(range(1, nz, 2))[::-1]


def ring_step(nz, back):
    places = ring(nz)
    pairs = [(places[i], places[(i + 1) % nz]) for i in range(nz)]
    return [(b, a) for a, b in pairs] if back else pairs


def gather_stores(store):
    nz = lax.axis_size("z")
    along_z, along_x = Line(), Line()
    blocks = [store]
    for _ in range(1, nz):
        blocks.append(along_z.send(blocks[-1], "z", ring_step(nz, False)))
    return blocks + [along_x.send(v, "x", SWAP) for v in blocks]


class ScatterSums:
    def __init__(self, grads):
        self.grads, self.count = grads, len(grads) // 2
        self.along_z, self.along_x = Line(), Line()
        self.come = None
        self.parts = []

    def step(self):
        s = self.count - 1 - len(self.parts)
        got = self.along_x.send(self.grads[self.count + s], "x", SWAP)
        ours = self.grads[s]
        if self.parts:
            ours = after(ours, self.parts[-1])
        part = ours.astype(f32) + got.astype(f32)
        if s:
            if self.come is not None:
                part = part + self.come.astype(f32)
            part = part.astype(bf16)
            self.come = self.along_z.send(part, "z", ring_step(self.count, True))
        self.parts.append(part)


def after(v, *others):
    return lax.optimization_barrier((v,) + others)[0]


def sum_over(v, axis):
    size = lax.axis_size(axis)
    step = 1
    while step < size:
        v = v + lax.ppermute(v, axis, [(i, i ^ step) for i in range(size)])
        step *= 2
    return v


def deal_kernel(near_unit, *refs, low):
    *blocks, first, second, third, semaphores = refs
    group = first.shape[0]
    outs = (first, second, third)
    for owner, block in enumerate(blocks):
        for k in range(block.shape[0]):
            unit = near_unit[owner, k] - low
            for j, out in enumerate(outs):

                @pl.when((unit >= j * group) & (unit < (j + 1) * group))
                def _():
                    pltpu.make_async_copy(block.at[k], out.at[unit - j * group], semaphores.at[j]).start()

    for j, out in enumerate(outs):
        pltpu.make_async_copy(out, out, semaphores.at[j]).wait()


def lifting(rows):
    return jnp.where(
        SIDE - 1 - iota((rows, SPREAD), 1) // PITCH == iota((rows, SPREAD), 0), 1.0, 0.0
    ).astype(bf16)


def column_offset():
    return iota((32, SPREAD), 0) + (iota((32, SPREAD), 1) % PITCH) - (GRID - 1)


def prepare_kernel(
    table, ends, code_c, seg_c, code_r, seg_r, hot, hot_t, *rest
):
    *biases, spread, tile = rest
    heads = table.shape[0] // len(biases)
    tokens = code_c.shape[0]
    hot[...] = jnp.where(code_c[...] == iota((tokens, CODES), 1), 1.0, 0.0).astype(bf16)
    hot_t[...] = jnp.where(code_r[...] == iota((CODES, tokens), 0), 1.0, 0.0).astype(bf16)
    lift = lifting(32)
    offset = column_offset()
    spread[...] = jnp.zeros(spread.shape, f32)
    for h in range(table.shape[0]):
        high, low = two_parts(table[h])
        lifted = matmul_tn(high, lift) + matmul_tn(low, lift)
        for c in range(GRID):
            line = jnp.sum(jnp.where(offset == c, lifted, 0.0), axis=0, keepdims=True)
            spread[h, c : c + 1, :] = line
    row = iota((CODES, CODES), 0)
    col = iota((CODES, CODES), 1)
    for level, bias in enumerate(biases):

        def one(head, carry):
            h = level * heads + head
            lines = spread[h]
            for r in range(GRID):
                back = (GRID - 1 - r) * PITCH
                moved = pltpu.roll(lines, (SPREAD - back) % SPREAD, 1) if back else lines
                tile[r * PITCH : (r + 1) * PITCH, :] = moved[:, :CODES]
            tile[CLASS_CODE:, :] = jnp.zeros((CODES - CLASS_CODE, CODES), f32)
            full = jnp.where(row == CLASS_CODE, ends[h, 0], tile[...])
            full = jnp.where(col == CLASS_CODE, ends[h, 1], full)
            full = jnp.where((col == CLASS_CODE) & (row == CLASS_CODE), ends[h, 2], full)
            high, low = two_parts(full)
            left_high = matmul(hot[...], high).astype(bf16)
            left_low = matmul(hot[...], low).astype(bf16)
            values = matmul(left_high, hot_t[...]) + matmul(left_low, hot_t[...])
            bias[head] = jnp.where(seg_c[...] == seg_r[...], values, masked_score)
            return carry

        lax.fori_loop(0, heads, one, 0)


def normed(v):
    center = v - jnp.mean(v, axis=-1, keepdims=True)
    inverse = lax.rsqrt(jnp.mean(center * center, axis=-1, keepdims=True) + norm_eps)
    return center * inverse, inverse


def start_kernel(tokens, grads, near, shared, x, low, x_saved, upper, e):
    rows = tokens.shape[0]
    x[:rows, :] = tokens[...].astype(f32)
    x[rows:, :] = near[:rows, :].astype(f32)
    x_saved[...] = x[...]
    hat, _ = normed(x[...])
    low[...] = (hat * shared[0, 0:1, :] + shared[0, 1:2, :]).astype(bf16)
    upper[:rows, :] = grads[...].astype(f32)
    upper[rows:, :] = near[rows:, :].astype(f32)
    e[...] = (shared[LAYERS - 1, 6:7, :] * upper[...]).astype(bf16)


def attention_kernel(a0, a1, vector, bias, w, qkv, mixed, logs, a0_saved, a1_saved, keep, send):
    a0_saved[...] = a0[...]
    a1_saved[...] = a1[...]
    half = a0.shape[0]
    heads = bias.shape[0]
    width = heads * HEAD
    out = qkv
    for i, a in enumerate((a0, a1)):
        rows = pl.ds(i * half, half)
        proj = matmul_nt(a[...], w[: 3 * width, :]) + vector[:, : 3 * width]
        out[rows, :] = proj.astype(bf16)
    bias = bias
    parts = []
    for h in range(heads):
        q = out[:, h * HEAD : (h + 1) * HEAD] * jnp.asarray(HEAD**-0.5, bf16)
        k = out[:, width + h * HEAD : width + (h + 1) * HEAD]
        v = out[:, 2 * width + h * HEAD : 2 * width + (h + 1) * HEAD]
        s = matmul_nt(q, k) + bias[h]
        top = jnp.max(s, axis=-1, keepdims=True)
        e = jnp.exp(s - top)
        total = jnp.sum(e, axis=-1, keepdims=True)
        p = (e * (1.0 / total)).astype(bf16)
        parts.append(matmul(p, v))
        logs[:, h : h + 1] = top + jnp.log(total)
    mixed[...] = jnp.concatenate(parts, axis=1).astype(bf16)
    w_out = w[3 * width :, :]
    keep[...] = matmul(mixed[:half, :], w_out).astype(bf16)
    send[...] = matmul(mixed[half:, :], w_out).astype(bf16)


def attention_back_kernel(
    e0, e1, w_true, qkv, logs, bias, d_qkv, d_scores, e0_saved, e1_saved, keep, send
):
    e0_saved[...] = e0[...]
    e1_saved[...] = e1[...]
    half = e0.shape[0]
    heads = bias.shape[0]
    width = heads * HEAD
    scale = HEAD**-0.5
    w = w_true
    w_out = w[3 * width :, :]
    d_mixed = jnp.concatenate(
        [matmul_nt(e0[...], w_out), matmul_nt(e1[...], w_out)], axis=0
    ).astype(bf16)
    qkv, logs, bias = qkv, logs, bias
    dq, dk, dv = [], [], []
    for h in range(heads):
        q = qkv[:, h * HEAD : (h + 1) * HEAD] * jnp.asarray(scale, bf16)
        k = qkv[:, width + h * HEAD : width + (h + 1) * HEAD]
        v = qkv[:, 2 * width + h * HEAD : 2 * width + (h + 1) * HEAD]
        g = d_mixed[:, h * HEAD : (h + 1) * HEAD]
        p = jnp.exp(matmul_nt(q, k) + bias[h] - logs[:, h : h + 1])
        dp = matmul_nt(g, v)
        pdp = p * dp
        ds = (pdp - p * jnp.sum(pdp, axis=-1, keepdims=True)).astype(bf16)
        d_scores[h] = ds
        dq.append(matmul(ds, k) * scale)
        dk.append(matmul_tn(ds, q))
        dv.append(matmul_tn(p.astype(bf16), g))
    out = d_qkv
    out[...] = jnp.concatenate(dq + dk + dv, axis=1).astype(bf16)
    keep[...] = matmul(out[:half, :], w[: 3 * width, :]).astype(bf16)
    send[...] = matmul(out[half:, :], w[: 3 * width, :]).astype(bf16)


def table_kernel(d_qkv, d_b1, scores, hot, hot_t, packed):
    heads = scores.shape[0]
    width = heads * HEAD
    packed[...] = jnp.zeros(packed.shape, f32)
    line = jnp.sum(d_qkv[...].astype(f32), axis=0, keepdims=True)
    for start in range(0, 3 * width, 128):
        stop = min(start + 128, 3 * width)
        packed[start // 128 : start // 128 + 1, : stop - start] = line[:, start:stop]
    line = d_b1[...]
    for start in range(0, line.shape[1], 128):
        at = PACK_B1 + start // 128
        packed[at : at + 1, :] = line[:, start : start + 128]
    lift = lifting(32)
    offset = column_offset()
    row = iota((CODES, CODES), 0)
    col = iota((CODES, CODES), 1)
    for h in range(heads):
        high, low = two_parts(matmul(hot_t[...], scores[h]))
        tile = matmul(high, hot[...]) + matmul(low, hot[...])
        class_row = jnp.where(row == CLASS_CODE, tile, 0.0)
        class_col = jnp.where(col == CLASS_CODE, tile, 0.0)
        both = jnp.where(col == CLASS_CODE, class_row, 0.0)
        both_sum = jnp.sum(both, keepdims=True)
        row_sum = jnp.sum(class_row, keepdims=True) - both_sum
        col_sum = jnp.sum(class_col, keepdims=True) - both_sum
        lane = iota((1, 128), 1)
        packed[PACK_ENDS + h : PACK_ENDS + h + 1, :] = jnp.where(
            lane == 0, row_sum, jnp.where(lane == 1, col_sum, jnp.where(lane == 2, both_sum, 0.0))
        )
        inner = jnp.where((row < CLASS_CODE) & (col < CLASS_CODE), tile, 0.0)
        lines = jnp.zeros((PITCH, SPREAD), f32)
        for r in range(GRID):
            wide = jnp.concatenate(
                [inner[r * PITCH : (r + 1) * PITCH, :], jnp.zeros((PITCH, SPREAD - CODES), f32)],
                axis=1,
            )
            shift = (GRID - 1 - r) * PITCH
            lines = lines + (pltpu.roll(wide, shift, 1) if shift else wide)
        spread = jnp.zeros((32, SPREAD), f32)
        for c in range(GRID):
            spread = spread + jnp.where(offset == c, lines[c : c + 1, :], 0.0)
        high, low = two_parts(spread)
        packed[PACK_TABLE : PACK_TABLE + 32, 32 * h : 32 * h + 32] = matmul_nt(
            lift, high
        ) + matmul_nt(lift, low)


def gelu_parts(z):
    cdf = 0.5 * (1.0 + lax.erf(z * (0.5**0.5)))
    density = jnp.exp(-0.5 * z * z) * 0.3989422804014327
    return z * cdf, cdf + z * density


def hidden_kernel(c0, c1, b1, w1, w2, u, slope, c0_saved, c1_saved, keep, send):
    c0_saved[...] = c0[...]
    c1_saved[...] = c1[...]
    rows = c0.shape[0]
    cols = w1.shape[0] // 2
    for i, (c, out) in ((1, (c1, send)), (0, (c0, keep))):
        span = pl.ds(i * rows, rows)
        total = None
        for j in range(2):
            lanes = slice(j * cols, (j + 1) * cols)
            z = matmul_nt(c[...], w1[lanes, :]) + b1[:, lanes]
            value, grade = gelu_parts(z)
            value = value.astype(bf16)
            u[span, lanes] = value
            slope[span, lanes] = grade
            part = matmul(value, w2[lanes, :])
            total = part if total is None else total + part
        out[...] = total.astype(bf16)


def hidden_back_kernel(e0, e1, w1, w2, slope, dz, e0_saved, e1_saved, d_b1, keep, send):
    e0_saved[...] = e0[...]
    e1_saved[...] = e1[...]
    rows = e0.shape[0]
    cols = w1.shape[0] // 2
    w2, slope, w1 = w2, slope, w1
    sums = [None, None]
    for i, (e, out) in ((1, (e1, send)), (0, (e0, keep))):
        span = pl.ds(i * rows, rows)
        total = None
        for j in range(2):
            lanes = slice(j * cols, (j + 1) * cols)
            grad = matmul_nt(e[...], w2[lanes, :]) * slope[span, lanes]
            line = jnp.sum(grad, axis=0, keepdims=True)
            sums[j] = line if sums[j] is None else sums[j] + line
            grad = grad.astype(bf16)
            dz[span, lanes] = grad
            part = matmul(grad, w1[lanes, :])
            total = part if total is None else total + part
        out[...] = total.astype(bf16)
    d_b1[...] = jnp.concatenate(sums, axis=1)


def hidden_turn_kernel(
    c0, c1, e0, e1, b1, w1, w2, u, dz, c0_saved, c1_saved, e0_saved, e1_saved, d_b1, keep, send
):
    for source, saved in ((c0, c0_saved), (c1, c1_saved), (e0, e0_saved), (e1, e1_saved)):
        saved[...] = source[...]
    rows = c0.shape[0]
    cols = w1.shape[0] // 2
    sums = [None, None]
    for i, (c, e, out) in ((1, (c1, e1, send)), (0, (c0, e0, keep))):
        span = pl.ds(i * rows, rows)
        total = None
        for j in range(2):
            lanes = slice(j * cols, (j + 1) * cols)
            z = matmul_nt(c[...], w1[lanes, :]) + b1[:, lanes]
            value, grade = gelu_parts(z)
            u[span, lanes] = value.astype(bf16)
            grad = matmul_nt(e[...], w2[lanes, :]) * grade
            line = jnp.sum(grad, axis=0, keepdims=True)
            sums[j] = line if sums[j] is None else sums[j] + line
            grad = grad.astype(bf16)
            dz[span, lanes] = grad
            part = matmul(grad, w1[lanes, :])
            total = part if total is None else total + part
        out[...] = total.astype(bf16)
    d_b1[...] = jnp.concatenate(sums, axis=1)


def project_kernel(u, w2, keep, send):
    rows = keep.shape[0]
    keep[...] = matmul(u[:rows, :], w2[...]).astype(bf16)
    send[...] = matmul(u[rows:, :], w2[...]).astype(bf16)


def put_blocks(blocks, near_slot, first, outs, capacity, semaphore):
    for u in range(blocks.shape[0]):
        place = near_slot[first + u]
        if len(outs) == 1:
            pltpu.make_async_copy(blocks.at[u], outs[0].at[place], semaphore).start()
            continue
        for j, out in enumerate(outs):

            @pl.when((place >= j * capacity) & (place < (j + 1) * capacity))
            def _():
                pltpu.make_async_copy(blocks.at[u], out.at[place - j * capacity], semaphore).start()


def weights_kernel(near_slot, left0, right00, right01, left1, right10, right11, *refs, first, count, capacity):
    *refs, blocks, semaphore = refs
    outs = refs[-count:]
    half = right00.shape[0]
    at = 0
    for left, right0, right1 in ((left0, right00, right01), (left1, right10, right11)):
        grad = matmul_tn(left[:half, :], right0[...]) + matmul_tn(left[half:, :], right1[...])
        stop = at + grad.shape[0] // HEAD
        blocks[at:stop] = grad.astype(bf16).reshape(stop - at, HEAD, grad.shape[1])
        put_blocks(blocks.at[at:stop], near_slot, first + at, outs, capacity, semaphore)
        at = stop
    pltpu.make_async_copy(blocks, blocks, semaphore).wait()


def both_sums(ours, theirs):
    rows = ours.shape[0] // 2
    return jnp.concatenate(
        [
            ours[:rows, :].astype(f32) + theirs[rows:, :].astype(f32),
            ours[rows:, :].astype(f32) + theirs[:rows, :].astype(f32),
        ],
        axis=0,
    )


def join(level, kind):
    def kernel(ours, theirs, x, shared, x_next, low, branch, x_saved):
        rows = branch.shape[0]
        here = (level, 2, 3) if kind == 0 else (level, 6, 7)
        then = (level, 4, 5) if kind == 0 else (level + 1, 0, 1)
        y = both_sums(ours, theirs) + shared[here[0], here[2] : here[2] + 1, :]
        branch[...] = y[:rows, :]
        value = x[...] + shared[here[0], here[1] : here[1] + 1, :] * y
        x_next[...] = value
        x_saved[...] = x_next[...]
        hat, _ = normed(value)
        gain, shift = (shared[then[0], i : i + 1, :] for i in then[1:])
        low[...] = (hat * gain + shift).astype(bf16)

    return kernel


def through_norm(d_normed, x, upper, gain):
    hat, inverse = normed(x)
    d_hat = d_normed * gain
    mean_a = jnp.mean(d_hat, axis=-1, keepdims=True)
    mean_b = jnp.mean(d_hat * hat, axis=-1, keepdims=True)
    return upper + inverse * (d_hat - mean_a - hat * mean_b), d_normed * hat


def join_back(gain_at, scale_at):
    def kernel(ours, theirs, x, upper, branch, shared, dx, low, sums):
        rows = branch.shape[0]
        gain, scale = (shared[i, j : j + 1, :] for i, j in (gain_at, scale_at))
        d_normed = both_sums(ours, theirs)
        value, product = through_norm(d_normed, x[...], upper[...], gain)
        dx[...] = value
        e = scale * value
        low[...] = e.astype(bf16)
        sums[0:1, :] = jnp.sum(product[:rows, :], axis=0, keepdims=True)
        sums[1:2, :] = jnp.sum(d_normed[:rows, :], axis=0, keepdims=True)
        sums[2:3, :] = jnp.sum(value[:rows, :] * branch[...], axis=0, keepdims=True)
        sums[3:4, :] = jnp.sum(e[:rows, :], axis=0, keepdims=True)

    return kernel


def last_back_kernel(ours, theirs, x, upper, shared, dx, sums):
    rows = dx.shape[0]
    d_normed = ours[:rows, :].astype(f32) + theirs[...].astype(f32)
    value, product = through_norm(d_normed, x[:rows, :], upper[:rows, :], shared[0, 0:1, :])
    dx[...] = value
    sums[0:1, :] = jnp.sum(product, axis=0, keepdims=True)
    sums[1:2, :] = jnp.sum(d_normed, axis=0, keepdims=True)


def adam_step(weight, first, second, grad, rate, decay):
    first_new = beta_first * first + (1.0 - beta_first) * grad
    second_new = beta_second * second + (1.0 - beta_second) * grad * grad
    fix_first = 1.0 - beta_first**STEP
    fix_second = 1.0 - beta_second**STEP
    weight_new = weight - rate * (
        first_new / fix_first / (jnp.sqrt(second_new / fix_second) + adam_eps) + decay * weight
    )
    return (first_new, second_new, weight_new)


def fetch_kernel(*refs):
    count = len(refs) // 2
    copies = [
        pltpu.make_async_copy(refs[i], refs[count + i], refs[-1].at[i]) for i in range(count)
    ]
    for copy in copies:
        copy.start()
    for copy in copies:
        copy.wait()


def update_kernel(used, base, come, weight, first, second, *refs):
    outs, scratch, semaphores = refs[:4], refs[4:8], refs[8]
    for k in range(base.shape[0]):
        grad = base[k] + come[k].astype(f32)
        values = (grad,) + adam_step(weight[k], first[k], second[k], grad, rate_matrix, weight_decay)
        for i, value in enumerate(values):
            scratch[i][k] = jnp.where(used[k] > 0, value, 0.0)
            pltpu.make_async_copy(scratch[i].at[k], outs[i].at[k], semaphores.at[i]).start()
    for i in range(4):
        pltpu.make_async_copy(scratch[i], outs[i], semaphores.at[i]).wait()


def image_layout(row_lengths, count):
    endings = jnp.cumsum(row_lengths)
    openings = endings - row_lengths
    places = jnp.arange(count, dtype=jnp.int32)
    inside = places[:, None] >= openings[None, :]
    segment = jnp.sum(inside.astype(jnp.int32), axis=1) - 1
    opening = jnp.max(jnp.where(inside, openings[None, :], 0), axis=1)
    return (segment, places - opening)


def unit_slots(owners, capacity):
    count = owners.shape[0]
    order = jnp.arange(count, dtype=jnp.int32)
    same_owner = owners[:, None] == owners[None, :]
    earlier = order[None, :] < order[:, None]
    rank = jnp.sum((same_owner & earlier).astype(jnp.int32), axis=1)
    return owners * capacity + rank


def per_device(
    tokens_in,
    out_grad,
    lengths,
    owners,
    weight_store,
    first_store,
    second_store,
    shared_params,
    shared_first,
    shared_second,
    split_params,
    split_first,
    split_second,
):
    nz = lax.axis_size("z")
    owners_all = nz * 2
    parts = 4
    heads_here = HEADS // parts
    width = heads_here * HEAD
    hidden = FF // parts
    rows = tokens_in.shape[0]
    tokens = rows * parts
    half = tokens // 2
    capacity = weight_store.shape[0]
    my_z, my_x = lax.axis_index("z"), lax.axis_index("x")
    my_y, my_c = lax.axis_index("y"), lax.axis_index("core")

    slots = unit_slots(owners, capacity)
    both = swap(jnp.concatenate([tokens_in, out_grad], axis=0), "y")
    blocks = gather_stores(weight_store.astype(bf16))

    group = hidden // HEAD
    near_x = (my_x + jnp.arange(2, dtype=jnp.int32)) % 2
    places = jnp.asarray(ring(nz), jnp.int32)
    my_place = jnp.sum(jnp.where(places == my_z, jnp.arange(nz, dtype=jnp.int32), 0))
    near_place = (my_place - jnp.arange(nz, dtype=jnp.int32)) % nz
    near_z = jnp.sum(
        jnp.where(near_place[:, None] == jnp.arange(nz, dtype=jnp.int32)[None, :], places[None, :], 0), axis=1
    )
    owner_of = (near_z[None, :] * 2 + near_x[:, None]).reshape(-1)
    unit_ids = jnp.arange(slots.shape[0], dtype=jnp.int32)
    near_slots = owner_of[:, None] * capacity + jnp.arange(capacity, dtype=jnp.int32)[None, :]
    near_match = near_slots[:, :, None] == slots[None, None, :]
    near_unit = jnp.sum(jnp.where(near_match, unit_ids, 0), axis=2)
    near_unit = jnp.where(jnp.any(near_match, axis=2), near_unit, slots.shape[0])
    in_pieces = owners_all == 8
    sizes = [capacity] * owners_all if in_pieces else [owners_all * capacity]
    near_ids = jnp.arange(owners_all * capacity, dtype=jnp.int32).reshape(owners_all, capacity, 1)
    near_slot = jnp.sum(jnp.where(near_match, near_ids, 0), axis=(0, 1))

    segment, position = image_layout(lengths[0], tokens)
    patch = position - 1
    code = jnp.where(position == 0, CLASS_CODE, (patch // GRID) * PITCH + patch % GRID)

    def local(v):
        v = jnp.roll(v.reshape(2, 2, rows), (-my_y, -my_c), (0, 1))
        return v.transpose(1, 0, 2).reshape(tokens)

    code, segment = local(code), local(segment)
    split = split_params[:, 0, :]
    bias_qv = jnp.concatenate(
        [split[:, :width], jnp.zeros((LAYERS, width), f32), split[:, width : 2 * width]], axis=1
    )
    bias_1 = split[:, 2 * width : 2 * width + hidden]
    table = split[:, 2 * width + hidden :].reshape(LAYERS * heads_here, RELS)
    inner = table[:, : SIDE * SIDE].reshape(-1, SIDE, SIDE)
    inner = jnp.pad(inner, ((0, 0), (0, 32 - SIDE), (0, 32 - SIDE)))
    hot, hot_t, *bias = call(
        prepare_kernel,
        [
            ((tokens, CODES), bf16, STAY),
            ((CODES, tokens), bf16, STAY),
        ]
        + [((heads_here, tokens, tokens), f32, STAY)] * LAYERS,
        [
            inner,
            (table[:, SIDE * SIDE :], SMEM),
            code[:, None],
            segment[:, None],
            code[None, :],
            segment[None, :],
        ],
        "prepare",
        6,
        scratch=[
            pltpu.VMEM((LAYERS * heads_here, PITCH, SPREAD), f32),
            pltpu.VMEM((CODES, CODES), f32),
        ],
    )
    def weights_of(level, *others):
        shape = (group, HEAD, D)
        low = 3 * group * level
        if in_pieces:
            taken = call(
                deal_kernel,
                [(shape, bf16, STAY)] * 3,
                [(after(near_unit, *others) if others else near_unit, SMEM)]
                + [(b, FAR) for b in blocks],
                "deal",
                2,
                scratch=[pltpu.SemaphoreType.DMA((3,))],
                low=low,
            )
        else:
            whole = jnp.concatenate(blocks, axis=0)
            place = jnp.sum(
                jnp.where(near_unit.reshape(-1)[None, :] == unit_ids[:, None], jnp.arange(whole.shape[0])[None, :], 0),
                axis=1,
            )
            whole = jnp.take(whole, place, axis=0)
            taken = [whole[low + i * group : low + (i + 1) * group] for i in range(3)]
        return [v.reshape(-1, D) for v in taken]

    x, a0, x_far, upper, e0 = call(
        start_kernel,
        [
            ((half, D), f32),
            ((half, D), bf16),
            ((half, D), f32, STAY),
            ((half, D), f32, STAY),
            ((half, D), bf16),
        ],
        [tokens_in, out_grad, both, shared_params],
        "start",
        0,
    )
    a1 = swap(a0, "core")

    def chip_sum(keep, send):
        return (keep.astype(f32) + swap(send, "core").astype(f32)).astype(bf16)

    def joined(level, kind, ours, theirs, x):
        return call(
            join(level, kind),
            [
                ((half, D), f32),
                ((half, D), bf16),
                ((rows, D), f32, STAY),
                ((half, D), f32, STAY),
            ],
            [ours, theirs, x, shared_params],
            "join",
            0,
        )

    saved = []
    for level in range(LAYERS):
        if level == 0:
            weights = [weights_of(0)]
        w_head, w1, w2 = weights[level]
        qkv, mixed, logs, a0_far, a1_far, keep, send = call(
            attention_kernel,
            [
                ((tokens, 3 * width), bf16, STAY),
                ((tokens, width), bf16, STAY),
                ((tokens, 128), f32, STAY),
                ((half, D), bf16, STAY),
                ((half, D), bf16, STAY),
                ((half, D), bf16),
                ((half, D), bf16),
            ],
            [a0, a1, bias_qv[level : level + 1], bias[level], w_head],
            "attention",
            0,
        )
        ours = chip_sum(keep, send)
        theirs = swap(ours, "y")
        if level == 0:
            weights.append(weights_of(1, ours))
            x = after(x, *weights[1])
        else:
            e0 = after(e0, ours)
            e1 = swap(e0, "core")
        x_mid, c0, branch, x_mid_far = joined(level, 0, ours, theirs, x)
        c1 = swap(c0, "core")
        if level + 1 < LAYERS:
            u, slope, c0_far, c1_far, keep, send = call(
                hidden_kernel,
                [
                    ((tokens, hidden), bf16, STAY),
                    ((tokens, hidden), f32, STAY),
                    ((half, D), bf16, STAY),
                    ((half, D), bf16, STAY),
                    ((half, D), bf16),
                    ((half, D), bf16),
                ],
                [c0, c1, bias_1[level : level + 1], w1, w2],
                "hidden",
                0,
            )
        else:
            u, dz, c0_far, c1_far, e0_far, e1_far, d_b1, keep, send = call(
                hidden_turn_kernel,
                [((tokens, hidden), bf16, STAY)] * 2
                + [((half, D), bf16, STAY)] * 4
                + [((1, hidden), f32), ((half, D), bf16), ((half, D), bf16)],
                [c0, c1, e0, e1, bias_1[level : level + 1], w1, w2],
                "hidden_turn",
                0,
            )
            slope = None
        state = (x_far, a0_far, a1_far, qkv, mixed, logs, w_head, branch)
        state += (x_mid_far, c0_far, c1_far, u, slope, w1, w2)
        if level + 1 < LAYERS:
            ours = chip_sum(keep, send)
            theirs = swap(ours, "y")
            x, a0, branch_two, x_far = joined(level, 1, ours, theirs, x_mid)
            a1 = swap(a0, "core")
        else:
            branch_two = None
        saved.append(state + (branch_two,))

    grads = None
    buffers = [((size, HEAD, D), bf16, FAR) for size in sizes]
    norm_sums, tables = [], [None] * LAYERS
    for level in reversed(range(LAYERS)):
        x_far, a0_far, a1_far, qkv, mixed, logs, w_head, branch = saved[level][:8]
        x_mid_far, c0_far, c1_far, u, slope, w1, w2 = saved[level][8:15]
        if level + 1 < LAYERS:
            dz, e0_far, e1_far, d_b1, keep, send = call(
                hidden_back_kernel,
                [
                    ((tokens, hidden), bf16, STAY),
                    ((half, D), bf16, STAY),
                    ((half, D), bf16, STAY),
                    ((1, hidden), f32),
                    ((half, D), bf16),
                    ((half, D), bf16),
                ],
                [e0, e1, w1, w2, slope],
                "hidden_back",
                0,
            )
        ours = chip_sum(keep, send)
        theirs = swap(ours, "y")
        first = 3 * group * level
        args = [(near_slot, SMEM), after(dz, ours), c0_far, c1_far, u, e0_far, e1_far]
        grads = call(
            weights_kernel,
            buffers,
            args + [(v, FAR) for v in grads or ()],
            "hidden_weights",
            2.5,
            scratch=[pltpu.VMEM((2 * group, HEAD, D), bf16), pltpu.SemaphoreType.DMA],
            alias=len(args) if grads else None,
            first=first + group,
            count=len(buffers),
            capacity=capacity,
        )
        waiting = [grads[0]]
        if level + 1 < LAYERS:
            args = [after(above[0], ours)] + list(above[1:])
            tables[level + 1] = call(table_kernel, [((PACKED, 128), f32)], args, "table", 3)[0]
            waiting += [tables[level + 1], theirs_early]
        d_mid, e0, sums_two = call(
            join_back((level, 4), (level, 2)),
            [((half, D), f32), ((half, D), bf16), ((4, D), f32)],
            [
                ours,
                theirs,
                after(x_mid_far, *waiting),
                upper,
                branch,
                shared_params,
            ],
            "join_back",
            0,
        )
        e1 = swap(e0, "core")
        d_qkv, d_scores, e0_far, e1_far, keep, send = call(
            attention_back_kernel,
            [
                ((tokens, 3 * width), bf16, STAY),
                ((heads_here, tokens, tokens), bf16, STAY),
                ((half, D), bf16, STAY),
                ((half, D), bf16, STAY),
                ((half, D), bf16),
                ((half, D), bf16),
            ],
            [e0, e1, w_head, qkv, logs, bias[level]],
            "attention_back",
            0,
        )
        if level > 0:
            ours = chip_sum(keep, send)
            theirs = swap(ours, "y")
            d_qkv = after(d_qkv, ours)
        args = [(near_slot, SMEM), d_qkv, a0_far, a1_far, mixed, e0_far, e1_far]
        grads = call(
            weights_kernel,
            buffers,
            args + [(v, FAR) for v in grads],
            "attention_weights",
            2,
            scratch=[pltpu.VMEM((group, HEAD, D), bf16), pltpu.SemaphoreType.DMA],
            alias=len(args),
            first=first,
            count=len(buffers),
            capacity=capacity,
        )
        table_args = (d_qkv, d_b1, d_scores, hot, hot_t)
        if level > 0:
            x_far = after(x_far, grads[0])
            upper, e0, sums_one = call(
                join_back((level, 0), (level - 1, 6)),
                [((half, D), f32), ((half, D), bf16), ((4, D), f32)],
                [ours, theirs, x_far, d_mid, saved[level - 1][-1], shared_params],
                "join_back",
                0,
                )
            e1 = swap(e0, "core")
            above = table_args
            final_parts = call(
                project_kernel,
                [((half, D), bf16), ((half, D), bf16)],
                [after(u, ours), w2],
                "project",
                1,
            )
            early = chip_sum(after(final_parts[0], e0), after(final_parts[1], e0))
            theirs_early = swap(early[rows:], "y")
        else:
            if not in_pieces:
                grads = jnp.split(grads[0], owners_all, axis=0)
            args = [after(table_args[0], grads[0])] + list(table_args[1:])
            tables[0] = call(table_kernel, [((PACKED, 128), f32)], args, "table", 3)[0]
            ours = chip_sum(keep, after(send, grads[0]))
            scatter = ScatterSums(grads)
            scatter.step()
            input_grad, sums_one = call(
                last_back_kernel,
                [((rows, D), f32), ((2, D), f32)],
                [ours, swap(ours[rows:], "y"), x_far, d_mid, shared_params],
                "last_back",
                0,
                )
        norm_sums.append((sums_one, sums_two))

    final_branch = (
        early[:rows].astype(f32) + theirs_early.astype(f32) + shared_params[LAYERS - 1, 7]
    )
    last_scale = shared_params[LAYERS - 1, 6]
    block_out = (x_mid[:rows] + last_scale * final_branch).astype(bf16)
    own_grad = out_grad.astype(f32)
    branch_sums = jnp.stack(
        [jnp.sum(own_grad * final_branch, axis=0), jnp.sum(last_scale * own_grad, axis=0)]
    )
    shared_grads = []
    for sums_one, sums_two in norm_sums:
        shared_grads = [sums_one[0:2], sums_two[2:4], sums_two[0:2], branch_sums] + shared_grads
        branch_sums = sums_one[2:4]

    shared_part = jnp.concatenate(shared_grads, axis=0)
    shared_part = sum_over(sum_over(shared_part, "core"), "y")
    small = jnp.concatenate([shared_part.reshape(-1, 128)] + tables, axis=0)
    small = after(small, scatter.parts[0])
    scatter.step()
    small = small + scatter.along_x.send(small, "x", SWAP)
    small = after(small, scatter.parts[1])
    step = nz // 2
    while step:
        small = small + lax.ppermute(small, "z", [(i, i ^ step) for i in range(nz)])
        step //= 2
    while len(scatter.parts) < scatter.count:
        scatter.step()
    lines = shared_part.size // 128
    shared_total = small[:lines].reshape(shared_params.shape)
    split_grads = []
    for level in range(LAYERS):
        part = small[lines + level * PACKED : lines + (level + 1) * PACKED]
        flat = part[: 3 * width // 128 + hidden // 128 + 1].reshape(-1)
        d_bias, d_b1 = flat[: 3 * width], flat[PACK_B1 * 128 : PACK_B1 * 128 + hidden]
        d_rel = jnp.concatenate(
            [
                part[PACK_TABLE : PACK_TABLE + SIDE, : 32 * heads_here]
                .reshape(SIDE, heads_here, 32)[:, :, :SIDE]
                .transpose(1, 0, 2)
                .reshape(heads_here, -1),
                part[PACK_ENDS : PACK_ENDS + heads_here, :3],
            ],
            axis=1,
        )
        split_grads.append(
            jnp.concatenate([d_bias[:width], d_bias[2 * width :], d_b1, d_rel.reshape(-1)])
        )
    split_total = jnp.stack(split_grads)[:, None, :]

    my_ids = (my_z * 2 + my_x) * capacity + jnp.arange(capacity, dtype=jnp.int32)
    used = jnp.any(my_ids[:, None] == slots[None, :], axis=1).astype(jnp.int32)
    base, come = scatter.parts[-1], scatter.come
    store = (weight_store.shape, f32)
    state = call(
        fetch_kernel,
        [(*store, STAY)] * 3,
        [(v, FAR) for v in after((weight_store, first_store, second_store), base)],
        "fetch",
        2,
        scratch=[pltpu.SemaphoreType.DMA((3,))],
    )
    mine, matrix_first, matrix_second, matrix_weight = call(
        update_kernel,
        [(*store, FAR)] * 4,
        [(used, SMEM), base, come] + list(state),
        "update",
        3,
        scratch=[pltpu.VMEM(*store)] * 4 + [pltpu.SemaphoreType.DMA((4,))],
        limit=24,
    )
    shared_moment, shared_square, shared_value = adam_step(
        shared_params, shared_first, shared_second, shared_total, rate_small, 0.0
    )
    split_moment, split_square, split_value = adam_step(
        split_params, split_first, split_second, split_total, rate_small, 0.0
    )
    return (
        block_out,
        input_grad,
        mine,
        matrix_first,
        matrix_second,
        matrix_weight,
        shared_total,
        shared_moment,
        shared_square,
        shared_value,
        split_total,
        split_moment,
        split_square,
        split_value,
    )


def solution(mesh):
    dp, tensor = mesh.shape["dp"], mesh.shape["tensor"]
    fine = Mesh(mesh.devices.reshape(dp // 2, 2, tensor // 2, 2), ("z", "x", "y", "core"))
    data, split = ("z", "x"), ("y", "core")
    tokens = P(data + split, None)
    store = P(data, split, None)
    shards = P(None, split, None)
    return jax.shard_map(
        per_device,
        mesh=fine,
        in_specs=(tokens, tokens, P(data, None), P(), store, store, store, P(), P(), P())
        + (shards,) * 3,
        out_specs=(tokens, tokens) + (store,) * 4 + (P(),) * 4 + (shards,) * 4,
        check_vma=False,
    )
```
